256 devices in a mesh: pipe: 8 (over y, core), vocab: 2 (over x_lo), expert: 16 (over z, x_hi).
Axes of the slice: x: 4 (x_hi: 2, x_lo: 2; x = x_hi * 2 + x_lo), y: 4, z: 8, core: 2. Of those that a mesh axis runs over, the one named last changes fastest.
Arguments:
- token_ids: int32 [768], replicated, may hold values from 0 to 65535
- routes: int32 [768, 2], replicated, may hold values from 0 to 15, all different within a row; in each aligned block of 768 rows (0 to 767, 768 to 1535, ...) at most 144 rows name the same one
- gate_weights: float32 [768, 2], replicated, may hold values from 0.2 to 1
- embed_table: bfloat16 [65536, 7168], P(('pipe', 'vocab'), 'expert'), may hold values from -0.59765625 to 0.59765625
- w_gate: bfloat16 [16, 7168, 2048], P('expert', None, ('pipe', 'vocab')), may hold values from -0.5 to 0.5
- w_up: bfloat16 [16, 7168, 2048], P('expert', None, ('pipe', 'vocab')), may hold values from -0.5 to 0.5
- w_down: bfloat16 [16, 2048, 7168], P('expert', ('pipe', 'vocab')), may hold values from -0.125 to 0.125
Outputs:
- logits: bfloat16 [768, 65536], P('expert', ('pipe', 'vocab'))
The draws below stay inside these ranges and needn't reach their ends.
Inputs may be any that keep to these rules, and one draw needn't show every extreme that they name: `routes`: each row names 2 different experts; over all 768 rows no expert is named more than 144 times, a bound that some block reaches.
All inputs are finite; a program needn't handle non-finite values.
Results may differ from the reference program's by a relative error of at most 0.025.
Values may be sent and summed in bfloat16 or wider, within the bound.
No kernel may reach another device: no remote copies, remote signals or barrier semaphores. Data moves between devices by JAX's collectives and lax.ppermute only.
A program may use at most 64 MiB of HBM per device.

```python
import math
import jax
import jax.numpy as jnp
import numpy as np
from jax import lax

D = 7168
FF = 2048
VOC = 65536
TOPK = 2
EXPERTS = 16
TOKENS = 768
CAP = 144
N_EXPERT = 16


def set_ends(entries, stream_key, smallest, largest):
    shape = entries.shape
    spot = [jax.random.randint(jax.random.fold_in(stream_key, axis), (), 0, shape[axis]) for axis in range(len(shape))]
    entries = entries.at[tuple(spot)].set(smallest)
    longest = shape.index(max(shape))
    spot[longest] = (spot[longest] + 1) % shape[longest]
    return entries.at[tuple(spot)].set(largest)


def shard_levels(key, shape, split, low, largest):
    gain, own = 1.0, jax.random.fold_in(key, 6)
    for axis_at, blocks in split:
        draws = jnp.exp(jax.random.uniform(jax.random.fold_in(own, axis_at), (blocks,), jnp.float32, low / len(split), largest / len(split)))
        gain = gain * jnp.repeat(draws, shape[axis_at] // blocks).reshape([-1 if axis == axis_at else 1 for axis in range(len(shape))])
    return gain


def cumulative_ranks(count, lean):
    weights = [(1 << 20) // math.isqrt(rank ** lean) + 1 for rank in range(1, count + 1)]
    width = 1 + sum(weights) // (1 << 30)
    return np.cumsum(np.array([max(1, weight // width) for weight in weights]))


def ranked(key, extent, count, slope):
    grid = cumulative_ranks(count, slope)
    pick = jax.random.randint(jax.random.fold_in(key, 1), extent, 0, int(grid[count - 1]))
    grade = jnp.searchsorted(jnp.asarray(grid, jnp.int32), pick, side="right")
    return jax.random.permutation(jax.random.fold_in(key, 2), count)[grade].astype(jnp.int32)


def shared_out(key, own, number, rows, amount, top, reach, slope):
    ranking = jax.random.permutation(key, amount)
    packed, usual = portions_of(amount, rows * top, reach, slope, True), portions_of(amount, rows * top, reach, slope, False)
    places = jnp.arange(amount)

    def named(tallies, turn):
        used = int((tallies > 0).sum())
        fixed = max(1, used // 4)
        passed = fixed + (places - fixed + turn * (used - fixed)) % max(1, amount - fixed)
        return jnp.zeros((amount,), jnp.int32).at[ranking[jnp.where(places < fixed, places, passed)]].set(jnp.asarray(tallies, jnp.int32))

    tallies = jnp.where(number % 4 == 0, named(packed, number // 4), named(usual, number - number // 4 - 1))
    mixed = jax.random.permutation(jax.random.fold_in(own, 3), amount)
    giver, sink = mixed[0:amount // 2 * 2:2], mixed[1:amount // 2 * 2:2]
    margin = jnp.minimum(tallies[giver] - 1, reach - tallies[sink]) // 2
    margin = jnp.where((giver == ranking[0]) | (sink == ranking[0]) | (tallies[sink] == 0), 0, jnp.maximum(margin, 0))
    passed = jax.random.randint(jax.random.fold_in(own, 4), (amount // 2,), 0, 1 << 20) % (margin + 1)
    tallies = tallies.at[giver].add(-passed).at[sink].add(passed)
    members = jnp.searchsorted(jnp.cumsum(tallies), jnp.arange(rows * top), side="right").astype(jnp.int32)
    listing = members.reshape(top, rows).T
    listing = listing[jax.random.permutation(jax.random.fold_in(own, 1), rows)]
    turn = jax.random.randint(jax.random.fold_in(own, 2), (rows, 1), 0, top)
    return jnp.take_along_axis(listing, (jnp.arange(top)[None, :] + turn) % top, axis=1)


def portions_of(number_of, total, most, slope, full):
    loads = [(1 << 20) // math.isqrt(rank ** slope) + 1 for rank in range(1, number_of + 1)]
    largest = most if full else min(most, max(-(-total // number_of), total * loads[0] // sum(loads)))
    least = 1 if total - largest >= number_of - 1 else 0
    given, spare = [largest] + [least] * (number_of - 1), total - largest - least * (number_of - 1)
    while spare > 0:
        candidates = [i for i in range(1, number_of) if given[i] < largest] or [i for i in range(1, number_of) if given[i] < most]
        whole, budget = sum([loads[i] for i in candidates]), spare
        for i in candidates:
            more = min(most - given[i], max(1, budget * loads[i] // whole), spare)
            given[i] = given[i] + more
            spare = spare - more
    return np.array(given)


def normal_values(key, dims, width, reach, cuts=(), held_as=jnp.bfloat16):
    result = jax.random.normal(key, dims, jnp.float32) * width
    if len(cuts) > 0:
        result = shard_levels(key, dims, cuts, -0.22, 0.18) * result
    return jnp.clip(result, min=-reach, max=reach).astype(held_as)


def setup_inputs(seed: int = 0) -> dict:
    streams_of = jax.random.split(jax.random.key(seed), 8)
    token_ids = set_ends(ranked(streams_of[0], (TOKENS,), VOC, 2), jax.random.fold_in(streams_of[0], 3), 0, VOC - 1).astype(jnp.int32)
    routes_keys = jax.random.split(jax.random.fold_in(streams_of[1], 1), TOKENS // TOKENS)
    routes_turns = jax.random.permutation(jax.random.fold_in(streams_of[1], 3), TOKENS // TOKENS)
    routes = jax.vmap(lambda own, number: shared_out(jax.random.fold_in(streams_of[1], 2), own, number, TOKENS, EXPERTS, TOPK, CAP, 1))(routes_keys, routes_turns).reshape((TOKENS, TOPK))
    gate_weights = jnp.clip(jax.random.uniform(streams_of[2], (TOKENS, TOPK), jnp.float32, 0.2, 1.0), 0.2, 1.0)
    embed_table = normal_values(streams_of[3], (VOC, D), 0.1, 0.59765625, ((0, 16), (1, 16)))
    w_gate = normal_values(streams_of[4], (EXPERTS, D, FF), (D // 64) ** -0.5, 0.5, ((0, 16), (2, 16)))
    w_up = normal_values(streams_of[5], (EXPERTS, D, FF), (D // 64) ** -0.5, 0.5, ((0, 16), (2, 16)))
    w_down = normal_values(streams_of[6], (EXPERTS, FF, D), FF ** -0.5, 0.125, ((0, 16), (1, 16)))
    return {"token_ids": token_ids, "routes": routes, "gate_weights": gate_weights, "embed_table": embed_table, "w_gate": w_gate, "w_up": w_up, "w_down": w_down}


def reference(token_ids, routes, gate_weights, embed_table, w_gate, w_up, w_down):
    embedded = embed_table[token_ids]
    flat_routes = routes.reshape(-1)
    one_hot = (flat_routes[:, None] == jnp.arange(EXPERTS, dtype=jnp.int32)[None, :]).astype(jnp.int32)
    slot_index = jnp.sum((jnp.cumsum(one_hot, axis=0) - one_hot) * one_hot, axis=1).astype(jnp.int32)
    slot_dest = (flat_routes * CAP + slot_index).astype(jnp.int32)
    repeated = jnp.repeat(embedded, TOPK, axis=0)
    buffer = jnp.zeros((EXPERTS * CAP, D), jnp.bfloat16).at[slot_dest].set(repeated)
    buffer = buffer.reshape(EXPERTS, CAP, D)

    def expert(operands):
        rows_in, gate_mat, up_mat, down_mat = operands
        gate_proj = jnp.dot(rows_in, gate_mat, preferred_element_type=jnp.float32)
        up_proj = jnp.dot(rows_in, up_mat, preferred_element_type=jnp.float32)
        hidden = (jax.nn.silu(gate_proj) * up_proj).astype(jnp.bfloat16)
        return jnp.dot(hidden, down_mat, preferred_element_type=jnp.float32)

    expert_out = lax.map(expert, (buffer, w_gate, w_up, w_down))
    picked = expert_out.reshape(EXPERTS * CAP, D)[slot_dest].reshape(TOKENS, TOPK, D)
    moe_out = jnp.sum(picked * gate_weights[:, :, None].astype(jnp.float32), axis=1)
    residual = (embedded.astype(jnp.float32) + moe_out).astype(jnp.bfloat16)
    block_width = D // N_EXPERT

    def add_block(total, block):
        start = (block * block_width).astype(jnp.int32)
        res_block = lax.dynamic_slice_in_dim(residual, start, block_width, 1)
        tab_block = lax.dynamic_slice_in_dim(embed_table, start, block_width, 1)
        part = lax.dot_general(res_block, tab_block, (((1,), (1,)), ((), ())), preferred_element_type=jnp.float32)
        rounded = lax.optimization_barrier(part.astype(jnp.bfloat16))
        return total + rounded.astype(jnp.float32), None

    start_total = jnp.zeros((TOKENS, VOC), jnp.float32)
    logits, unused = lax.scan(add_block, start_total, jnp.arange(N_EXPERT, dtype=jnp.int32))
    return logits.astype(jnp.bfloat16)
```

```python
import functools

import jax
import jax.numpy as jnp
from jax import lax
from jax.experimental import pallas as pl
from jax.experimental.pallas import tpu as pltpu
from jax.sharding import Mesh
from jax.sharding import PartitionSpec as P

Y, C, V, Z, H = 4, 2, 2, 8, 2
ALL = ("y", "c", "v", "z", "h")
PV = ("y", "c", "v")
EXPERT = ("z", "h")
GROUP = 16
CAP = 144
BF16 = jnp.bfloat16
F32 = jnp.float32
LIMIT = 48 * 1024 * 1024

VMEM = pl.BlockSpec(memory_space=pltpu.VMEM)
SMEM = pl.BlockSpec(memory_space=pltpu.SMEM)


def call(kernel, out_shape, *args, smem=1, scratch=(), flops=0, size=0):
    return pl.pallas_call(
        kernel,
        out_shape=out_shape,
        in_specs=[SMEM] * smem + [VMEM] * (len(args) - smem),
        out_specs=jax.tree.map(lambda _: VMEM, out_shape),
        scratch_shapes=list(scratch),
        compiler_params=pltpu.CompilerParams(vmem_limit_bytes=LIMIT),
        cost_estimate=pl.CostEstimate(flops=flops, bytes_accessed=size, transcendentals=0),
    )(*args)


def shape(dims, dtype=BF16):
    return jax.ShapeDtypeStruct(dims, dtype)


def ranks(coords, experts, sign):
    y, c, v = coords[0], coords[1], coords[2]
    dy = (sign * (lax.shift_right_logical(experts, 2) - y)) & 3
    dc = (lax.shift_right_logical(experts, 1) & 1) ^ c
    dv = (experts & 1) ^ v
    return dc * 8 + dy * 2 + dv


def lookup_kernel(coords, ids, routes, gates, table, keep, send, dest_cols, slot_w):
    tokens = ids.shape[1]
    rows = table.shape[1]
    step = 512
    base = ids[...] - coords[5] * rows
    acc = jnp.zeros((table.shape[0], tokens), F32)
    for k in range(rows // step):
        place = lax.broadcasted_iota(jnp.int32, (step, tokens), 0) + k * step
        hot = jnp.where(place == base, 1.0, 0.0).astype(BF16)
        acc += jnp.dot(table[:, k * step : (k + 1) * step], hot, preferred_element_type=F32)
    emb_t = acc.astype(BF16)

    experts = lax.broadcasted_iota(jnp.int32, (GROUP, tokens), 0)
    r0 = routes[0:1, :]
    r1 = routes[1:2, :]
    hot0 = experts == r0
    hot1 = experts == r1
    named = jnp.where(hot0 | hot1, 1.0, 0.0).astype(BF16)
    earlier = lax.broadcasted_iota(jnp.int32, (tokens, tokens), 0) < lax.broadcasted_iota(
        jnp.int32, (tokens, tokens), 1
    )
    count = jnp.dot(named, jnp.where(earlier, 1.0, 0.0).astype(BF16), preferred_element_type=F32)
    count = count.astype(jnp.int32)

    def picked(hot, sign):
        where = ranks(coords, experts, sign) * CAP + count
        return jnp.sum(jnp.where(hot, where, 0), axis=0, keepdims=True)

    d0, d1 = picked(hot0, 1), picked(hot1, 1)
    back = jnp.concatenate(
        [picked(hot0, -1), picked(hot1, -1), jnp.zeros((6, tokens), jnp.int32)], axis=0
    )
    dest_cols[...] = back.astype(F32).T
    for r in range(GROUP):
        slot = lax.broadcasted_iota(jnp.int32, (CAP, tokens), 0) + r * CAP
        eq0, eq1 = slot == d0, slot == d1
        spread = jnp.where(eq0 | eq1, 1.0, 0.0).astype(BF16)
        out = lax.dot_general(
            spread, emb_t, (((1,), (1,)), ((), ())), preferred_element_type=F32
        ).astype(BF16)
        if r < 8:
            keep[r] = out
        else:
            send[r - 8] = out
        if r == 0:
            w = jnp.where(eq0, gates[0:1, :], 0.0) + jnp.where(eq1, gates[1:2, :], 0.0)
            slot_w[:, 0:1] = jnp.sum(w, axis=1, keepdims=True)
            slot_w[:, 1:2] = jnp.sum(jnp.where(eq0, 1.0, 0.0), axis=1, keepdims=True)


def add_split_kernel(keep, got, *outs):
    for i, out in enumerate(outs):
        out[...] = (keep[i].astype(F32) + got[i].astype(F32)).astype(BF16)


def expert_kernel(coords, w_gate, w_up, w_down, *refs):
    blocks, (keep, send) = refs[:GROUP], refs[GROUP:]
    y, c, v = coords[0], coords[1], coords[2]
    acc = jnp.zeros((CAP, 256), F32)
    for r in range(GROUP):
        s, dy, dv = r // 8, (r // 2) % 4, r % 2
        at = ((y - dy) & 3) * 4 + (c ^ s) * 2 + (v ^ dv)
        w = jnp.concatenate([w_gate[at], w_up[at]], axis=1)
        acc += jnp.dot(blocks[r][...], w, preferred_element_type=F32)
    gate, up = acc[:, :128], acc[:, 128:]
    hidden = (gate / (1.0 + jnp.exp(-gate)) * up).astype(BF16)
    wide = 2 * keep.shape[2]
    half = keep.shape[2]
    for s, out in ((0, keep), (1, send)):
        for dy in range(4):
            pair = ((y + dy) & 3) * 2 + (c ^ s)
            w = w_down[:, pl.ds(pl.multiple_of(pair * wide, 128), wide)]
            o = jnp.dot(hidden, w, preferred_element_type=F32).astype(BF16)
            out[dy * 2 + v] = o[:, :half]
            out[dy * 2 + (1 - v)] = o[:, half:]


def combine_kernel(coords, dest_cols, *refs):
    blocks, (res, part), held = refs[:GROUP], refs[GROUP:-1], refs[-1]
    for r in range(GROUP):
        held[r * CAP : (r + 1) * CAP, :] = blocks[r][...]
    tokens = dest_cols.shape[0]
    d0 = dest_cols[:, 0:1].astype(jnp.int32)
    d1 = dest_cols[:, 1:2].astype(jnp.int32)
    acc = jnp.zeros(res.shape, F32)
    step = 256
    for k in range(GROUP * CAP // step):
        at = lax.broadcasted_iota(jnp.int32, (tokens, step), 1) + k * step
        pick = jnp.where((at == d0) | (at == d1), 1.0, 0.0).astype(BF16)
        acc += jnp.dot(pick, held[k * step : (k + 1) * step, :], preferred_element_type=F32)
    res[...] = acc.astype(BF16)
    n = part.shape[0]
    part[...] = res[pl.ds(pl.multiple_of(coords[1] * n, 16), n), :]


def logits_kernel(coords, res, got_own, got_other, table, table_got, *refs):
    outs, (held, held_got, other) = refs[:-3], refs[-3:]
    c, z, h = coords[1], coords[3], coords[4]
    n = got_own.shape[0]
    other[pl.ds(pl.multiple_of(c * n, 16), n), :] = got_own[...]
    other[pl.ds(pl.multiple_of((1 - c) * n, 16), n), :] = got_other[...]
    rows = res.shape[0] // Z
    for dz in range(Z):
        at = pl.ds(pl.multiple_of(((z + dz) & 7) * rows, 16), rows)
        held[dz * rows : (dz + 1) * rows, :] = res[at, :]
        held_got[dz * rows : (dz + 1) * rows, :] = other[at, :]
    width = table_got.shape[1]
    step = 256
    for k in range(width // step):
        at = pl.ds(pl.multiple_of(h * width + k * step, 128), step)
        val = jnp.dot(held[...], table[:, at], preferred_element_type=F32)
        val += jnp.dot(
            held_got[...], table_got[:, k * step : (k + 1) * step], preferred_element_type=F32
        )
        val = val.astype(BF16)
        for dz in range(Z):
            outs[dz][:, k * step : (k + 1) * step] = val[dz * rows : (dz + 1) * rows, :]


def chain_kernel(*refs):
    half = len(refs) // 3
    for a, b, out in zip(refs[:half], refs[half : 2 * half], refs[2 * half :]):
        out[...] = (a[...].astype(F32) + b[...].astype(F32)).astype(BF16)


def last_kernel(coords, own, below, above, keep, send, total):
    h = coords[4]
    n = keep.shape[0]
    total[...] = (
        own[...].astype(F32) + below[...].astype(F32) + above[...].astype(F32)
    ).astype(BF16)
    keep[...] = total[pl.ds(pl.multiple_of(h * n, 16), n), :]
    send[...] = total[pl.ds(pl.multiple_of((1 - h) * n, 16), n), :]


def swap(x, axis):
    return lax.ppermute(x, axis, [(0, 1), (1, 0)])


def shift_yv(x, dy, dv):
    pairs = [
        (y * V + v, ((y + dy) % Y) * V + (v ^ dv)) for y in range(Y) for v in range(V)
    ]
    return lax.ppermute(x, ("y", "v"), pairs)


def shift_z(x, dz):
    return lax.ppermute(x, "z", [(z, (z + dz) % Z) for z in range(Z)])


def transposed(x):
    pairs = [(a * GROUP + b, b * GROUP + a) for a in range(GROUP) for b in range(GROUP)]
    return lax.ppermute(x, ALL, pairs)


FAR_FIRST = ((2, 1), (2, 0), (1, 1), (3, 1), (1, 0), (3, 0), (0, 1))


def scatter_sum(keep, send):
    got = swap(send, "c")
    one = shape(keep.shape[1:])
    parts = call(add_split_kernel, [one] * 8, keep, got, smem=0, size=3 * keep.size * 2)
    total = parts[0].astype(F32)
    arrived = [shift_yv(parts[dy * 2 + dv], dy, dv) for dy, dv in FAR_FIRST]
    for x in arrived:
        total = total + x.astype(F32)
    return total.astype(BF16)


def gather_all(own):
    arrived = [None] * GROUP
    arrived[0] = own
    for dy, dv in FAR_FIRST:
        arrived[dy * 2 + dv] = shift_yv(own, dy, dv)
    for r in range(8):
        arrived[8 + r] = swap(arrived[r], "c")
    return arrived


def per_device(token_ids, routes, gate_weights, embed_table, w_gate, w_up, w_down):
    vocab_rows, width = embed_table.shape
    tokens = token_ids.shape[0]
    coords = jnp.stack(
        [lax.axis_index(a) for a in ALL] + [lax.axis_index(PV), jnp.int32(0), jnp.int32(0)]
    ).astype(jnp.int32)
    table = embed_table.T
    h = lax.axis_index("h")
    half = vocab_rows // H
    table_got = swap(lax.dynamic_slice_in_dim(table, (1 - h) * half, half, axis=1), "h")

    slots = (8, CAP, width)
    keep, send, dest_cols, slot_w = call(
        lookup_kernel,
        [shape(slots), shape(slots), shape((tokens, 8), F32), shape((CAP, 2), F32)],
        coords,
        token_ids.reshape(1, tokens),
        routes.T,
        gate_weights.T,
        table,
        flops=2 * tokens * width * (vocab_rows + GROUP * CAP),
        size=8 * 1024 * 1024,
    )
    rows_in = scatter_sum(keep, send)
    blocks = gather_all(transposed(rows_in))
    keep, send = call(
        expert_kernel,
        [shape(slots), shape(slots)],
        coords,
        w_gate.reshape(GROUP, width, 128),
        w_up.reshape(GROUP, width, 128),
        w_down[0],
        *blocks,
        flops=6 * CAP * GROUP * width * 128,
        size=10 * 1024 * 1024,
    )
    back = transposed(scatter_sum(keep, send))
    back = (
        slot_w[:, 0:1] * back.astype(F32) + slot_w[:, 1:2] * rows_in.astype(F32)
    ).astype(BF16)
    blocks = gather_all(back)
    res, part = call(
        combine_kernel,
        [shape((tokens, width)), shape((tokens // 2, width))],
        coords,
        dest_cols,
        *blocks,
        scratch=[pltpu.VMEM((GROUP * CAP, width), BF16)],
        flops=2 * tokens * GROUP * CAP * width,
        size=4 * 1024 * 1024,
    )
    got_own = swap(part, "h")
    got_other = swap(got_own, "c")
    rows = tokens // Z
    outs = call(
        logits_kernel,
        [shape((rows, half))] * Z,
        coords,
        res,
        got_own,
        got_other,
        table,
        table_got,
        scratch=[pltpu.VMEM((tokens, width), BF16)] * 3,
        flops=2 * tokens * width * vocab_rows,
        size=9 * 1024 * 1024,
    )
    mid = half // 2
    down = shift_z(outs[4][:, :mid], -1)
    up = shift_z(outs[4][:, mid:], 1)
    down = jnp.concatenate(
        [(outs[5][:, :mid].astype(F32) + down.astype(F32)).astype(BF16), outs[5][:, mid:]], axis=1
    )
    up = jnp.concatenate(
        [outs[3][:, :mid], (outs[3][:, mid:].astype(F32) + up.astype(F32)).astype(BF16)], axis=1
    )
    for k in (2, 1):
        down, up = shift_z(down, -1), shift_z(up, 1)
        down, up = call(
            chain_kernel,
            [shape((rows, half))] * 2,
            down,
            up,
            outs[Z - k],
            outs[k],
            smem=0,
            size=6 * rows * half * 2,
        )
    down, up = shift_z(down, -1), shift_z(up, 1)
    mine, theirs = call(
        last_kernel,
        [shape((rows // 2, half))] * 2,
        coords,
        outs[0],
        down,
        up,
        scratch=[pltpu.VMEM((rows, half), BF16)],
        size=4 * rows * half * 2,
    )
    got = swap(theirs, "h")
    return jnp.where(
        h == 0, jnp.concatenate([mine, got], axis=1), jnp.concatenate([got, mine], axis=1)
    )


def solution(mesh):
    finer = Mesh(mesh.devices.reshape(Y, C, V, Z, H), ALL)
    return jax.shard_map(
        per_device,
        mesh=finer,
        in_specs=(
            P(),
            P(),
            P(),
            P(PV, EXPERT),
            P(EXPERT, None, PV),
            P(EXPERT, None, PV),
            P(EXPERT, PV, None),
        ),
        out_specs=P(EXPERT, PV),
        check_vma=False,
    )
```

```python
import functools

import jax
import jax.numpy as jnp
from jax import lax
from jax.experimental import pallas as pl
from jax.experimental.pallas import tpu as pltpu
from jax.sharding import Mesh
from jax.sharding import PartitionSpec as P

Y, C, V, Z, H = 4, 2, 2, 8, 2
ALL = ("y", "c", "v", "z", "h")
PV = ("y", "c", "v")
EXPERT = ("z", "h")
GROUP = 16
CAP = 144
BF16 = jnp.bfloat16
F32 = jnp.float32
LIMIT = 48 * 1024 * 1024

VMEM = pl.BlockSpec(memory_space=pltpu.VMEM)
SMEM = pl.BlockSpec(memory_space=pltpu.SMEM)


def call(kernel, out_shape, *args, smem=1, scratch=(), flops=0, size=0):
    return pl.pallas_call(
        kernel,
        out_shape=out_shape,
        in_specs=[SMEM] * smem + [VMEM] * (len(args) - smem),
        out_specs=jax.tree.map(lambda _: VMEM, out_shape),
        scratch_shapes=list(scratch),
        compiler_params=pltpu.CompilerParams(vmem_limit_bytes=LIMIT),
        cost_estimate=pl.CostEstimate(flops=flops, bytes_accessed=size, transcendentals=0),
    )(*args)


def shape(dims, dtype=BF16):
    return jax.ShapeDtypeStruct(dims, dtype)


def stride(y, c):
    return jnp.where(c == 0, y, jnp.where(y == 0, 4, 8 - y))


def ranks(coords, experts, sign):
    y, c, z = coords[0], coords[1], coords[3]
    d = (lax.shift_right_logical(experts, 1) - z) & 7
    cc = jnp.where(d >= 4, 1, 0)
    yy = jnp.where(d < 4, d, (8 - d) & 3)
    return ((cc ^ c) * 4 + ((sign * (yy - y)) & 3)) * 2 + (experts & 1)


def lookup_kernel(coords, ids, routes, gates, table, keep, send, dest_cols, slot_w):
    tokens = ids.shape[1]
    rows = table.shape[1]
    step = 512
    base = ids[...] - coords[5] * rows
    acc = jnp.zeros((table.shape[0], tokens), F32)
    for k in range(rows // step):
        place = lax.broadcasted_iota(jnp.int32, (step, tokens), 0) + k * step
        hot = jnp.where(place == base, 1.0, 0.0).astype(BF16)
        acc += jnp.dot(table[:, k * step : (k + 1) * step], hot, preferred_element_type=F32)
    emb_t = acc.astype(BF16)

    experts = lax.broadcasted_iota(jnp.int32, (GROUP, tokens), 0)
    r0 = routes[0:1, :]
    r1 = routes[1:2, :]
    hot0 = experts == r0
    hot1 = experts == r1
    named = jnp.where(hot0 | hot1, 1.0, 0.0).astype(BF16)
    earlier = lax.broadcasted_iota(jnp.int32, (tokens, tokens), 0) < lax.broadcasted_iota(
        jnp.int32, (tokens, tokens), 1
    )
    count = jnp.dot(named, jnp.where(earlier, 1.0, 0.0).astype(BF16), preferred_element_type=F32)
    count = count.astype(jnp.int32)

    def picked(hot, sign):
        where = ranks(coords, experts, sign) * CAP + count
        return jnp.sum(jnp.where(hot, where, 0), axis=0, keepdims=True)

    d0, d1 = picked(hot0, 1), picked(hot1, 1)
    back = jnp.concatenate(
        [picked(hot0, -1), picked(hot1, -1), jnp.zeros((6, tokens), jnp.int32)], axis=0
    )
    dest_cols[...] = back.astype(F32).T

    def spread(r):
        slot = lax.broadcasted_iota(jnp.int32, (CAP, tokens), 0) + r * CAP
        hot = jnp.where((slot == d0) | (slot == d1), 1.0, 0.0).astype(BF16)
        return lax.dot_general(
            hot, emb_t, (((1,), (1,)), ((), ())), preferred_element_type=F32
        ).astype(BF16)

    for r in range(8):
        both = jnp.concatenate([spread(2 * r), spread(2 * r + 1)], axis=1)
        if r < 4:
            keep[r] = both
        else:
            send[r - 4] = both
    mine = coords[4] ^ coords[2]
    slot = lax.broadcasted_iota(jnp.int32, (CAP, tokens), 0) + mine * CAP
    eq0, eq1 = slot == d0, slot == d1
    w = jnp.where(eq0, gates[0:1, :], 0.0) + jnp.where(eq1, gates[1:2, :], 0.0)
    slot_w[:, 0:1] = jnp.sum(w, axis=1, keepdims=True)
    slot_w[:, 1:2] = jnp.sum(jnp.where(eq0, 1.0, 0.0), axis=1, keepdims=True)


def add_split_kernel(keep, got, *outs):
    for i, out in enumerate(outs):
        out[...] = (keep[i].astype(F32) + got[i].astype(F32)).astype(BF16)


def sum_split_kernel(coords, *refs):
    parts, (keep, send) = refs[:4], refs[4:]
    total = parts[0][...].astype(F32)
    for p in parts[1:]:
        total += p[...].astype(F32)
    n = keep.shape[1]
    left, right = total[:, :n], total[:, n:]
    first = (coords[4] ^ coords[2]) == 0
    keep[...] = jnp.where(first, left, right)
    send[...] = jnp.where(first, right, left).astype(BF16)


def pair_kernel(coords, own, got, out):
    first = (coords[4] ^ coords[2]) == 0
    a, b = own[...].astype(F32), got[...].astype(F32)
    out[...] = jnp.concatenate(
        [jnp.where(first, a, b).astype(BF16), jnp.where(first, b, a).astype(BF16)], axis=1
    )


def expert_kernel(coords, w_gate, w_up, w_down, *refs):
    blocks, (keep, send) = refs[:8], refs[8:]
    y, c, z = coords[0], coords[1], coords[3]
    acc = jnp.zeros((CAP, 256), F32)
    for r in range(8):
        s, dy = r // 4, r % 4
        at = (z - stride((y - dy) & 3, c ^ s)) & 7
        w = jnp.concatenate([w_gate[at], w_up[at]], axis=1)
        acc += jnp.dot(blocks[r][...], w, preferred_element_type=F32)
    gate, up = acc[:, :128], acc[:, 128:]
    hidden = (gate / (1.0 + jnp.exp(-gate)) * up).astype(BF16)
    wide = keep.shape[2]
    for s, out in ((0, keep), (1, send)):
        for dy in range(4):
            at = (z - stride((y + dy) & 3, c ^ s)) & 7
            w = w_down[:, pl.ds(pl.multiple_of(at * wide, 128), wide)]
            out[dy] = jnp.dot(hidden, w, preferred_element_type=F32).astype(BF16)


def combine_kernel(coords, dest_cols, *refs):
    blocks, (res, part), held = refs[:8], refs[8:-1], refs[-1]
    n = res.shape[1]
    for r in range(8):
        held[2 * r * CAP : (2 * r + 1) * CAP, :] = blocks[r][:, :n]
        held[(2 * r + 1) * CAP : (2 * r + 2) * CAP, :] = blocks[r][:, n:]
    tokens = dest_cols.shape[0]
    d0 = dest_cols[:, 0:1].astype(jnp.int32)
    d1 = dest_cols[:, 1:2].astype(jnp.int32)
    acc = jnp.zeros(res.shape, F32)
    step = 256
    for k in range(GROUP * CAP // step):
        at = lax.broadcasted_iota(jnp.int32, (tokens, step), 1) + k * step
        pick = jnp.where((at == d0) | (at == d1), 1.0, 0.0).astype(BF16)
        acc += jnp.dot(pick, held[k * step : (k + 1) * step, :], preferred_element_type=F32)
    res[...] = acc.astype(BF16)
    n = part.shape[0]
    part[...] = res[pl.ds(pl.multiple_of(coords[1] * n, 16), n), :]


def logits_kernel(dzs, coords, res, got_own, got_other, table, got0, got1, *refs):
    outs, (held, held_got, other) = refs[:-3], refs[-3:]
    c, z, h = coords[1], coords[3], coords[4]
    n = got_own.shape[0]
    other[pl.ds(pl.multiple_of(c * n, 16), n), :] = got_own[...]
    other[pl.ds(pl.multiple_of((1 - c) * n, 16), n), :] = got_other[...]
    rows = res.shape[0] // Z
    for i, dz in enumerate(dzs):
        at = pl.ds(pl.multiple_of(((z + dz) & 7) * rows, 16), rows)
        held[i * rows : (i + 1) * rows, :] = res[at, :]
        held_got[i * rows : (i + 1) * rows, :] = other[at, :]
    width = got0.shape[1]
    step = 256
    for u, got in enumerate((got0, got1)):
        for k in range(width // step):
            at = pl.ds(pl.multiple_of((2 * h + u) * width + k * step, 128), step)
            val = jnp.dot(held[...], table[:, at], preferred_element_type=F32)
            val += jnp.dot(
                held_got[...], got[:, k * step : (k + 1) * step], preferred_element_type=F32
            )
            val = val.astype(BF16)
            for i in range(len(dzs)):
                outs[2 * i + u][:, k * step : (k + 1) * step] = val[i * rows : (i + 1) * rows, :]


def last_kernel(coords, own0, own1, below0, below1, above0, above1, keep, send, total):
    h = coords[4]
    n, width = keep.shape[0], own0.shape[1]
    for u, (a, b, d) in enumerate(((own0, below0, above0), (own1, below1, above1))):
        total[:, u * width : (u + 1) * width] = (
            a[...].astype(F32) + b[...].astype(F32) + d[...].astype(F32)
        ).astype(BF16)
    keep[...] = total[pl.ds(pl.multiple_of(h * n, 16), n), :]
    send[...] = total[pl.ds(pl.multiple_of((1 - h) * n, 16), n), :]


def swap(x, axis):
    return lax.ppermute(x, axis, [(0, 1), (1, 0)])


def shift_y(x, dy):
    return lax.ppermute(x, "y", [(y, (y + dy) % Y) for y in range(Y)])


def shift_z(x, dz):
    return lax.ppermute(x, "z", [(z, (z + dz) % Z) for z in range(Z)])


def crossed(x, forward):
    pairs = []
    for y in range(Y):
        for c in range(C):
            far = y if c == 0 else (8 - y if y else 4)
            for v in range(V):
                for z in range(Z):
                    for h in range(H):
                        at = ((y * C + c) * V + v) * Z
                        a = (at + z) * H + h
                        b = (at + (z + far) % Z) * H + (h ^ v)
                        pairs.append((a, b) if forward else (b, a))
    return lax.ppermute(x, ALL, pairs)


def scatter_sum(coords, keep, send):
    got = swap(send, "c")
    one = shape(keep.shape[1:])
    parts = call(add_split_kernel, [one] * 4, keep, got, smem=0, size=3 * keep.size * 2)
    arrived = [shift_y(parts[dy], dy) for dy in (2, 1, 3)]
    half = (one.shape[0], one.shape[1] // 2)
    own, away = call(
        sum_split_kernel,
        [shape(half, F32), shape(half)],
        coords,
        parts[0],
        *arrived,
        size=6 * parts[0].size * 2,
    )
    return (own + swap(away, "v").astype(F32)).astype(BF16)


def gather_all(coords, own):
    got = swap(own, "v")
    pair = call(
        pair_kernel, shape((own.shape[0], 2 * own.shape[1])), coords, own, got, size=8 * own.size
    )
    near = [pair, None, None, None]
    for dy in (2, 1, 3):
        near[dy] = shift_y(pair, dy)
    return near + [swap(x, "c") for x in near]


def added(a, b):
    return (a.astype(F32) + b.astype(F32)).astype(BF16)


def per_device(token_ids, routes, gate_weights, embed_table, w_gate, w_up, w_down):
    vocab_rows, width = embed_table.shape
    tokens = token_ids.shape[0]
    coords = jnp.stack(
        [lax.axis_index(a) for a in ALL] + [lax.axis_index(PV), jnp.int32(0), jnp.int32(0)]
    ).astype(jnp.int32)
    table = embed_table.T
    h = lax.axis_index("h")
    quarter = vocab_rows // H // 2

    def table_piece(u):
        at = (1 - h) * 2 * quarter + u * quarter
        return lax.dynamic_slice_in_dim(table, at, quarter, axis=1)

    got0 = swap(table_piece(0), "h")

    slots = (4, CAP, 2 * width)
    keep, send, dest_cols, slot_w = call(
        lookup_kernel,
        [shape(slots), shape(slots), shape((tokens, 8), F32), shape((CAP, 2), F32)],
        coords,
        token_ids.reshape(1, tokens),
        routes.T,
        gate_weights.T,
        table,
        flops=2 * tokens * width * (vocab_rows + GROUP * CAP),
        size=8 * 1024 * 1024,
    )
    rows_in = scatter_sum(coords, keep, send)
    rows_in, got0 = lax.optimization_barrier((rows_in, got0))
    got1 = swap(table_piece(1), "h")
    blocks = gather_all(coords, crossed(rows_in, True))
    blocks[7], got1 = lax.optimization_barrier((blocks[7], got1))
    keep, send = call(
        expert_kernel,
        [shape(slots), shape(slots)],
        coords,
        w_gate.reshape(8, 2 * width, 128),
        w_up.reshape(8, 2 * width, 128),
        w_down[0],
        *blocks,
        flops=6 * CAP * GROUP * width * 128,
        size=10 * 1024 * 1024,
    )
    back = crossed(scatter_sum(coords, keep, send), False)
    back = (
        slot_w[:, 0:1] * back.astype(F32) + slot_w[:, 1:2] * rows_in.astype(F32)
    ).astype(BF16)
    blocks = gather_all(coords, back)
    res, part = call(
        combine_kernel,
        [shape((tokens, width)), shape((tokens // 2, width))],
        coords,
        dest_cols,
        *blocks,
        scratch=[pltpu.VMEM((GROUP * CAP, width), BF16)],
        flops=2 * tokens * GROUP * CAP * width,
        size=4 * 1024 * 1024,
    )
    got_own = swap(part, "h")
    got_other = swap(got_own, "c")
    rows = tokens // Z
    outs = {}
    for dzs in ((4, 5, 3), (6, 2, 7, 1, 0)):
        m = len(dzs) * rows
        vals = call(
            functools.partial(logits_kernel, dzs),
            [shape((rows, quarter))] * (2 * len(dzs)),
            coords,
            res,
            got_own,
            got_other,
            table,
            got0,
            got1,
            scratch=[
                pltpu.VMEM((m, width), BF16),
                pltpu.VMEM((m, width), BF16),
                pltpu.VMEM((tokens, width), BF16),
            ],
            flops=2 * m * width * vocab_rows,
            size=7 * 1024 * 1024,
        )
        for i, dz in enumerate(dzs):
            outs[dz] = vals[2 * i : 2 * i + 2]
    down = [shift_z(outs[4][0], -1), None]
    up = [None, shift_z(outs[4][1], 1)]
    down[1] = shift_z(outs[5][1], -1)
    up[0] = shift_z(outs[3][0], 1)
    down[0] = shift_z(added(down[0], outs[5][0]), -1)
    up[1] = shift_z(added(up[1], outs[3][1]), 1)
    for k in (2, 1):
        for u in (1, 0):
            down[u] = shift_z(added(down[u], outs[Z - k][u]), -1)
            up[1 - u] = shift_z(added(up[1 - u], outs[k][1 - u]), 1)
    mine, theirs = call(
        last_kernel,
        [shape((rows // 2, 2 * quarter))] * 2,
        coords,
        *outs[0],
        *down,
        *up,
        scratch=[pltpu.VMEM((rows, 2 * quarter), BF16)],
        size=8 * rows * quarter * 2,
    )
    got = swap(theirs, "h")
    return jnp.where(
        h == 0, jnp.concatenate([mine, got], axis=1), jnp.concatenate([got, mine], axis=1)
    )


def solution(mesh):
    finer = Mesh(mesh.devices.reshape(Y, C, V, Z, H), ALL)
    return jax.shard_map(
        per_device,
        mesh=finer,
        in_specs=(
            P(),
            P(),
            P(),
            P(PV, EXPERT),
            P(EXPERT, None, PV),
            P(EXPERT, None, PV),
            P(EXPERT, PV, None),
        ),
        out_specs=P(EXPERT, PV),
        check_vma=False,
    )
```

```python
import functools

import jax
import jax.numpy as jnp
from jax import lax
from jax.experimental import pallas as pl
from jax.experimental.pallas import tpu as pltpu
from jax.sharding import Mesh
from jax.sharding import PartitionSpec as P

Y, C, V, Z, H = 4, 2, 2, 8, 2
ALL = ("y", "c", "v", "z", "h")
PV = ("y", "c", "v")
EXPERT = ("z", "h")
GROUP = 16
CAP = 144
BF16 = jnp.bfloat16
F32 = jnp.float32
LIMIT = 48 * 1024 * 1024

VMEM = pl.BlockSpec(memory_space=pltpu.VMEM)
SMEM = pl.BlockSpec(memory_space=pltpu.SMEM)


def call(kernel, out_shape, *args, smem=1, scratch=(), flops=0, size=0):
    return pl.pallas_call(
        kernel,
        out_shape=out_shape,
        in_specs=[SMEM] * smem + [VMEM] * (len(args) - smem),
        out_specs=jax.tree.map(lambda _: VMEM, out_shape),
        scratch_shapes=list(scratch),
        compiler_params=pltpu.CompilerParams(vmem_limit_bytes=LIMIT),
        cost_estimate=pl.CostEstimate(flops=flops, bytes_accessed=size, transcendentals=0),
    )(*args)


def shape(dims, dtype=BF16):
    return jax.ShapeDtypeStruct(dims, dtype)


def stride(y, c):
    return jnp.where(c == 0, y, jnp.where(y == 0, 4, 8 - y))


def ranks(coords, experts, sign):
    y, c, z = coords[0], coords[1], coords[3]
    d = (lax.shift_right_logical(experts, 1) - z) & 7
    cc = jnp.where(d >= 4, 1, 0)
    yy = jnp.where(d < 4, d, (8 - d) & 3)
    return ((cc ^ c) * 4 + ((sign * (yy - y)) & 3)) * 2 + (experts & 1)


def slots_kernel(coords, routes, gates, dest_rows, dest_cols, slot_w):
    tokens = routes.shape[1]
    experts = lax.broadcasted_iota(jnp.int32, (GROUP, tokens), 0)
    hot0 = experts == routes[0:1, :]
    hot1 = experts == routes[1:2, :]
    named = jnp.where(hot0 | hot1, 1.0, 0.0).astype(BF16)
    earlier = lax.broadcasted_iota(jnp.int32, (tokens, tokens), 0) < lax.broadcasted_iota(
        jnp.int32, (tokens, tokens), 1
    )
    count = jnp.dot(named, jnp.where(earlier, 1.0, 0.0).astype(BF16), preferred_element_type=F32)
    count = count.astype(jnp.int32)

    def picked(hot, sign):
        where = ranks(coords, experts, sign) * CAP + count
        return jnp.sum(jnp.where(hot, where, 0), axis=0, keepdims=True)

    d0, d1 = picked(hot0, 1), picked(hot1, 1)
    rest = jnp.zeros((6, tokens), jnp.int32)
    dest_rows[...] = jnp.concatenate([d0, d1, rest], axis=0)
    back = jnp.concatenate([picked(hot0, -1), picked(hot1, -1), rest], axis=0)
    dest_cols[...] = back.astype(F32).T
    mine = coords[4] ^ coords[2]
    slot = lax.broadcasted_iota(jnp.int32, (CAP, tokens), 0) + mine * CAP
    eq0, eq1 = slot == d0, slot == d1
    w = jnp.where(eq0, gates[0:1, :], 0.0) + jnp.where(eq1, gates[1:2, :], 0.0)
    slot_w[:, 0:1] = jnp.sum(w, axis=1, keepdims=True)
    slot_w[:, 1:2] = jnp.sum(jnp.where(eq0, 1.0, 0.0), axis=1, keepdims=True)


def lookup_kernel(coords, ids, dest_rows, table, keep, send):
    tokens = ids.shape[1]
    rows = table.shape[1]
    step = 512
    base = ids[...] - coords[5] * rows
    acc = jnp.zeros((table.shape[0], tokens), F32)
    for k in range(rows // step):
        place = lax.broadcasted_iota(jnp.int32, (step, tokens), 0) + k * step
        hot = jnp.where(place == base, 1.0, 0.0).astype(BF16)
        acc += jnp.dot(table[:, k * step : (k + 1) * step], hot, preferred_element_type=F32)
    emb_t = acc.astype(BF16)
    d0, d1 = dest_rows[0:1, :], dest_rows[1:2, :]

    def spread(r):
        slot = lax.broadcasted_iota(jnp.int32, (CAP, tokens), 0) + r * CAP
        hot = jnp.where((slot == d0) | (slot == d1), 1.0, 0.0).astype(BF16)
        return lax.dot_general(
            hot, emb_t, (((1,), (1,)), ((), ())), preferred_element_type=F32
        ).astype(BF16)

    for r in range(8):
        both = jnp.concatenate([spread(2 * r), spread(2 * r + 1)], axis=1)
        if r < 4:
            keep[r] = both
        else:
            send[r - 4] = both


def add_split_kernel(keep, got, *outs):
    for i, out in enumerate(outs):
        out[...] = (keep[i].astype(F32) + got[i].astype(F32)).astype(BF16)


def sum_split_kernel(coords, *refs):
    parts, (keep, send) = refs[:4], refs[4:]
    total = parts[0][...].astype(F32)
    for p in parts[1:]:
        total += p[...].astype(F32)
    n = keep.shape[1]
    left, right = total[:, :n], total[:, n:]
    first = (coords[4] ^ coords[2]) == 0
    keep[...] = jnp.where(first, left, right)
    send[...] = jnp.where(first, right, left).astype(BF16)


def pair_kernel(coords, own, got, out):
    first = (coords[4] ^ coords[2]) == 0
    a, b = own[...].astype(F32), got[...].astype(F32)
    out[...] = jnp.concatenate(
        [jnp.where(first, a, b).astype(BF16), jnp.where(first, b, a).astype(BF16)], axis=1
    )


def expert_in_kernel(dys, coords, w_gate, w_up, *refs):
    blocks, acc = refs[: 2 * len(dys)], refs[-1]
    y, c, z = coords[0], coords[1], coords[3]
    total = jnp.zeros(acc.shape, F32)
    for i, dy in enumerate(dys):
        for s in range(2):
            at = (z - stride((y - dy) & 3, c ^ s)) & 7
            w = jnp.concatenate([w_gate[at], w_up[at]], axis=1)
            total += jnp.dot(blocks[2 * i + s][...], w, preferred_element_type=F32)
    acc[...] = total


def expert_out_kernel(dy, coords, acc, w_gate, w_up, w_down, near, far, keep, send):
    y, c, z = coords[0], coords[1], coords[3]
    total = acc[...]
    for s, block in enumerate((near, far)):
        at = (z - stride((y - dy) & 3, c ^ s)) & 7
        w = jnp.concatenate([w_gate[at], w_up[at]], axis=1)
        total += jnp.dot(block[...], w, preferred_element_type=F32)
    gate, up = total[:, :128], total[:, 128:]
    hidden = (gate / (1.0 + jnp.exp(-gate)) * up).astype(BF16)
    wide = keep.shape[2]
    for s, out in ((0, keep), (1, send)):
        for d in range(4):
            at = (z - stride((y + d) & 3, c ^ s)) & 7
            w = w_down[:, pl.ds(pl.multiple_of(at * wide, 128), wide)]
            out[d] = jnp.dot(hidden, w, preferred_element_type=F32).astype(BF16)


def picked_sum(dest_cols, blocks, dys, held, total):
    n = held.shape[1]
    tokens = dest_cols.shape[0]
    d0 = dest_cols[:, 0:1].astype(jnp.int32)
    d1 = dest_cols[:, 1:2].astype(jnp.int32)
    for i, dy in enumerate(dys):
        for s in range(2):
            at = (2 * i + s) * 2 * CAP
            held[at : at + CAP, :] = blocks[2 * i + s][:, :n]
            held[at + CAP : at + 2 * CAP, :] = blocks[2 * i + s][:, n:]
    for i, dy in enumerate(dys):
        picks = []
        for s in range(2):
            at = lax.broadcasted_iota(jnp.int32, (tokens, 2 * CAP), 1) + (s * 4 + dy) * 2 * CAP
            picks.append(jnp.where((at == d0) | (at == d1), 1.0, 0.0))
        pick = jnp.concatenate(picks, axis=1).astype(BF16)
        part = held[4 * i * CAP : 4 * (i + 1) * CAP, :]
        total = total + jnp.dot(pick, part, preferred_element_type=F32)
    return total


def combine_first_kernel(dys, dest_cols, *refs):
    blocks, acc, held = refs[: 2 * len(dys)], refs[-2], refs[-1]
    acc[...] = picked_sum(dest_cols, blocks, dys, held, jnp.zeros(acc.shape, F32))


def combine_last_kernel(dy, coords, dest_cols, acc, near, far, res, part, held):
    res[...] = picked_sum(dest_cols, (near, far), (dy,), held, acc[...]).astype(BF16)
    n = part.shape[0]
    part[...] = res[pl.ds(pl.multiple_of(coords[1] * n, 16), n), :]


def logits_kernel(dzs, coords, res, got_own, got_other, table, got0, got1, *refs):
    outs, (held, held_got, other) = refs[:-3], refs[-3:]
    c, z, h = coords[1], coords[3], coords[4]
    n = got_own.shape[0]
    other[pl.ds(pl.multiple_of(c * n, 16), n), :] = got_own[...]
    other[pl.ds(pl.multiple_of((1 - c) * n, 16), n), :] = got_other[...]
    rows = res.shape[0] // Z
    for i, dz in enumerate(dzs):
        at = pl.ds(pl.multiple_of(((z + dz) & 7) * rows, 16), rows)
        held[i * rows : (i + 1) * rows, :] = res[at, :]
        held_got[i * rows : (i + 1) * rows, :] = other[at, :]
    width = got0.shape[1]
    step = 256
    for u, got in enumerate((got0, got1)):
        for k in range(width // step):
            at = pl.ds(pl.multiple_of((2 * h + u) * width + k * step, 128), step)
            val = jnp.dot(held[...], table[:, at], preferred_element_type=F32)
            val += jnp.dot(
                held_got[...], got[:, k * step : (k + 1) * step], preferred_element_type=F32
            )
            val = val.astype(BF16)
            for i in range(len(dzs)):
                outs[2 * i + u][:, k * step : (k + 1) * step] = val[i * rows : (i + 1) * rows, :]


def last_kernel(coords, own, below, above, keep, send, total):
    h = coords[4]
    n = keep.shape[0]
    total[...] = (
        own[...].astype(F32) + below[...].astype(F32) + above[...].astype(F32)
    ).astype(BF16)
    keep[...] = total[pl.ds(pl.multiple_of(h * n, 16), n), :]
    send[...] = total[pl.ds(pl.multiple_of((1 - h) * n, 16), n), :]


def swap(x, axis):
    return lax.ppermute(x, axis, [(0, 1), (1, 0)])


def shift_y(x, dy):
    return lax.ppermute(x, "y", [(y, (y + dy) % Y) for y in range(Y)])


def shift_z(x, dz):
    return lax.ppermute(x, "z", [(z, (z + dz) % Z) for z in range(Z)])


def crossed(x, forward):
    pairs = []
    for y in range(Y):
        for c in range(C):
            far = y if c == 0 else (8 - y if y else 4)
            for v in range(V):
                for z in range(Z):
                    for h in range(H):
                        at = ((y * C + c) * V + v) * Z
                        a = (at + z) * H + h
                        b = (at + (z + far) % Z) * H + (h ^ v)
                        pairs.append((a, b) if forward else (b, a))
    return lax.ppermute(x, ALL, pairs)


def scatter_sum(coords, keep, send, piece):
    got = swap(send, "c")
    one = shape(keep.shape[1:])
    parts = call(add_split_kernel, [one] * 4, keep, got, smem=0, size=3 * keep.size * 2)
    arrived = [shift_y(parts[dy], dy) for dy in (2, 1, 3)]
    arrived[0], piece = lax.optimization_barrier((arrived[0], piece))
    half = (one.shape[0], one.shape[1] // 2)
    own, away = call(
        sum_split_kernel,
        [shape(half, F32), shape(half)],
        coords,
        parts[0],
        *arrived,
        size=6 * parts[0].size * 2,
    )
    return (own + swap(away, "v").astype(F32)).astype(BF16), piece


def gather_all(coords, own, piece=None):
    got = swap(own, "v")
    pair = call(
        pair_kernel, shape((own.shape[0], 2 * own.shape[1])), coords, own, got, size=8 * own.size
    )
    if piece is not None:
        pair, piece = lax.optimization_barrier((pair, piece))
        piece = swap(piece, "h")
    near = [pair, None, None, None]
    for dy in (2, 1, 3):
        near[dy] = shift_y(pair, dy)
    return [(x, swap(x, "c")) for x in near], piece


def added(a, b):
    return (a.astype(F32) + b.astype(F32)).astype(BF16)


def per_device(token_ids, routes, gate_weights, embed_table, w_gate, w_up, w_down):
    vocab_rows, width = embed_table.shape
    tokens = token_ids.shape[0]
    coords = jnp.stack(
        [lax.axis_index(a) for a in ALL] + [lax.axis_index(PV), jnp.int32(0), jnp.int32(0)]
    ).astype(jnp.int32)
    table = embed_table.T
    h = lax.axis_index("h")
    quarter = vocab_rows // H // 2

    def table_piece(u):
        at = (1 - h) * 2 * quarter + u * quarter
        return lax.dynamic_slice_in_dim(table, at, quarter, axis=1)

    got0 = swap(table_piece(0), "h")

    dest_rows, dest_cols, slot_w = call(
        slots_kernel,
        [shape((8, tokens), jnp.int32), shape((tokens, 8), F32), shape((CAP, 2), F32)],
        coords,
        routes.T,
        gate_weights.T,
        flops=2 * GROUP * tokens * tokens,
        size=64 * 1024,
    )
    slots = (4, CAP, 2 * width)
    keep, send = call(
        lookup_kernel,
        [shape(slots), shape(slots)],
        coords,
        token_ids.reshape(1, tokens),
        dest_rows,
        table,
        flops=2 * tokens * width * (vocab_rows + GROUP * CAP),
        size=8 * 1024 * 1024,
    )
    rows_in, got0 = scatter_sum(coords, keep, send, got0)
    blocks, got1 = gather_all(coords, crossed(rows_in, True), table_piece(1))
    wg = w_gate.reshape(8, 2 * width, 128)
    wu = w_up.reshape(8, 2 * width, 128)
    early, late = (0, 3, 2), 1
    acc = call(
        functools.partial(expert_in_kernel, early),
        shape((CAP, 256), F32),
        coords,
        wg,
        wu,
        *[x for dy in early for x in blocks[dy]],
        flops=3 * CAP * GROUP * width * 128,
        size=5 * 1024 * 1024,
    )
    keep, send = call(
        functools.partial(expert_out_kernel, late),
        [shape(slots), shape(slots)],
        coords,
        acc,
        wg,
        wu,
        w_down[0],
        *blocks[late],
        flops=3 * CAP * GROUP * width * 128,
        size=6 * 1024 * 1024,
    )
    sums, got1 = scatter_sum(coords, keep, send, got1)
    back = crossed(sums, False)
    back = (
        slot_w[:, 0:1] * back.astype(F32) + slot_w[:, 1:2] * rows_in.astype(F32)
    ).astype(BF16)
    blocks, _ = gather_all(coords, back)
    acc = call(
        functools.partial(combine_first_kernel, early),
        shape((tokens, width), F32),
        dest_cols,
        *[x for dy in early for x in blocks[dy]],
        smem=0,
        scratch=[pltpu.VMEM((12 * CAP, width), BF16)],
        flops=2 * tokens * 12 * CAP * width,
        size=3 * 1024 * 1024,
    )
    res, part = call(
        functools.partial(combine_last_kernel, late),
        [shape((tokens, width)), shape((tokens // 2, width))],
        coords,
        dest_cols,
        acc,
        *blocks[late],
        scratch=[pltpu.VMEM((4 * CAP, width), BF16)],
        flops=2 * tokens * 4 * CAP * width,
        size=3 * 1024 * 1024,
    )
    got_own = swap(part, "h")
    got_other = swap(got_own, "c")
    rows = tokens // Z
    outs = {}
    for dzs in ((4, 5, 3), (6, 2, 7, 1, 0)):
        m = len(dzs) * rows
        vals = call(
            functools.partial(logits_kernel, dzs),
            [shape((rows, quarter))] * (2 * len(dzs)),
            coords,
            res,
            got_own,
            got_other,
            table,
            got0,
            got1,
            scratch=[
                pltpu.VMEM((m, width), BF16),
                pltpu.VMEM((m, width), BF16),
                pltpu.VMEM((tokens, width), BF16),
            ],
            flops=2 * m * width * vocab_rows,
            size=7 * 1024 * 1024,
        )
        for i, dz in enumerate(dzs):
            outs[dz] = vals[2 * i : 2 * i + 2]
    down = [shift_z(outs[4][0], -1), None]
    up = [None, shift_z(outs[4][1], 1)]
    down[1] = shift_z(outs[5][1], -1)
    up[0] = shift_z(outs[3][0], 1)
    down[0] = shift_z(added(down[0], outs[5][0]), -1)
    up[1] = shift_z(added(up[1], outs[3][1]), 1)
    for k in (2, 1):
        for u in (1, 0):
            down[u] = shift_z(added(down[u], outs[Z - k][u]), -1)
            up[1 - u] = shift_z(added(up[1 - u], outs[k][1 - u]), 1)
    mine, got = [], []
    for u in range(2):
        keep, send = call(
            last_kernel,
            [shape((rows // 2, quarter))] * 2,
            coords,
            outs[0][u],
            down[u],
            up[u],
            scratch=[pltpu.VMEM((rows, quarter), BF16)],
            size=8 * rows * quarter,
        )
        mine.append(keep)
        got.append(swap(send, "h"))
    return jnp.where(
        h == 0, jnp.concatenate(mine + got, axis=1), jnp.concatenate(got + mine, axis=1)
    )


def solution(mesh):
    finer = Mesh(mesh.devices.reshape(Y, C, V, Z, H), ALL)
    return jax.shard_map(
        per_device,
        mesh=finer,
        in_specs=(
            P(),
            P(),
            P(),
            P(PV, EXPERT),
            P(EXPERT, None, PV),
            P(EXPERT, None, PV),
            P(EXPERT, PV, None),
        ),
        out_specs=P(EXPERT, PV),
        check_vma=False,
    )
```

```python
import functools

import jax
import jax.numpy as jnp
from jax import lax
from jax.experimental import pallas as pl
from jax.experimental.pallas import tpu as pltpu
from jax.sharding import Mesh
from jax.sharding import PartitionSpec as P

Y, C, V, Z, H = 4, 2, 2, 8, 2
ALL = ("y", "c", "v", "z", "h")
PV = ("y", "c", "v")
EXPERT = ("z", "h")
GROUP = 16
CAP = 144
BF16 = jnp.bfloat16
F32 = jnp.float32
LIMIT = 48 * 1024 * 1024

VMEM = pl.BlockSpec(memory_space=pltpu.VMEM)
SMEM = pl.BlockSpec(memory_space=pltpu.SMEM)


def call(kernel, out_shape, *args, smem=1, scratch=(), flops=0, size=0):
    return pl.pallas_call(
        kernel,
        out_shape=out_shape,
        in_specs=[SMEM] * smem + [VMEM] * (len(args) - smem),
        out_specs=jax.tree.map(lambda _: VMEM, out_shape),
        scratch_shapes=list(scratch),
        compiler_params=pltpu.CompilerParams(vmem_limit_bytes=LIMIT),
        cost_estimate=pl.CostEstimate(flops=flops, bytes_accessed=size, transcendentals=0),
    )(*args)


def shape(dims, dtype=BF16):
    return jax.ShapeDtypeStruct(dims, dtype)


def stride(y, c):
    return jnp.where(c == 0, y, jnp.where(y == 0, 4, 8 - y))


def ranks(coords, experts, sign):
    y, c, z = coords[0], coords[1], coords[3]
    d = (lax.shift_right_logical(experts, 1) - z) & 7
    cc = jnp.where(d >= 4, 1, 0)
    yy = jnp.where(d < 4, d, (8 - d) & 3)
    return ((cc ^ c) * 4 + ((sign * (yy - y)) & 3)) * 2 + (experts & 1)


def lookup_kernel(
    coords, ids, routes, gates, table, keep, send, dest_cols, slot_w, p0, p1, p2, p3
):
    tokens = ids.shape[1]
    rows = table.shape[1]
    step = 512
    base = ids[...] - coords[5] * rows
    acc = jnp.zeros((table.shape[0], tokens), F32)
    place = lax.broadcasted_iota(jnp.int32, (step, tokens), 0)
    for k in range(rows // step):
        hot = jnp.where(place == base - k * step, 1.0, 0.0).astype(BF16)
        acc += jnp.dot(table[:, k * step : (k + 1) * step], hot, preferred_element_type=F32)
    emb_t = acc.astype(BF16)

    experts = lax.broadcasted_iota(jnp.int32, (GROUP, tokens), 0)
    r0 = routes[0:1, :]
    r1 = routes[1:2, :]
    hot0 = experts == r0
    hot1 = experts == r1
    named = jnp.where(hot0 | hot1, 1.0, 0.0).astype(BF16)
    earlier = lax.broadcasted_iota(jnp.int32, (tokens, tokens), 0) < lax.broadcasted_iota(
        jnp.int32, (tokens, tokens), 1
    )
    count = jnp.dot(named, jnp.where(earlier, 1.0, 0.0).astype(BF16), preferred_element_type=F32)
    count = count.astype(jnp.int32)

    def picked(hot, sign):
        where = ranks(coords, experts, sign) * CAP + count
        return jnp.sum(jnp.where(hot, where, 0), axis=0, keepdims=True)

    d0, d1 = picked(hot0, 1), picked(hot1, 1)
    back = jnp.concatenate(
        [picked(hot0, -1), picked(hot1, -1), jnp.zeros((6, tokens), jnp.int32)], axis=0
    )
    dest_cols[...] = back.astype(F32).T

    many = 4 * CAP
    for r in range(0, 8, 2):
        slot = lax.broadcasted_iota(jnp.int32, (many, tokens), 0) + 2 * r * CAP
        hot = jnp.where((slot == d0) | (slot == d1), 1.0, 0.0).astype(BF16)
        out = lax.dot_general(
            hot, emb_t, (((1,), (1,)), ((), ())), preferred_element_type=F32
        ).astype(BF16)
        for i in range(2):
            at = 2 * i * CAP
            both = jnp.concatenate([out[at : at + CAP], out[at + CAP : at + 2 * CAP]], axis=1)
            if r < 4:
                keep[r + i] = both
            else:
                send[r + i - 4] = both
    away = (1 - coords[4]) * (rows // 2)
    width = p0.shape[1]
    for u, piece in enumerate((p0, p1, p2, p3)):
        piece[...] = table[:, pl.ds(pl.multiple_of(away + u * width, 128), width)]
    mine = coords[4] ^ coords[2]
    slot = lax.broadcasted_iota(jnp.int32, (CAP, tokens), 0) + mine * CAP
    eq0, eq1 = slot == d0, slot == d1
    w = jnp.where(eq0, gates[0:1, :], 0.0) + jnp.where(eq1, gates[1:2, :], 0.0)
    slot_w[:, 0:1] = jnp.sum(w, axis=1, keepdims=True)
    slot_w[:, 1:2] = jnp.sum(jnp.where(eq0, 1.0, 0.0), axis=1, keepdims=True)


def add_split_kernel(keep, got, *outs):
    for i, out in enumerate(outs):
        out[...] = (keep[i].astype(F32) + got[i].astype(F32)).astype(BF16)


def sum_split_kernel(coords, *refs):
    parts, (keep, send) = refs[:4], refs[4:]
    total = parts[0][...].astype(F32)
    for p in parts[1:]:
        total += p[...].astype(F32)
    n = keep.shape[1]
    left, right = total[:, :n], total[:, n:]
    first = (coords[4] ^ coords[2]) == 0
    keep[...] = jnp.where(first, left, right)
    send[...] = jnp.where(first, right, left).astype(BF16)


def pair_kernel(coords, own, got, out):
    first = (coords[4] ^ coords[2]) == 0
    a, b = own[...].astype(F32), got[...].astype(F32)
    out[...] = jnp.concatenate(
        [jnp.where(first, a, b).astype(BF16), jnp.where(first, b, a).astype(BF16)], axis=1
    )


def expert_kernel(coords, w_gate, w_up, w_down, *refs):
    blocks, (keep, send) = refs[:8], refs[8:]
    y, c, z = coords[0], coords[1], coords[3]
    acc = jnp.zeros((CAP, 256), F32)
    for r in range(8):
        s, dy = r // 4, r % 4
        at = (z - stride((y - dy) & 3, c ^ s)) & 7
        w = jnp.concatenate([w_gate[at], w_up[at]], axis=1)
        acc += jnp.dot(blocks[r][...], w, preferred_element_type=F32)
    gate, up = acc[:, :128], acc[:, 128:]
    hidden = (gate / (1.0 + jnp.exp(-gate)) * up).astype(BF16)
    wide = keep.shape[2]
    for s, out in ((0, keep), (1, send)):
        for dy in range(4):
            at = (z - stride((y + dy) & 3, c ^ s)) & 7
            w = w_down[:, pl.ds(pl.multiple_of(at * wide, 128), wide)]
            out[dy] = jnp.dot(hidden, w, preferred_element_type=F32).astype(BF16)


def combine_kernel(coords, dest_cols, *refs):
    blocks, (res, part), held = refs[:8], refs[8:-1], refs[-1]
    n = res.shape[1]
    for r in range(8):
        held[2 * r * CAP : (2 * r + 1) * CAP, :] = blocks[r][:, :n]
        held[(2 * r + 1) * CAP : (2 * r + 2) * CAP, :] = blocks[r][:, n:]
    tokens = dest_cols.shape[0]
    d0 = dest_cols[:, 0:1].astype(jnp.int32)
    d1 = dest_cols[:, 1:2].astype(jnp.int32)
    acc = jnp.zeros(res.shape, F32)
    step = 256
    for k in range(GROUP * CAP // step):
        at = lax.broadcasted_iota(jnp.int32, (tokens, step), 1) + k * step
        pick = jnp.where((at == d0) | (at == d1), 1.0, 0.0).astype(BF16)
        acc += jnp.dot(pick, held[k * step : (k + 1) * step, :], preferred_element_type=F32)
    res[...] = acc.astype(BF16)
    m = part.shape[0]
    at = coords[1] * 2 * m
    part[:, :n] = res[pl.ds(pl.multiple_of(at, 16), m), :]
    part[:, n:] = res[pl.ds(pl.multiple_of(at + m, 16), m), :]


def logits_kernel(dzs, coords, res, got_own, got_other, table, g0, g1, g2, g3, *refs):
    outs, (held, held_got, other) = refs[:-3], refs[-3:]
    c, z, h = coords[1], coords[3], coords[4]
    m, n = got_own.shape[0], res.shape[1]
    for half, got in ((c, got_own), (1 - c, got_other)):
        other[pl.ds(pl.multiple_of(half * 2 * m, 16), m), :] = got[:, :n]
        other[pl.ds(pl.multiple_of(half * 2 * m + m, 16), m), :] = got[:, n:]
    rows = res.shape[0] // Z
    for i, dz in enumerate(dzs):
        at = pl.ds(pl.multiple_of(((z + dz) & 7) * rows, 16), rows)
        held[i * rows : (i + 1) * rows, :] = res[at, :]
        held_got[i * rows : (i + 1) * rows, :] = other[at, :]
    width = g0.shape[1]
    for k, got in enumerate((g0, g1, g2, g3)):
        at = pl.ds(pl.multiple_of((4 * h + k) * width, 128), width)
        val = jnp.dot(held[...], table[:, at], preferred_element_type=F32)
        val += jnp.dot(held_got[...], got[...], preferred_element_type=F32)
        val = val.astype(BF16)
        u, at = k // 2, (k % 2) * width
        for i in range(len(dzs)):
            outs[2 * i + u][:, at : at + width] = val[i * rows : (i + 1) * rows, :]


def last_kernel(coords, own, below, above, keep, send, total):
    h = coords[4]
    n = keep.shape[0]
    total[...] = (
        own[...].astype(F32) + below[...].astype(F32) + above[...].astype(F32)
    ).astype(BF16)
    keep[...] = total[pl.ds(pl.multiple_of(h * n, 16), n), :]
    send[...] = total[pl.ds(pl.multiple_of((1 - h) * n, 16), n), :]


def swap(x, axis):
    return lax.ppermute(x, axis, [(0, 1), (1, 0)])


def shift_y(x, dy):
    return lax.ppermute(x, "y", [(y, (y + dy) % Y) for y in range(Y)])


def shift_z(x, dz):
    return lax.ppermute(x, "z", [(z, (z + dz) % Z) for z in range(Z)])


def crossed(x, forward):
    pairs = []
    for y in range(Y):
        for c in range(C):
            far = y if c == 0 else (8 - y if y else 4)
            for v in range(V):
                for z in range(Z):
                    for h in range(H):
                        at = ((y * C + c) * V + v) * Z
                        a = (at + z) * H + h
                        b = (at + (z + far) % Z) * H + (h ^ v)
                        pairs.append((a, b) if forward else (b, a))
    return lax.ppermute(x, ALL, pairs)


def scatter_sum(coords, keep, send, piece):
    got = swap(send, "c")
    one = shape(keep.shape[1:])
    parts = list(call(add_split_kernel, [one] * 4, keep, got, smem=0, size=3 * keep.size * 2))
    parts[3], piece = lax.optimization_barrier((parts[3], piece))
    arrived = [shift_y(parts[dy], dy) for dy in (2, 1, 3)]
    piece = swap(piece, "h")
    arrived[0], piece = lax.optimization_barrier((arrived[0], piece))
    half = (one.shape[0], one.shape[1] // 2)
    own, away = call(
        sum_split_kernel,
        [shape(half, F32), shape(half)],
        coords,
        parts[0],
        *arrived,
        size=6 * parts[0].size * 2,
    )
    return (own + swap(away, "v").astype(F32)).astype(BF16), piece


def gather_all(coords, own, piece):
    got = swap(own, "v")
    pair = call(
        pair_kernel, shape((own.shape[0], 2 * own.shape[1])), coords, own, got, size=8 * own.size
    )
    pair, piece = lax.optimization_barrier((pair, piece))
    near = [pair, None, None, None]
    for dy in (2, 1, 3):
        near[dy] = shift_y(pair, dy)
    piece = swap(piece, "h")
    near[0], near[3] = lax.optimization_barrier((pair, near[3]))
    far = [swap(x, "c") for x in near]
    far[1], piece = lax.optimization_barrier((far[1], piece))
    return near + far, piece


def added(a, b):
    return (a.astype(F32) + b.astype(F32)).astype(BF16)


def per_device(token_ids, routes, gate_weights, embed_table, w_gate, w_up, w_down):
    vocab_rows, width = embed_table.shape
    tokens = token_ids.shape[0]
    coords = jnp.stack(
        [lax.axis_index(a) for a in ALL] + [lax.axis_index(PV), jnp.int32(0), jnp.int32(0)]
    ).astype(jnp.int32)
    table = embed_table.T
    h = lax.axis_index("h")
    eighth = vocab_rows // 8
    quarter = 2 * eighth
    slots = (4, CAP, 2 * width)
    keep, send, dest_cols, slot_w, *pieces = call(
        lookup_kernel,
        [shape(slots), shape(slots), shape((tokens, 8), F32), shape((CAP, 2), F32)]
        + [shape((width, eighth))] * 4,
        coords,
        token_ids.reshape(1, tokens),
        routes.T,
        gate_weights.T,
        table,
        flops=2 * tokens * width * (vocab_rows + GROUP * CAP),
        size=8 * 1024 * 1024,
    )
    rows_in, got0 = scatter_sum(coords, keep, send, pieces[0])
    blocks, got1 = gather_all(coords, crossed(rows_in, True), pieces[1])
    keep, send = call(
        expert_kernel,
        [shape(slots), shape(slots)],
        coords,
        w_gate.reshape(8, 2 * width, 128),
        w_up.reshape(8, 2 * width, 128),
        w_down[0],
        *blocks,
        flops=6 * CAP * GROUP * width * 128,
        size=10 * 1024 * 1024,
    )
    sums, got2 = scatter_sum(coords, keep, send, pieces[2])
    back = crossed(sums, False)
    back = (
        slot_w[:, 0:1] * back.astype(F32) + slot_w[:, 1:2] * rows_in.astype(F32)
    ).astype(BF16)
    blocks, got3 = gather_all(coords, back, pieces[3])
    res, part = call(
        combine_kernel,
        [shape((tokens, width)), shape((tokens // 4, 2 * width))],
        coords,
        dest_cols,
        *blocks,
        scratch=[pltpu.VMEM((GROUP * CAP, width), BF16)],
        flops=2 * tokens * GROUP * CAP * width,
        size=4 * 1024 * 1024,
    )
    got_own = swap(part, "h")
    got_other = swap(got_own, "c")
    rows = tokens // Z
    outs = {}
    for dzs in ((4, 5, 3), (6, 2, 7, 1, 0)):
        m = len(dzs) * rows
        vals = call(
            functools.partial(logits_kernel, dzs),
            [shape((rows, quarter))] * (2 * len(dzs)),
            coords,
            res,
            got_own,
            got_other,
            table,
            got0,
            got1,
            got2,
            got3,
            scratch=[
                pltpu.VMEM((m, width), BF16),
                pltpu.VMEM((m, width), BF16),
                pltpu.VMEM((tokens, width), BF16),
            ],
            flops=2 * m * width * vocab_rows,
            size=7 * 1024 * 1024,
        )
        for i, dz in enumerate(dzs):
            outs[dz] = vals[2 * i : 2 * i + 2]
    down = [shift_z(outs[4][0], -1), None]
    up = [None, shift_z(outs[4][1], 1)]
    down[1] = shift_z(outs[5][1], -1)
    up[0] = shift_z(outs[3][0], 1)
    down[0] = shift_z(added(down[0], outs[5][0]), -1)
    up[1] = shift_z(added(up[1], outs[3][1]), 1)
    for k in (2, 1):
        for u in (1, 0):
            down[u] = shift_z(added(down[u], outs[Z - k][u]), -1)
            up[1 - u] = shift_z(added(up[1 - u], outs[k][1 - u]), 1)
    mine, got = [], []
    for u in range(2):
        keep, send = call(
            last_kernel,
            [shape((rows // 2, quarter))] * 2,
            coords,
            outs[0][u],
            down[u],
            up[u],
            scratch=[pltpu.VMEM((rows, quarter), BF16)],
            size=8 * rows * quarter,
        )
        mine.append(keep)
        got.append(swap(send, "h"))
    return jnp.where(
        h == 0, jnp.concatenate(mine + got, axis=1), jnp.concatenate(got + mine, axis=1)
    )


def solution(mesh):
    finer = Mesh(mesh.devices.reshape(Y, C, V, Z, H), ALL)
    return jax.shard_map(
        per_device,
        mesh=finer,
        in_specs=(
            P(),
            P(),
            P(),
            P(PV, EXPERT),
            P(EXPERT, None, PV),
            P(EXPERT, None, PV),
            P(EXPERT, PV, None),
        ),
        out_specs=P(EXPERT, PV),
        check_vma=False,
    )
```

```python
import functools

import jax
import jax.numpy as jnp
from jax import lax
from jax.experimental import pallas as pl
from jax.experimental.pallas import tpu as pltpu
from jax.sharding import Mesh
from jax.sharding import PartitionSpec as P

Y, C, V, Z, H = 4, 2, 2, 8, 2
ALL = ("y", "c", "v", "z", "h")
PV = ("y", "c", "v")
EXPERT = ("z", "h")
GROUP = 16
CAP = 144
BF16 = jnp.bfloat16
F32 = jnp.float32
LIMIT = 28 * 1024 * 1024

VMEM = pl.BlockSpec(memory_space=pltpu.VMEM)
SMEM = pl.BlockSpec(memory_space=pltpu.SMEM)


def call(kernel, out_shape, *args, smem=1, scratch=(), flops=0, size=0):
    return pl.pallas_call(
        kernel,
        out_shape=out_shape,
        in_specs=[SMEM] * smem + [VMEM] * (len(args) - smem),
        out_specs=jax.tree.map(lambda _: VMEM, out_shape),
        scratch_shapes=list(scratch),
        compiler_params=pltpu.CompilerParams(vmem_limit_bytes=LIMIT),
        cost_estimate=pl.CostEstimate(flops=flops, bytes_accessed=size, transcendentals=0),
    )(*args)


def shape(dims, dtype=BF16):
    return jax.ShapeDtypeStruct(dims, dtype)


def stride(y, c):
    return jnp.where(c == 0, y, jnp.where(y == 0, 4, 8 - y))


def ranks(coords, experts, sign):
    y, c, z = coords[0], coords[1], coords[3]
    d = (lax.shift_right_logical(experts, 1) - z) & 7
    cc = jnp.where(d >= 4, 1, 0)
    yy = jnp.where(d < 4, d, (8 - d) & 3)
    return ((cc ^ c) * 4 + ((sign * (yy - y)) & 3)) * 2 + (experts & 1)


def lookup_kernel(
    coords, ids, routes, gates, table, keep, send, dest_cols, slot_w, plain, own, p0, p1, p2, p3
):
    tokens = ids.shape[1]
    rows = table.shape[1]
    step = 512
    base = ids[...] - coords[5] * rows
    acc = jnp.zeros((table.shape[0], tokens), F32)
    place = lax.broadcasted_iota(jnp.int32, (step, tokens), 0)
    for k in range(rows // step):
        hot = jnp.where(place == base - k * step, 1.0, 0.0).astype(BF16)
        acc += jnp.dot(table[:, k * step : (k + 1) * step], hot, preferred_element_type=F32)
    emb_t = acc.astype(BF16)

    experts = lax.broadcasted_iota(jnp.int32, (GROUP, tokens), 0)
    r0 = routes[0:1, :]
    r1 = routes[1:2, :]
    hot0 = experts == r0
    hot1 = experts == r1
    named = jnp.where(hot0 | hot1, 1.0, 0.0).astype(BF16)
    earlier = lax.broadcasted_iota(jnp.int32, (tokens, tokens), 0) < lax.broadcasted_iota(
        jnp.int32, (tokens, tokens), 1
    )
    count = jnp.dot(named, jnp.where(earlier, 1.0, 0.0).astype(BF16), preferred_element_type=F32)
    count = count.astype(jnp.int32)

    def picked(hot, sign):
        where = ranks(coords, experts, sign) * CAP + count
        return jnp.sum(jnp.where(hot, where, 0), axis=0, keepdims=True)

    d0, d1 = picked(hot0, 1), picked(hot1, 1)
    back = jnp.concatenate(
        [picked(hot0, -1), picked(hot1, -1), jnp.zeros((6, tokens), jnp.int32)], axis=0
    )
    dest_cols[...] = back.astype(F32).T

    many = 4 * CAP
    for r in range(0, 8, 2):
        slot = lax.broadcasted_iota(jnp.int32, (many, tokens), 0) + 2 * r * CAP
        hot = jnp.where((slot == d0) | (slot == d1), 1.0, 0.0).astype(BF16)
        out = lax.dot_general(
            hot, emb_t, (((1,), (1,)), ((), ())), preferred_element_type=F32
        ).astype(BF16)
        for i in range(2):
            at = 2 * i * CAP
            both = jnp.concatenate([out[at : at + CAP], out[at + CAP : at + 2 * CAP]], axis=1)
            if r < 4:
                keep[r + i] = both
            else:
                send[r + i - 4] = both
    base = plain.shape[1]
    half = own.shape[1]
    plain[...] = table[:, :base]
    own[...] = table[:, pl.ds(pl.multiple_of(base + coords[4] * half, 128), half)]
    away = base + (1 - coords[4]) * half
    width = p0.shape[1]
    for u, piece in enumerate((p0, p1, p2, p3)):
        piece[...] = table[:, pl.ds(pl.multiple_of(away + u * width, 128), width)]
    mine = coords[4] ^ coords[2]
    slot = lax.broadcasted_iota(jnp.int32, (CAP, tokens), 0) + mine * CAP
    eq0, eq1 = slot == d0, slot == d1
    w = jnp.where(eq0, gates[0:1, :], 0.0) + jnp.where(eq1, gates[1:2, :], 0.0)
    slot_w[:, 0:1] = jnp.sum(w, axis=1, keepdims=True)
    slot_w[:, 1:2] = jnp.sum(jnp.where(eq0, 1.0, 0.0), axis=1, keepdims=True)


def add_split_kernel(keep, got, *outs):
    for i, out in enumerate(outs):
        out[...] = (keep[i].astype(F32) + got[i].astype(F32)).astype(BF16)


def sum_split_kernel(coords, *refs):
    parts, (keep, send) = refs[:4], refs[4:]
    total = parts[0][...].astype(F32)
    for p in parts[1:]:
        total += p[...].astype(F32)
    n = keep.shape[1]
    left, right = total[:, :n], total[:, n:]
    first = (coords[4] ^ coords[2]) == 0
    keep[...] = jnp.where(first, left, right)
    send[...] = jnp.where(first, right, left).astype(BF16)


def pair_kernel(coords, own, got, out):
    first = (coords[4] ^ coords[2]) == 0
    a, b = own[...].astype(F32), got[...].astype(F32)
    out[...] = jnp.concatenate(
        [jnp.where(first, a, b).astype(BF16), jnp.where(first, b, a).astype(BF16)], axis=1
    )


def expert_kernel(coords, w_gate, w_up, w_down, *refs):
    blocks, (keep, send) = refs[:8], refs[8:]
    y, c, z = coords[0], coords[1], coords[3]
    acc = jnp.zeros((CAP, 256), F32)
    for r in range(8):
        s, dy = r // 4, r % 4
        at = (z - stride((y - dy) & 3, c ^ s)) & 7
        w = jnp.concatenate([w_gate[at], w_up[at]], axis=1)
        acc += jnp.dot(blocks[r][...], w, preferred_element_type=F32)
    gate, up = acc[:, :128], acc[:, 128:]
    hidden = (gate / (1.0 + jnp.exp(-gate)) * up).astype(BF16)
    wide = keep.shape[2]
    for s, out in ((0, keep), (1, send)):
        for dy in range(4):
            at = (z - stride((y + dy) & 3, c ^ s)) & 7
            w = w_down[:, pl.ds(pl.multiple_of(at * wide, 128), wide)]
            out[dy] = jnp.dot(hidden, w, preferred_element_type=F32).astype(BF16)


def combine_kernel(coords, dest_cols, *refs):
    blocks, (res, part), held = refs[:8], refs[8:-1], refs[-1]
    n = res.shape[1]
    for r in range(8):
        held[2 * r * CAP : (2 * r + 1) * CAP, :] = blocks[r][:, :n]
        held[(2 * r + 1) * CAP : (2 * r + 2) * CAP, :] = blocks[r][:, n:]
    tokens = dest_cols.shape[0]
    d0 = dest_cols[:, 0:1].astype(jnp.int32)
    d1 = dest_cols[:, 1:2].astype(jnp.int32)
    acc = jnp.zeros(res.shape, F32)
    step = 256
    for k in range(GROUP * CAP // step):
        at = lax.broadcasted_iota(jnp.int32, (tokens, step), 1) + k * step
        pick = jnp.where((at == d0) | (at == d1), 1.0, 0.0).astype(BF16)
        acc += jnp.dot(pick, held[k * step : (k + 1) * step, :], preferred_element_type=F32)
    res[...] = acc.astype(BF16)
    m = part.shape[0]
    at = coords[1] * 2 * m
    part[:, :n] = res[pl.ds(pl.multiple_of(at, 16), m), :]
    part[:, n:] = res[pl.ds(pl.multiple_of(at + m, 16), m), :]


def plain_logits_kernel(coords, res, table, *refs):
    outs, held = refs[:-1], refs[-1]
    z = coords[3]
    rows = res.shape[0] // Z
    for dz in range(Z):
        at = pl.ds(pl.multiple_of(((z + dz) & 7) * rows, 16), rows)
        held[dz * rows : (dz + 1) * rows, :] = res[at, :]
    step = 256
    for k in range(table.shape[1] // step):
        at = slice(k * step, (k + 1) * step)
        val = jnp.dot(held[...], table[:, at], preferred_element_type=F32).astype(BF16)
        for dz in range(Z):
            outs[dz][:, at] = val[dz * rows : (dz + 1) * rows, :]


def logits_kernel(dzs, coords, res, got_own, got_other, table, g0, g1, g2, g3, *refs):
    outs, (held, held_got, other) = refs[:-3], refs[-3:]
    c, z = coords[1], coords[3]
    m, n = got_own.shape[0], res.shape[1]
    for half, got in ((c, got_own), (1 - c, got_other)):
        other[pl.ds(pl.multiple_of(half * 2 * m, 16), m), :] = got[:, :n]
        other[pl.ds(pl.multiple_of(half * 2 * m + m, 16), m), :] = got[:, n:]
    rows = res.shape[0] // Z
    for i, dz in enumerate(dzs):
        at = pl.ds(pl.multiple_of(((z + dz) & 7) * rows, 16), rows)
        held[i * rows : (i + 1) * rows, :] = res[at, :]
        held_got[i * rows : (i + 1) * rows, :] = other[at, :]
    width = g0.shape[1]
    for k, got in enumerate((g0, g1, g2, g3)):
        val = jnp.dot(
            held[...], table[:, k * width : (k + 1) * width], preferred_element_type=F32
        )
        val += jnp.dot(held_got[...], got[...], preferred_element_type=F32)
        val = val.astype(BF16)
        u, at = k // 2, (k % 2) * width
        for i in range(len(dzs)):
            outs[2 * i + u][:, at : at + width] = val[i * rows : (i + 1) * rows, :]


def last_kernel(coords, own, below, above, keep, send, total):
    h = coords[4]
    n = keep.shape[0]
    total[...] = (
        own[...].astype(F32) + below[...].astype(F32) + above[...].astype(F32)
    ).astype(BF16)
    keep[...] = total[pl.ds(pl.multiple_of(h * n, 16), n), :]
    send[...] = total[pl.ds(pl.multiple_of((1 - h) * n, 16), n), :]


def output_kernel(coords, mine2, mine0, mine1, got2, got0, got1, out):
    h = coords[4]
    base, width = mine2.shape[1], mine0.shape[1]
    out[:, :base] = (mine2[...].astype(F32) + got2[...].astype(F32)).astype(BF16)
    for side, pieces in ((h, (mine0, mine1)), (1 - h, (got0, got1))):
        for u, x in enumerate(pieces):
            at = base + (2 * side + u) * width
            out[:, pl.ds(pl.multiple_of(at, 128), width)] = x[...]


def swap(x, axis):
    return lax.ppermute(x, axis, [(0, 1), (1, 0)])


def shift_y(x, dy):
    return lax.ppermute(x, "y", [(y, (y + dy) % Y) for y in range(Y)])


def shift_z(x, dz):
    return lax.ppermute(x, "z", [(z, (z + dz) % Z) for z in range(Z)])


def crossed(x, forward):
    pairs = []
    for y in range(Y):
        for c in range(C):
            far = y if c == 0 else (8 - y if y else 4)
            for v in range(V):
                for z in range(Z):
                    for h in range(H):
                        at = ((y * C + c) * V + v) * Z
                        a = (at + z) * H + h
                        b = (at + (z + far) % Z) * H + (h ^ v)
                        pairs.append((a, b) if forward else (b, a))
    return lax.ppermute(x, ALL, pairs)


def scatter_sum(coords, keep, send, piece):
    got = swap(send, "c")
    one = shape(keep.shape[1:])
    parts = list(call(add_split_kernel, [one] * 4, keep, got, smem=0, size=3 * keep.size * 2))
    parts[3], piece = lax.optimization_barrier((parts[3], piece))
    arrived = [shift_y(parts[dy], dy) for dy in (2, 1, 3)]
    piece = swap(piece, "h")
    arrived[0], piece = lax.optimization_barrier((arrived[0], piece))
    half = (one.shape[0], one.shape[1] // 2)
    own, away = call(
        sum_split_kernel,
        [shape(half, F32), shape(half)],
        coords,
        parts[0],
        *arrived,
        size=6 * parts[0].size * 2,
    )
    return (own + swap(away, "v").astype(F32)).astype(BF16), piece


def gather_all(coords, own, piece):
    got = swap(own, "v")
    pair = call(
        pair_kernel, shape((own.shape[0], 2 * own.shape[1])), coords, own, got, size=8 * own.size
    )
    pair, piece = lax.optimization_barrier((pair, piece))
    near = [pair, None, None, None]
    for dy in (2, 1, 3):
        near[dy] = shift_y(pair, dy)
    piece = swap(piece, "h")
    near[0], near[3] = lax.optimization_barrier((pair, near[3]))
    far = [swap(x, "c") for x in near]
    far[1], piece = lax.optimization_barrier((far[1], piece))
    return near + far, piece


def added(a, b):
    return (a.astype(F32) + b.astype(F32)).astype(BF16)


def per_device(token_ids, routes, gate_weights, embed_table, w_gate, w_up, w_down):
    vocab_rows, width = embed_table.shape
    tokens = token_ids.shape[0]
    coords = jnp.stack(
        [lax.axis_index(a) for a in ALL] + [lax.axis_index(PV), jnp.int32(0), jnp.int32(0)]
    ).astype(jnp.int32)
    table = embed_table.T
    base = vocab_rows // 4
    half = (vocab_rows - base) // 2
    piece = half // 4
    slots = (4, CAP, 2 * width)
    keep, send, dest_cols, slot_w, plain, own, *pieces = call(
        lookup_kernel,
        [shape(slots), shape(slots), shape((tokens, 8), F32), shape((CAP, 2), F32)]
        + [shape((width, base)), shape((width, half))]
        + [shape((width, piece))] * 4,
        coords,
        token_ids.reshape(1, tokens),
        routes.T,
        gate_weights.T,
        table,
        flops=2 * tokens * width * (vocab_rows + GROUP * CAP),
        size=8 * 1024 * 1024,
    )
    gots = [None] * 4
    rows_in, gots[0] = scatter_sum(coords, keep, send, pieces[0])
    blocks, gots[1] = gather_all(coords, crossed(rows_in, True), pieces[1])
    keep, send = call(
        expert_kernel,
        [shape(slots), shape(slots)],
        coords,
        w_gate.reshape(8, 2 * width, 128),
        w_up.reshape(8, 2 * width, 128),
        w_down[0],
        *blocks,
        flops=6 * CAP * GROUP * width * 128,
        size=10 * 1024 * 1024,
    )
    sums, gots[2] = scatter_sum(coords, keep, send, pieces[2])
    back = crossed(sums, False)
    back = (
        slot_w[:, 0:1] * back.astype(F32) + slot_w[:, 1:2] * rows_in.astype(F32)
    ).astype(BF16)
    blocks, gots[3] = gather_all(coords, back, pieces[3])
    res, part = call(
        combine_kernel,
        [shape((tokens, width)), shape((tokens // 4, 2 * width))],
        coords,
        dest_cols,
        *blocks,
        scratch=[pltpu.VMEM((GROUP * CAP, width), BF16)],
        flops=2 * tokens * GROUP * CAP * width,
        size=4 * 1024 * 1024,
    )
    got_own = swap(part, "h")
    got_other = swap(got_own, "c")
    rows = tokens // Z
    first = call(
        plain_logits_kernel,
        [shape((rows, base))] * Z,
        coords,
        res,
        plain,
        scratch=[pltpu.VMEM((tokens, width), BF16)],
        flops=2 * tokens * width * base,
        size=3 * 1024 * 1024,
    )
    down = [None, None, shift_z(first[4], -1)]
    up = [None, None, shift_z(first[3], 1)]
    outs = {}
    for dzs in ((4, 5, 3), (6, 2, 7, 1, 0)):
        m = len(dzs) * rows
        vals = call(
            functools.partial(logits_kernel, dzs),
            [shape((rows, half // 2))] * (2 * len(dzs)),
            coords,
            res,
            got_own,
            got_other,
            own,
            *gots,
            scratch=[
                pltpu.VMEM((m, width), BF16),
                pltpu.VMEM((m, width), BF16),
                pltpu.VMEM((tokens, width), BF16),
            ],
            flops=4 * m * width * half,
            size=6 * 1024 * 1024,
        )
        for i, dz in enumerate(dzs):
            outs[dz] = vals[2 * i : 2 * i + 2]
    for dz in (5, 6, 7):
        down[2] = shift_z(added(down[2], first[dz]), -1)
    for dz in (2, 1):
        up[2] = shift_z(added(up[2], first[dz]), 1)
    for u in (0, 1):
        up[u] = shift_z(outs[4][u], 1)
        down[u] = shift_z(outs[5][u], -1)
    for u in (0, 1):
        up[u] = shift_z(added(up[u], outs[3][u]), 1)
    for k in (2, 1):
        for u in (0, 1):
            down[u] = shift_z(added(down[u], outs[Z - k][u]), -1)
            up[u] = shift_z(added(up[u], outs[k][u]), 1)
    mine, got = [], []
    for u in (2, 0, 1):
        a = first[0] if u == 2 else outs[0][u]
        keep, send = call(
            last_kernel,
            [shape((rows // 2, a.shape[1]))] * 2,
            coords,
            a,
            down[u],
            up[u],
            scratch=[pltpu.VMEM(a.shape, BF16)],
            size=8 * a.size,
        )
        mine.append(keep)
        got.append(swap(send, "h"))
    return call(
        output_kernel,
        shape((rows // 2, vocab_rows)),
        coords,
        *mine,
        *got,
        size=4 * rows * vocab_rows,
    )


def solution(mesh):
    finer = Mesh(mesh.devices.reshape(Y, C, V, Z, H), ALL)
    return jax.shard_map(
        per_device,
        mesh=finer,
        in_specs=(
            P(),
            P(),
            P(),
            P(PV, EXPERT),
            P(EXPERT, None, PV),
            P(EXPERT, None, PV),
            P(EXPERT, PV, None),
        ),
        out_specs=P(EXPERT, PV),
        check_vma=False,
    )
```

```python
import functools

import jax
import jax.numpy as jnp
from jax import lax
from jax.experimental import pallas as pl
from jax.experimental.pallas import tpu as pltpu
from jax.sharding import Mesh
from jax.sharding import PartitionSpec as P

Y, C, V, Z, H = 4, 2, 2, 8, 2
ALL = ("y", "c", "v", "z", "h")
PV = ("y", "c", "v")
EXPERT = ("z", "h")
GROUP = 16
CAP = 144
BF16 = jnp.bfloat16
F32 = jnp.float32
LIMIT = 28 * 1024 * 1024

VMEM = pl.BlockSpec(memory_space=pltpu.VMEM)
SMEM = pl.BlockSpec(memory_space=pltpu.SMEM)


def call(kernel, out_shape, *args, smem=1, hbm=0, scratch=(), flops=0, size=0):
    return pl.pallas_call(
        kernel,
        out_shape=out_shape,
        in_specs=[SMEM] * smem
        + [VMEM] * (len(args) - smem - hbm)
        + [pl.BlockSpec(memory_space=pltpu.HBM)] * hbm,
        out_specs=jax.tree.map(lambda _: VMEM, out_shape),
        scratch_shapes=list(scratch),
        compiler_params=pltpu.CompilerParams(vmem_limit_bytes=LIMIT),
        cost_estimate=pl.CostEstimate(flops=flops, bytes_accessed=size, transcendentals=0),
    )(*args)


def shape(dims, dtype=BF16):
    return jax.ShapeDtypeStruct(dims, dtype)


def stride(y, c):
    return jnp.where(c == 0, y, jnp.where(y == 0, 4, 8 - y))


def ranks(coords, experts, sign):
    y, c, z = coords[0], coords[1], coords[3]
    d = (lax.shift_right_logical(experts, 1) - z) & 7
    cc = jnp.where(d >= 4, 1, 0)
    yy = jnp.where(d < 4, d, (8 - d) & 3)
    return ((cc ^ c) * 4 + ((sign * (yy - y)) & 3)) * 2 + (experts & 1)


def lookup_kernel(coords, ids, routes_far, gates_far, table_far, *refs):
    keep, send, dest_cols, slot_w, own, p0, p1, p2, p3 = refs[:9]
    routes, gates, table, small, large = refs[9:]
    copies = [
        pltpu.make_async_copy(routes_far, routes, small.at[0]),
        pltpu.make_async_copy(gates_far, gates, small.at[1]),
    ]
    tokens = ids.shape[1]
    rows = table.shape[1]
    step = 512
    block = rows // 4
    loads = []
    for b in range(4):
        at = pl.ds(b * block, block)
        loads.append(
            pltpu.make_async_copy(table_far.at[:, at], table.at[:, at], large.at[b])
        )
    for x in copies + loads:
        x.start()
    for x in copies:
        x.wait()
    experts = lax.broadcasted_iota(jnp.int32, (GROUP, tokens), 0)
    r0 = routes[0:1, :]
    r1 = routes[1:2, :]
    hot0 = experts == r0
    hot1 = experts == r1
    named = jnp.where(hot0 | hot1, 1.0, 0.0).astype(BF16)
    earlier = lax.broadcasted_iota(jnp.int32, (tokens, tokens), 0) < lax.broadcasted_iota(
        jnp.int32, (tokens, tokens), 1
    )
    count = jnp.dot(named, jnp.where(earlier, 1.0, 0.0).astype(BF16), preferred_element_type=F32)
    count = count.astype(jnp.int32)

    def picked(hot, sign):
        where = ranks(coords, experts, sign) * CAP + count
        return jnp.sum(jnp.where(hot, where, 0), axis=0, keepdims=True)

    d0, d1 = picked(hot0, 1), picked(hot1, 1)
    back = jnp.concatenate(
        [picked(hot0, -1), picked(hot1, -1), jnp.zeros((6, tokens), jnp.int32)], axis=0
    )
    dest_cols[...] = back.astype(F32).T

    mine = coords[4] ^ coords[2]
    slot = lax.broadcasted_iota(jnp.int32, (CAP, tokens), 0) + mine * CAP
    eq0, eq1 = slot == d0, slot == d1
    w = jnp.where(eq0, gates[0:1, :], 0.0) + jnp.where(eq1, gates[1:2, :], 0.0)
    slot_w[:, 0:1] = jnp.sum(w, axis=1, keepdims=True)
    slot_w[:, 1:2] = jnp.sum(jnp.where(eq0, 1.0, 0.0), axis=1, keepdims=True)

    base = ids[...] - coords[5] * rows
    acc = jnp.zeros((table.shape[0], tokens), F32)
    place = lax.broadcasted_iota(jnp.int32, (step, tokens), 0)
    for k in range(rows // step):
        if k * step % block == 0:
            loads[k * step // block].wait()
        hot = jnp.where(place == base - k * step, 1.0, 0.0).astype(BF16)
        acc += jnp.dot(table[:, k * step : (k + 1) * step], hot, preferred_element_type=F32)
    emb_t = acc.astype(BF16)

    many = 4 * CAP
    for r in range(0, 8, 2):
        slot = lax.broadcasted_iota(jnp.int32, (many, tokens), 0) + 2 * r * CAP
        hot = jnp.where((slot == d0) | (slot == d1), 1.0, 0.0).astype(BF16)
        out = lax.dot_general(
            hot, emb_t, (((1,), (1,)), ((), ())), preferred_element_type=F32
        ).astype(BF16)
        for i in range(2):
            at = 2 * i * CAP
            both = jnp.concatenate([out[at : at + CAP], out[at + CAP : at + 2 * CAP]], axis=1)
            if r < 4:
                keep[r + i] = both
            else:
                send[r + i - 4] = both
    half = own.shape[1]
    own[...] = table[:, pl.ds(pl.multiple_of(coords[4] * half, 128), half)]
    away = (1 - coords[4]) * half
    width = p0.shape[1]
    for u, piece in enumerate((p0, p1, p2, p3)):
        piece[...] = table[:, pl.ds(pl.multiple_of(away + u * width, 128), width)]


def add_split_kernel(keep, got, *outs):
    for i, out in enumerate(outs):
        out[...] = (keep[i].astype(F32) + got[i].astype(F32)).astype(BF16)


def sum_split_kernel(coords, *refs):
    parts, (keep, send) = refs[:4], refs[4:]
    total = parts[0][...].astype(F32)
    for p in parts[1:]:
        total += p[...].astype(F32)
    n = keep.shape[1]
    left, right = total[:, :n], total[:, n:]
    first = (coords[4] ^ coords[2]) == 0
    keep[...] = jnp.where(first, left, right)
    send[...] = jnp.where(first, right, left).astype(BF16)


def pair_kernel(coords, own, got, out):
    first = (coords[4] ^ coords[2]) == 0
    a, b = own[...].astype(F32), got[...].astype(F32)
    out[...] = jnp.concatenate(
        [jnp.where(first, a, b).astype(BF16), jnp.where(first, b, a).astype(BF16)], axis=1
    )


def expert_kernel(coords, w_gate, w_up, w_down, *refs):
    blocks, (keep, send) = refs[:8], refs[8:]
    y, c, z = coords[0], coords[1], coords[3]
    acc = jnp.zeros((CAP, 256), F32)
    for r in range(8):
        s, dy = r // 4, r % 4
        at = (z - stride((y - dy) & 3, c ^ s)) & 7
        w = jnp.concatenate([w_gate[at], w_up[at]], axis=1)
        acc += jnp.dot(blocks[r][...], w, preferred_element_type=F32)
    gate, up = acc[:, :128], acc[:, 128:]
    hidden = (gate / (1.0 + jnp.exp(-gate)) * up).astype(BF16)
    wide = keep.shape[2]
    for s, out in ((0, keep), (1, send)):
        for dy in range(4):
            at = (z - stride((y + dy) & 3, c ^ s)) & 7
            w = w_down[:, pl.ds(pl.multiple_of(at * wide, 128), wide)]
            out[dy] = jnp.dot(hidden, w, preferred_element_type=F32).astype(BF16)


def combine_kernel(coords, dest_cols, *refs):
    blocks, (res, part), held = refs[:8], refs[8:-1], refs[-1]
    n = res.shape[1]
    for r in range(8):
        held[2 * r * CAP : (2 * r + 1) * CAP, :] = blocks[r][:, :n]
        held[(2 * r + 1) * CAP : (2 * r + 2) * CAP, :] = blocks[r][:, n:]
    tokens = dest_cols.shape[0]
    d0 = dest_cols[:, 0:1].astype(jnp.int32)
    d1 = dest_cols[:, 1:2].astype(jnp.int32)
    acc = jnp.zeros(res.shape, F32)
    step = 256
    for k in range(GROUP * CAP // step):
        at = lax.broadcasted_iota(jnp.int32, (tokens, step), 1) + k * step
        pick = jnp.where((at == d0) | (at == d1), 1.0, 0.0).astype(BF16)
        acc += jnp.dot(pick, held[k * step : (k + 1) * step, :], preferred_element_type=F32)
    res[...] = acc.astype(BF16)
    m = part.shape[0]
    at = coords[1] * 2 * m
    part[:, :n] = res[pl.ds(pl.multiple_of(at, 16), m), :]
    part[:, n:] = res[pl.ds(pl.multiple_of(at + m, 16), m), :]


def own_logits_kernel(dzs, coords, res, table, out, held):
    z = coords[3]
    rows = res.shape[0] // Z
    for i, dz in enumerate(dzs):
        at = pl.ds(pl.multiple_of(((z + dz) & 7) * rows, 16), rows)
        held[i * rows : (i + 1) * rows, :] = res[at, :]
    step = 512
    for k in range(table.shape[1] // step):
        at = slice(k * step, (k + 1) * step)
        out[:, at] = jnp.dot(held[...], table[:, at], preferred_element_type=F32)


def logits_kernel(dzs, coords, first, got_own, got_other, g0, g1, g2, g3, *refs):
    outs, (held, other) = refs[:-2], refs[-2:]
    c, z = coords[1], coords[3]
    m, n = got_own.shape[0], held.shape[1]
    for half, got in ((c, got_own), (1 - c, got_other)):
        other[pl.ds(pl.multiple_of(half * 2 * m, 16), m), :] = got[:, :n]
        other[pl.ds(pl.multiple_of(half * 2 * m + m, 16), m), :] = got[:, n:]
    rows = other.shape[0] // Z
    for i, dz in enumerate(dzs):
        at = pl.ds(pl.multiple_of(((z + dz) & 7) * rows, 16), rows)
        held[i * rows : (i + 1) * rows, :] = other[at, :]
    width = g0.shape[1]
    for k, got in enumerate((g0, g1, g2, g3)):
        val = first[:, k * width : (k + 1) * width]
        val += jnp.dot(held[...], got[...], preferred_element_type=F32)
        val = val.astype(BF16)
        u, at = k // 2, (k % 2) * width
        for i in range(len(dzs)):
            outs[2 * i + u][:, at : at + width] = val[i * rows : (i + 1) * rows, :]


def last_kernel(coords, own, below, above, keep, send, total):
    h = coords[4]
    n = keep.shape[0]
    total[...] = (
        own[...].astype(F32) + below[...].astype(F32) + above[...].astype(F32)
    ).astype(BF16)
    keep[...] = total[pl.ds(pl.multiple_of(h * n, 16), n), :]
    send[...] = total[pl.ds(pl.multiple_of((1 - h) * n, 16), n), :]


def swap(x, axis):
    return lax.ppermute(x, axis, [(0, 1), (1, 0)])


def shift_y(x, dy):
    return lax.ppermute(x, "y", [(y, (y + dy) % Y) for y in range(Y)])


def shift_z(x, dz):
    return lax.ppermute(x, "z", [(z, (z + dz) % Z) for z in range(Z)])


def crossed(x, forward):
    pairs = []
    for y in range(Y):
        for c in range(C):
            far = y if c == 0 else (8 - y if y else 4)
            for v in range(V):
                for z in range(Z):
                    for h in range(H):
                        at = ((y * C + c) * V + v) * Z
                        a = (at + z) * H + h
                        b = (at + (z + far) % Z) * H + (h ^ v)
                        pairs.append((a, b) if forward else (b, a))
    return lax.ppermute(x, ALL, pairs)


def scatter_sum(coords, keep, send, piece):
    got = swap(send, "c")
    one = shape(keep.shape[1:])
    parts = list(call(add_split_kernel, [one] * 4, keep, got, smem=0, size=3 * keep.size * 2))
    parts[3], piece = lax.optimization_barrier((parts[3], piece))
    arrived = [shift_y(parts[dy], dy) for dy in (2, 1, 3)]
    piece = swap(piece, "h")
    arrived[0], piece = lax.optimization_barrier((arrived[0], piece))
    half = (one.shape[0], one.shape[1] // 2)
    own, away = call(
        sum_split_kernel,
        [shape(half, F32), shape(half)],
        coords,
        parts[0],
        *arrived,
        size=6 * parts[0].size * 2,
    )
    return (own + swap(away, "v").astype(F32)).astype(BF16), piece


def gather_all(coords, own, piece):
    got = swap(own, "v")
    pair = call(
        pair_kernel, shape((own.shape[0], 2 * own.shape[1])), coords, own, got, size=8 * own.size
    )
    pair, piece = lax.optimization_barrier((pair, piece))
    near = [pair, None, None, None]
    for dy in (2, 1, 3):
        near[dy] = shift_y(pair, dy)
    piece = swap(piece, "h")
    near[0], near[3] = lax.optimization_barrier((pair, near[3]))
    far = [swap(x, "c") for x in near]
    far[1], piece = lax.optimization_barrier((far[1], piece))
    return near + far, piece


def added(a, b):
    return (a.astype(F32) + b.astype(F32)).astype(BF16)


def per_device(token_ids, routes, gate_weights, embed_table, w_gate, w_up, w_down):
    vocab_rows, width = embed_table.shape
    tokens = token_ids.shape[0]
    coords = jnp.stack(
        [lax.axis_index(a) for a in ALL] + [lax.axis_index(PV), jnp.int32(0), jnp.int32(0)]
    ).astype(jnp.int32)
    table = embed_table.T
    h = lax.axis_index("h")
    eighth = vocab_rows // 8
    quarter = 2 * eighth
    half = 2 * quarter
    slots = (4, CAP, 2 * width)
    keep, send, dest_cols, slot_w, own, *pieces = call(
        lookup_kernel,
        [shape(slots), shape(slots), shape((tokens, 8), F32), shape((CAP, 2), F32)]
        + [shape((width, 2 * quarter))]
        + [shape((width, eighth))] * 4,
        coords,
        token_ids.reshape(1, tokens),
        *[
            pltpu.with_memory_space_constraint(x, pltpu.HBM)
            for x in (routes.T, gate_weights.T, table)
        ],
        hbm=3,
        scratch=[
            pltpu.VMEM((2, tokens), jnp.int32),
            pltpu.VMEM((2, tokens), F32),
            pltpu.VMEM((width, vocab_rows), BF16),
            pltpu.SemaphoreType.DMA((2,)),
            pltpu.SemaphoreType.DMA((4,)),
        ],
        flops=2 * tokens * width * (vocab_rows + GROUP * CAP),
        size=8 * 1024 * 1024,
    )
    gots = [None] * 4
    rows_in, gots[0] = scatter_sum(coords, keep, send, pieces[0])
    blocks, gots[1] = gather_all(coords, crossed(rows_in, True), pieces[1])
    keep, send = call(
        expert_kernel,
        [shape(slots), shape(slots)],
        coords,
        w_gate.reshape(8, 2 * width, 128),
        w_up.reshape(8, 2 * width, 128),
        w_down[0],
        *blocks,
        flops=6 * CAP * GROUP * width * 128,
        size=10 * 1024 * 1024,
    )
    sums, gots[2] = scatter_sum(coords, keep, send, pieces[2])
    back = crossed(sums, False)
    back = (
        slot_w[:, 0:1] * back.astype(F32) + slot_w[:, 1:2] * rows_in.astype(F32)
    ).astype(BF16)
    blocks, gots[3] = gather_all(coords, back, pieces[3])
    res, part = call(
        combine_kernel,
        [shape((tokens, width)), shape((tokens // 4, 2 * width))],
        coords,
        dest_cols,
        *blocks,
        scratch=[pltpu.VMEM((GROUP * CAP, width), BF16)],
        flops=2 * tokens * GROUP * CAP * width,
        size=4 * 1024 * 1024,
    )
    got_own = swap(part, "h")
    rows = tokens // Z
    outs = {}
    orders = ((4, 5, 3), (6, 2, 7, 1, 0))
    firsts = []
    for dzs in orders:
        m = len(dzs) * rows
        firsts.append(
            call(
                functools.partial(own_logits_kernel, dzs),
                shape((m, half), F32),
                coords,
                res,
                own,
                scratch=[pltpu.VMEM((m, width), BF16)],
                flops=2 * m * width * half,
                size=6 * 1024 * 1024,
            )
        )
    got_own, *firsts = lax.optimization_barrier((got_own, *firsts))
    got_other = swap(got_own, "c")
    for dzs, first in zip(orders, firsts):
        m = len(dzs) * rows
        vals = call(
            functools.partial(logits_kernel, dzs),
            [shape((rows, quarter))] * (2 * len(dzs)),
            coords,
            first,
            got_own,
            got_other,
            *gots,
            scratch=[pltpu.VMEM((m, width), BF16), pltpu.VMEM((tokens, width), BF16)],
            flops=2 * m * width * half,
            size=6 * 1024 * 1024,
        )
        for i, dz in enumerate(dzs):
            outs[dz] = vals[2 * i : 2 * i + 2]
    down = [shift_z(outs[4][0], -1), None]
    up = [None, shift_z(outs[4][1], 1)]
    down[1] = shift_z(outs[5][1], -1)
    up[0] = shift_z(outs[3][0], 1)
    down[0] = shift_z(added(down[0], outs[5][0]), -1)
    up[1] = shift_z(added(up[1], outs[3][1]), 1)
    for k in (2, 1):
        for u in (1, 0):
            down[u] = shift_z(added(down[u], outs[Z - k][u]), -1)
            up[1 - u] = shift_z(added(up[1 - u], outs[k][1 - u]), 1)
    mine, got = [], []
    for u in range(2):
        keep, send = call(
            last_kernel,
            [shape((rows // 2, quarter))] * 2,
            coords,
            outs[0][u],
            down[u],
            up[u],
            scratch=[pltpu.VMEM((rows, quarter), BF16)],
            size=8 * rows * quarter,
        )
        mine.append(keep)
        got.append(swap(send, "h"))
    return jnp.where(
        h == 0, jnp.concatenate(mine + got, axis=1), jnp.concatenate(got + mine, axis=1)
    )


def solution(mesh):
    finer = Mesh(mesh.devices.reshape(Y, C, V, Z, H), ALL)
    return jax.shard_map(
        per_device,
        mesh=finer,
        in_specs=(
            P(),
            P(),
            P(),
            P(PV, EXPERT),
            P(EXPERT, None, PV),
            P(EXPERT, None, PV),
            P(EXPERT, PV, None),
        ),
        out_specs=P(EXPERT, PV),
        check_vma=False,
    )
```

```python
import functools

import jax
import jax.numpy as jnp
from jax import lax
from jax.experimental import pallas as pl
from jax.experimental.pallas import tpu as pltpu
from jax.sharding import Mesh
from jax.sharding import PartitionSpec as P

Y, C, V, Z, H = 4, 2, 2, 8, 2
ALL = ("y", "c", "v", "z", "h")
PV = ("y", "c", "v")
EXPERT = ("z", "h")
GROUP = 16
CAP = 144
BF16 = jnp.bfloat16
F32 = jnp.float32
LIMIT = 28 * 1024 * 1024

VMEM = pl.BlockSpec(memory_space=pltpu.VMEM)
SMEM = pl.BlockSpec(memory_space=pltpu.SMEM)


def call(kernel, out_shape, *args, smem=1, hbm=0, scratch=(), flops=0, size=0):
    return pl.pallas_call(
        kernel,
        out_shape=out_shape,
        in_specs=[SMEM] * smem
        + [VMEM] * (len(args) - smem - hbm)
        + [pl.BlockSpec(memory_space=pltpu.HBM)] * hbm,
        out_specs=jax.tree.map(lambda _: VMEM, out_shape),
        scratch_shapes=list(scratch),
        compiler_params=pltpu.CompilerParams(vmem_limit_bytes=LIMIT),
        cost_estimate=pl.CostEstimate(flops=flops, bytes_accessed=size, transcendentals=0),
    )(*args)


def shape(dims, dtype=BF16):
    return jax.ShapeDtypeStruct(dims, dtype)


def stride(y, c):
    return jnp.where(c == 0, y, jnp.where(y == 0, 4, 8 - y))


def ranks(coords, experts, sign):
    y, c, z = coords[0], coords[1], coords[3]
    d = (lax.shift_right_logical(experts, 1) - z) & 7
    cc = jnp.where(d >= 4, 1, 0)
    yy = jnp.where(d < 4, d, (8 - d) & 3)
    return ((cc ^ c) * 4 + ((sign * (yy - y)) & 3)) * 2 + (experts & 1)


def spread(dest_rows, emb_t, out, start):
    tokens = dest_rows.shape[1]
    d0, d1 = dest_rows[0:1, :], dest_rows[1:2, :]
    many = 4 * CAP
    for r in range(0, 4, 2):
        slot = lax.broadcasted_iota(jnp.int32, (many, tokens), 0) + 2 * (start + r) * CAP
        hot = jnp.where((slot == d0) | (slot == d1), 1.0, 0.0).astype(BF16)
        rows = lax.dot_general(
            hot, emb_t, (((1,), (1,)), ((), ())), preferred_element_type=F32
        ).astype(BF16)
        for i in range(2):
            at = 2 * i * CAP
            out[r + i] = jnp.concatenate(
                [rows[at : at + CAP], rows[at + CAP : at + 2 * CAP]], axis=1
            )


def lookup_kernel(coords, ids, routes_far, table_far, *refs):
    send, emb_t, dest_rows, routes, table, small, large = refs
    load_routes = pltpu.make_async_copy(routes_far, routes, small)
    tokens = ids.shape[1]
    rows = table.shape[1]
    step = 512
    block = rows // 4
    loads = []
    for b in range(4):
        at = pl.ds(b * block, block)
        loads.append(
            pltpu.make_async_copy(table_far.at[:, at], table.at[:, at], large.at[b])
        )
    load_routes.start()
    for x in loads:
        x.start()
    load_routes.wait()
    experts = lax.broadcasted_iota(jnp.int32, (GROUP, tokens), 0)
    hot0 = experts == routes[0:1, :]
    hot1 = experts == routes[1:2, :]
    named = jnp.where(hot0 | hot1, 1.0, 0.0).astype(BF16)
    earlier = lax.broadcasted_iota(jnp.int32, (tokens, tokens), 0) < lax.broadcasted_iota(
        jnp.int32, (tokens, tokens), 1
    )
    count = jnp.dot(named, jnp.where(earlier, 1.0, 0.0).astype(BF16), preferred_element_type=F32)
    count = count.astype(jnp.int32)

    def picked(hot, sign):
        where = ranks(coords, experts, sign) * CAP + count
        return jnp.sum(jnp.where(hot, where, 0), axis=0, keepdims=True)

    dest_rows[...] = jnp.concatenate(
        [picked(hot0, 1), picked(hot1, 1), picked(hot0, -1), picked(hot1, -1)]
        + [jnp.zeros((4, tokens), jnp.int32)],
        axis=0,
    )
    base = ids[...] - coords[5] * rows
    acc = jnp.zeros((table.shape[0], tokens), F32)
    place = lax.broadcasted_iota(jnp.int32, (step, tokens), 0)
    for k in range(rows // step):
        if k * step % block == 0:
            loads[k * step // block].wait()
        hot = jnp.where(place == base - k * step, 1.0, 0.0).astype(BF16)
        acc += jnp.dot(table[:, k * step : (k + 1) * step], hot, preferred_element_type=F32)
    emb_t[...] = acc.astype(BF16)
    spread(dest_rows, emb_t[...], send, 4)


def rest_kernel(coords, dest_rows, emb_t, table_far, keep, own, p0, p1, p2, p3, sems):
    half = own.shape[1]
    width = p0.shape[1]
    at = pl.multiple_of(coords[4] * half, 128)
    loads = [pltpu.make_async_copy(table_far.at[:, pl.ds(at, half)], own, sems.at[4])]
    for u, piece in enumerate((p0, p1, p2, p3)):
        at = pl.multiple_of((1 - coords[4]) * half + u * width, 128)
        loads.append(
            pltpu.make_async_copy(table_far.at[:, pl.ds(at, width)], piece, sems.at[u])
        )
    for x in loads:
        x.start()
    spread(dest_rows, emb_t[...], keep, 0)
    for x in loads:
        x.wait()


def slots_kernel(coords, dest_rows, gates_far, dest_cols, slot_w, gates, sem):
    load = pltpu.make_async_copy(gates_far, gates, sem)
    load.start()
    tokens = dest_rows.shape[1]
    dest_cols[...] = dest_rows[...].astype(F32).T
    mine = coords[4] ^ coords[2]
    slot = lax.broadcasted_iota(jnp.int32, (CAP, tokens), 0) + mine * CAP
    eq0, eq1 = slot == dest_rows[0:1, :], slot == dest_rows[1:2, :]
    load.wait()
    w = jnp.where(eq0, gates[0:1, :], 0.0) + jnp.where(eq1, gates[1:2, :], 0.0)
    slot_w[:, 0:1] = jnp.sum(w, axis=1, keepdims=True)
    slot_w[:, 1:2] = jnp.sum(jnp.where(eq0, 1.0, 0.0), axis=1, keepdims=True)


def add_split_kernel(keep, got, *outs):
    for i, out in enumerate(outs):
        out[...] = (keep[i].astype(F32) + got[i].astype(F32)).astype(BF16)


def sum_split_kernel(coords, *refs):
    parts, (keep, send) = refs[:4], refs[4:]
    total = parts[0][...].astype(F32)
    for p in parts[1:]:
        total += p[...].astype(F32)
    n = keep.shape[1]
    left, right = total[:, :n], total[:, n:]
    first = (coords[4] ^ coords[2]) == 0
    keep[...] = jnp.where(first, left, right)
    send[...] = jnp.where(first, right, left).astype(BF16)


def pair_kernel(coords, own, got, out):
    first = (coords[4] ^ coords[2]) == 0
    a, b = own[...].astype(F32), got[...].astype(F32)
    out[...] = jnp.concatenate(
        [jnp.where(first, a, b).astype(BF16), jnp.where(first, b, a).astype(BF16)], axis=1
    )


def down_half(coords, hidden, w_down, out, s):
    y, c, z = coords[0], coords[1], coords[3]
    wide = out.shape[2]
    for dy in range(4):
        at = (z - stride((y + dy) & 3, c ^ s)) & 7
        w = w_down[:, pl.ds(pl.multiple_of(at * wide, 128), wide)]
        out[dy] = jnp.dot(hidden, w, preferred_element_type=F32).astype(BF16)


def expert_kernel(coords, w_gate, w_up, w_down, *refs):
    blocks, (send, hidden) = refs[:8], refs[8:]
    y, c, z = coords[0], coords[1], coords[3]
    acc = jnp.zeros((CAP, 256), F32)
    for r in range(8):
        s, dy = r // 4, r % 4
        at = (z - stride((y - dy) & 3, c ^ s)) & 7
        w = jnp.concatenate([w_gate[at], w_up[at]], axis=1)
        acc += jnp.dot(blocks[r][...], w, preferred_element_type=F32)
    gate, up = acc[:, :128], acc[:, 128:]
    hidden[...] = (gate / (1.0 + jnp.exp(-gate)) * up).astype(BF16)
    down_half(coords, hidden[...], w_down, send, 1)


def expert_rest_kernel(coords, hidden, w_down, keep):
    down_half(coords, hidden[...], w_down, keep, 0)


def picked_sum(dest_cols, at, m, held):
    d0 = dest_cols[pl.ds(at, m), 2:3].astype(jnp.int32)
    d1 = dest_cols[pl.ds(at, m), 3:4].astype(jnp.int32)
    acc = jnp.zeros((m, held.shape[1]), F32)
    step = 256
    for k in range(GROUP * CAP // step):
        place = lax.broadcasted_iota(jnp.int32, (m, step), 1) + k * step
        pick = jnp.where((place == d0) | (place == d1), 1.0, 0.0).astype(BF16)
        acc += jnp.dot(pick, held[k * step : (k + 1) * step, :], preferred_element_type=F32)
    return acc.astype(BF16)


def combine_kernel(coords, dest_cols, *refs):
    blocks, (part, held) = refs[:8], refs[8:]
    n = held.shape[1]
    for r in range(8):
        held[2 * r * CAP : (2 * r + 1) * CAP, :] = blocks[r][:, :n]
        held[(2 * r + 1) * CAP : (2 * r + 2) * CAP, :] = blocks[r][:, n:]
    m = part.shape[0]
    rows = picked_sum(dest_cols, pl.multiple_of(coords[1] * 2 * m, 16), 2 * m, held)
    part[:, :n] = rows[:m]
    part[:, n:] = rows[m:]


def combine_rest_kernel(coords, dest_cols, held, part, res):
    m, n = part.shape[0], held.shape[1]
    at = coords[1] * 2 * m
    res[pl.ds(pl.multiple_of(at, 16), m), :] = part[:, :n]
    res[pl.ds(pl.multiple_of(at + m, 16), m), :] = part[:, n:]
    at = pl.multiple_of((1 - coords[1]) * 2 * m, 16)
    res[pl.ds(at, 2 * m), :] = picked_sum(dest_cols, at, 2 * m, held)


def own_logits_kernel(dzs, coords, res, table, out, held):
    z = coords[3]
    rows = res.shape[0] // Z
    for i, dz in enumerate(dzs):
        at = pl.ds(pl.multiple_of(((z + dz) & 7) * rows, 16), rows)
        held[i * rows : (i + 1) * rows, :] = res[at, :]
    step = 512
    for k in range(table.shape[1] // step):
        at = slice(k * step, (k + 1) * step)
        out[:, at] = jnp.dot(held[...], table[:, at], preferred_element_type=F32)


def logits_kernel(dzs, coords, first, got_own, got_other, g0, g1, g2, g3, *refs):
    outs, (held, other) = refs[:-2], refs[-2:]
    c, z = coords[1], coords[3]
    m, n = got_own.shape[0], held.shape[1]
    for half, got in ((c, got_own), (1 - c, got_other)):
        other[pl.ds(pl.multiple_of(half * 2 * m, 16), m), :] = got[:, :n]
        other[pl.ds(pl.multiple_of(half * 2 * m + m, 16), m), :] = got[:, n:]
    rows = other.shape[0] // Z
    for i, dz in enumerate(dzs):
        at = pl.ds(pl.multiple_of(((z + dz) & 7) * rows, 16), rows)
        held[i * rows : (i + 1) * rows, :] = other[at, :]
    width = g0.shape[1]
    for k, got in enumerate((g0, g1, g2, g3)):
        val = first[:, k * width : (k + 1) * width]
        val += jnp.dot(held[...], got[...], preferred_element_type=F32)
        val = val.astype(BF16)
        u, at = k // 2, (k % 2) * width
        for i in range(len(dzs)):
            outs[2 * i + u][:, at : at + width] = val[i * rows : (i + 1) * rows, :]


def last_kernel(coords, own, below, above, keep, send, total):
    h = coords[4]
    n = keep.shape[0]
    total[...] = (
        own[...].astype(F32) + below[...].astype(F32) + above[...].astype(F32)
    ).astype(BF16)
    keep[...] = total[pl.ds(pl.multiple_of(h * n, 16), n), :]
    send[...] = total[pl.ds(pl.multiple_of((1 - h) * n, 16), n), :]


def swap(x, axis):
    return lax.ppermute(x, axis, [(0, 1), (1, 0)])


def shift_y(x, dy):
    return lax.ppermute(x, "y", [(y, (y + dy) % Y) for y in range(Y)])


def shift_z(x, dz):
    return lax.ppermute(x, "z", [(z, (z + dz) % Z) for z in range(Z)])


def crossed(x, forward):
    pairs = []
    for y in range(Y):
        for c in range(C):
            far = y if c == 0 else (8 - y if y else 4)
            for v in range(V):
                for z in range(Z):
                    for h in range(H):
                        at = ((y * C + c) * V + v) * Z
                        a = (at + z) * H + h
                        b = (at + (z + far) % Z) * H + (h ^ v)
                        pairs.append((a, b) if forward else (b, a))
    return lax.ppermute(x, ALL, pairs)


def scatter_sum(coords, keep, send, piece):
    got = swap(send, "c")
    one = shape(keep.shape[1:])
    parts = list(call(add_split_kernel, [one] * 4, keep, got, smem=0, size=3 * keep.size * 2))
    parts[3], piece = lax.optimization_barrier((parts[3], piece))
    arrived = [shift_y(parts[dy], dy) for dy in (2, 1, 3)]
    piece = swap(piece, "h")
    arrived[0], piece = lax.optimization_barrier((arrived[0], piece))
    half = (one.shape[0], one.shape[1] // 2)
    own, away = call(
        sum_split_kernel,
        [shape(half, F32), shape(half)],
        coords,
        parts[0],
        *arrived,
        size=6 * parts[0].size * 2,
    )
    return (own + swap(away, "v").astype(F32)).astype(BF16), piece


def gather_all(coords, own, piece):
    got = swap(own, "v")
    pair = call(
        pair_kernel, shape((own.shape[0], 2 * own.shape[1])), coords, own, got, size=8 * own.size
    )
    pair, piece = lax.optimization_barrier((pair, piece))
    near = [pair, None, None, None]
    for dy in (2, 1, 3):
        near[dy] = shift_y(pair, dy)
    piece = swap(piece, "h")
    near[0], near[3] = lax.optimization_barrier((pair, near[3]))
    far = [swap(x, "c") for x in near]
    far[1], piece = lax.optimization_barrier((far[1], piece))
    return near + far, piece


def added(a, b):
    return (a.astype(F32) + b.astype(F32)).astype(BF16)


def per_device(token_ids, routes, gate_weights, embed_table, w_gate, w_up, w_down):
    vocab_rows, width = embed_table.shape
    tokens = token_ids.shape[0]
    coords = jnp.stack(
        [lax.axis_index(a) for a in ALL] + [lax.axis_index(PV), jnp.int32(0), jnp.int32(0)]
    ).astype(jnp.int32)
    table = embed_table.T
    h = lax.axis_index("h")
    eighth = vocab_rows // 8
    quarter = 2 * eighth
    half = 2 * quarter
    slots = (4, CAP, 2 * width)
    def far(x):
        return pltpu.with_memory_space_constraint(x, pltpu.HBM)

    table = far(table)
    send, emb_t, dest_rows = call(
        lookup_kernel,
        [shape(slots), shape((width, tokens)), shape((8, tokens), jnp.int32)],
        coords,
        token_ids.reshape(1, tokens),
        far(routes.T),
        table,
        hbm=2,
        scratch=[
            pltpu.VMEM((2, tokens), jnp.int32),
            pltpu.VMEM((width, vocab_rows), BF16),
            pltpu.SemaphoreType.DMA,
            pltpu.SemaphoreType.DMA((4,)),
        ],
        flops=2 * tokens * width * (vocab_rows + GROUP * CAP),
        size=6 * 1024 * 1024,
    )
    keep, own, *pieces = call(
        rest_kernel,
        [shape(slots), shape((width, half))] + [shape((width, eighth))] * 4,
        coords,
        dest_rows,
        emb_t,
        table,
        hbm=1,
        scratch=[pltpu.SemaphoreType.DMA((5,))],
        flops=2 * tokens * width * GROUP * CAP // 2,
        size=6 * 1024 * 1024,
    )
    dest_cols, slot_w = call(
        slots_kernel,
        [shape((tokens, 8), F32), shape((CAP, 2), F32)],
        coords,
        dest_rows,
        far(gate_weights.T),
        hbm=1,
        scratch=[pltpu.VMEM((2, tokens), F32), pltpu.SemaphoreType.DMA],
        flops=tokens * CAP,
        size=512 * 1024,
    )
    gots = [None] * 4
    rows_in, gots[0] = scatter_sum(coords, keep, send, pieces[0])
    blocks, gots[1] = gather_all(coords, crossed(rows_in, True), pieces[1])
    send, hidden = call(
        expert_kernel,
        [shape(slots), shape((CAP, 128))],
        coords,
        w_gate.reshape(8, 2 * width, 128),
        w_up.reshape(8, 2 * width, 128),
        w_down[0],
        *blocks,
        flops=5 * CAP * GROUP * width * 128,
        size=9 * 1024 * 1024,
    )
    keep = call(
        expert_rest_kernel,
        shape(slots),
        coords,
        hidden,
        w_down[0],
        flops=CAP * GROUP * width * 128,
        size=3 * 1024 * 1024,
    )
    sums, gots[2] = scatter_sum(coords, keep, send, pieces[2])
    back = crossed(sums, False)
    back = (
        slot_w[:, 0:1] * back.astype(F32) + slot_w[:, 1:2] * rows_in.astype(F32)
    ).astype(BF16)
    blocks, gots[3] = gather_all(coords, back, pieces[3])
    part, held = call(
        combine_kernel,
        [shape((tokens // 4, 2 * width)), shape((GROUP * CAP, width))],
        coords,
        dest_cols,
        *blocks,
        flops=tokens * GROUP * CAP * width,
        size=5 * 1024 * 1024,
    )
    res = call(
        combine_rest_kernel,
        shape((tokens, width)),
        coords,
        dest_cols,
        held,
        part,
        flops=tokens * GROUP * CAP * width,
        size=3 * 1024 * 1024,
    )
    got_own = swap(part, "h")
    rows = tokens // Z
    outs = {}
    orders = ((4,), (5, 3, 6, 2, 7, 1, 0))
    firsts = []
    for dzs in orders:
        m = len(dzs) * rows
        firsts.append(
            call(
                functools.partial(own_logits_kernel, dzs),
                shape((m, half), F32),
                coords,
                res,
                own,
                scratch=[pltpu.VMEM((m, width), BF16)],
                flops=2 * m * width * half,
                size=6 * 1024 * 1024,
            )
        )
    got_own, *firsts = lax.optimization_barrier((got_own, *firsts))
    got_other = swap(got_own, "c")
    for k, dzs in enumerate(orders):
        m = len(dzs) * rows
        vals = call(
            functools.partial(logits_kernel, dzs),
            [shape((rows, quarter))] * (2 * len(dzs)),
            coords,
            firsts[k],
            got_own,
            got_other,
            *gots,
            scratch=[pltpu.VMEM((m, width), BF16), pltpu.VMEM((tokens, width), BF16)],
            flops=2 * m * width * half,
            size=6 * 1024 * 1024,
        )
        for i, dz in enumerate(dzs):
            outs[dz] = vals[2 * i : 2 * i + 2]
        if dzs == orders[0]:
            _, firsts[1] = lax.optimization_barrier((vals[0], firsts[1]))
    down = [shift_z(outs[4][0], -1), None]
    up = [None, shift_z(outs[4][1], 1)]
    down[1] = shift_z(outs[5][1], -1)
    up[0] = shift_z(outs[3][0], 1)
    down[0] = shift_z(added(down[0], outs[5][0]), -1)
    up[1] = shift_z(added(up[1], outs[3][1]), 1)
    for k in (2, 1):
        for u in (1, 0):
            down[u] = shift_z(added(down[u], outs[Z - k][u]), -1)
            up[1 - u] = shift_z(added(up[1 - u], outs[k][1 - u]), 1)
    mine, got = [], []
    for u in range(2):
        keep, send = call(
            last_kernel,
            [shape((rows // 2, quarter))] * 2,
            coords,
            outs[0][u],
            down[u],
            up[u],
            scratch=[pltpu.VMEM((rows, quarter), BF16)],
            size=8 * rows * quarter,
        )
        mine.append(keep)
        got.append(swap(send, "h"))
    return jnp.where(
        h == 0, jnp.concatenate(mine + got, axis=1), jnp.concatenate(got + mine, axis=1)
    )


def solution(mesh):
    finer = Mesh(mesh.devices.reshape(Y, C, V, Z, H), ALL)
    return jax.shard_map(
        per_device,
        mesh=finer,
        in_specs=(
            P(),
            P(),
            P(),
            P(PV, EXPERT),
            P(EXPERT, None, PV),
            P(EXPERT, None, PV),
            P(EXPERT, PV, None),
        ),
        out_specs=P(EXPERT, PV),
        check_vma=False,
    )
```

```python
import functools

import jax
import jax.numpy as jnp
from jax import lax
from jax.experimental import pallas as pl
from jax.experimental.pallas import tpu as pltpu
from jax.sharding import Mesh
from jax.sharding import PartitionSpec as P

Y, C, V, Z, H = 4, 2, 2, 8, 2
ALL = ("y", "c", "v", "z", "h")
PV = ("y", "c", "v")
EXPERT = ("z", "h")
GROUP = 16
CAP = 144
BF16 = jnp.bfloat16
F32 = jnp.float32
LIMIT = 28 * 1024 * 1024

VMEM = pl.BlockSpec(memory_space=pltpu.VMEM)
SMEM = pl.BlockSpec(memory_space=pltpu.SMEM)


def call(kernel, out_shape, *args, smem=1, hbm=0, scratch=(), flops=0, size=0):
    return pl.pallas_call(
        kernel,
        out_shape=out_shape,
        in_specs=[SMEM] * smem
        + [VMEM] * (len(args) - smem - hbm)
        + [pl.BlockSpec(memory_space=pltpu.HBM)] * hbm,
        out_specs=jax.tree.map(lambda _: VMEM, out_shape),
        scratch_shapes=list(scratch),
        compiler_params=pltpu.CompilerParams(vmem_limit_bytes=LIMIT),
        cost_estimate=pl.CostEstimate(flops=flops, bytes_accessed=size, transcendentals=0),
    )(*args)


def shape(dims, dtype=BF16):
    return jax.ShapeDtypeStruct(dims, dtype)


def stride(y, c):
    return jnp.where(c == 0, y, jnp.where(y == 0, 4, 8 - y))


def ranks(coords, experts, sign):
    y, c, z = coords[0], coords[1], coords[3]
    d = (lax.shift_right_logical(experts, 1) - z) & 7
    cc = jnp.where(d >= 4, 1, 0)
    yy = jnp.where(d < 4, d, (8 - d) & 3)
    return ((cc ^ c) * 4 + ((sign * (yy - y)) & 3)) * 2 + (experts & 1)


def spread(dest_rows, emb_t, out, start):
    tokens = dest_rows.shape[1]
    d0, d1 = dest_rows[0:1, :], dest_rows[1:2, :]
    many = 4 * CAP
    for r in range(0, 4, 2):
        slot = lax.broadcasted_iota(jnp.int32, (many, tokens), 0) + 2 * (start + r) * CAP
        hot = jnp.where((slot == d0) | (slot == d1), 1.0, 0.0).astype(BF16)
        rows = lax.dot_general(
            hot, emb_t, (((1,), (1,)), ((), ())), preferred_element_type=F32
        ).astype(BF16)
        for i in range(2):
            at = 2 * i * CAP
            out[r + i] = jnp.concatenate(
                [rows[at : at + CAP], rows[at + CAP : at + 2 * CAP]], axis=1
            )


def lookup_kernel(coords, ids, routes_far, table_far, *refs):
    send, emb_t, dest_rows, routes, table, small, large = refs
    load_routes = pltpu.make_async_copy(routes_far, routes, small)
    tokens = ids.shape[1]
    rows = table.shape[1]
    step = 512
    block = rows // 4
    loads = []
    for b in range(4):
        at = pl.ds(b * block, block)
        loads.append(
            pltpu.make_async_copy(table_far.at[:, at], table.at[:, at], large.at[b])
        )
    load_routes.start()
    for x in loads:
        x.start()
    load_routes.wait()
    experts = lax.broadcasted_iota(jnp.int32, (GROUP, tokens), 0)
    hot0 = experts == routes[0:1, :]
    hot1 = experts == routes[1:2, :]
    named = jnp.where(hot0 | hot1, 1.0, 0.0).astype(BF16)
    earlier = lax.broadcasted_iota(jnp.int32, (tokens, tokens), 0) < lax.broadcasted_iota(
        jnp.int32, (tokens, tokens), 1
    )
    count = jnp.dot(named, jnp.where(earlier, 1.0, 0.0).astype(BF16), preferred_element_type=F32)
    count = count.astype(jnp.int32)

    def picked(hot, sign):
        where = ranks(coords, experts, sign) * CAP + count
        return jnp.sum(jnp.where(hot, where, 0), axis=0, keepdims=True)

    dest_rows[...] = jnp.concatenate(
        [picked(hot0, 1), picked(hot1, 1), picked(hot0, -1), picked(hot1, -1)]
        + [jnp.zeros((4, tokens), jnp.int32)],
        axis=0,
    )
    base = ids[...] - coords[5] * rows
    acc = jnp.zeros((table.shape[0], tokens), F32)
    place = lax.broadcasted_iota(jnp.int32, (step, tokens), 0)
    for k in range(rows // step):
        if k * step % block == 0:
            loads[k * step // block].wait()
        hot = jnp.where(place == base - k * step, 1.0, 0.0).astype(BF16)
        acc += jnp.dot(table[:, k * step : (k + 1) * step], hot, preferred_element_type=F32)
    emb_t[...] = acc.astype(BF16)
    spread(dest_rows, emb_t[...], send, 4)


def rest_kernel(coords, dest_rows, emb_t, table_far, keep, own, p0, p1, p2, p3, sems):
    half = own.shape[1]
    width = p0.shape[1]
    at = pl.multiple_of(coords[4] * half, 128)
    loads = [pltpu.make_async_copy(table_far.at[:, pl.ds(at, half)], own, sems.at[4])]
    for u, piece in enumerate((p0, p1, p2, p3)):
        at = pl.multiple_of((1 - coords[4]) * half + u * width, 128)
        loads.append(
            pltpu.make_async_copy(table_far.at[:, pl.ds(at, width)], piece, sems.at[u])
        )
    for x in loads:
        x.start()
    spread(dest_rows, emb_t[...], keep, 0)
    for x in loads:
        x.wait()


def slots_kernel(coords, dest_rows, gates_far, dest_cols, slot_w, gates, sem):
    load = pltpu.make_async_copy(gates_far, gates, sem)
    load.start()
    tokens = dest_rows.shape[1]
    dest_cols[...] = dest_rows[...].astype(F32).T
    mine = coords[4] ^ coords[2]
    slot = lax.broadcasted_iota(jnp.int32, (CAP, tokens), 0) + mine * CAP
    eq0, eq1 = slot == dest_rows[0:1, :], slot == dest_rows[1:2, :]
    load.wait()
    w = jnp.where(eq0, gates[0:1, :], 0.0) + jnp.where(eq1, gates[1:2, :], 0.0)
    slot_w[:, 0:1] = jnp.sum(w, axis=1, keepdims=True)
    slot_w[:, 1:2] = jnp.sum(jnp.where(eq0, 1.0, 0.0), axis=1, keepdims=True)


def add_split_kernel(keep, got, *outs):
    for i, out in enumerate(outs):
        out[...] = (keep[i].astype(F32) + got[i].astype(F32)).astype(BF16)


def sum_split_kernel(coords, *refs):
    parts, (keep, send) = refs[:4], refs[4:]
    total = parts[0][...].astype(F32)
    for p in parts[1:]:
        total += p[...].astype(F32)
    n = keep.shape[1]
    left, right = total[:, :n], total[:, n:]
    first = (coords[4] ^ coords[2]) == 0
    keep[...] = jnp.where(first, left, right)
    send[...] = jnp.where(first, right, left).astype(BF16)


def pair_kernel(coords, own, got, out):
    first = (coords[4] ^ coords[2]) == 0
    a, b = own[...].astype(F32), got[...].astype(F32)
    out[...] = jnp.concatenate(
        [jnp.where(first, a, b).astype(BF16), jnp.where(first, b, a).astype(BF16)], axis=1
    )


def down_half(coords, hidden, w_down, out, s):
    y, c, z = coords[0], coords[1], coords[3]
    wide = out.shape[2]
    for dy in range(4):
        at = (z - stride((y + dy) & 3, c ^ s)) & 7
        w = w_down[:, pl.ds(pl.multiple_of(at * wide, 128), wide)]
        out[dy] = jnp.dot(hidden, w, preferred_element_type=F32).astype(BF16)


def expert_kernel(coords, w_gate, w_up, w_down, *refs):
    blocks, (send, hidden) = refs[:8], refs[8:]
    y, c, z = coords[0], coords[1], coords[3]
    acc = jnp.zeros((CAP, 256), F32)
    for r in range(8):
        s, dy = r // 4, r % 4
        at = (z - stride((y - dy) & 3, c ^ s)) & 7
        w = jnp.concatenate([w_gate[at], w_up[at]], axis=1)
        acc += jnp.dot(blocks[r][...], w, preferred_element_type=F32)
    gate, up = acc[:, :128], acc[:, 128:]
    hidden[...] = (gate / (1.0 + jnp.exp(-gate)) * up).astype(BF16)
    down_half(coords, hidden[...], w_down, send, 1)


def expert_rest_kernel(coords, hidden, w_down, keep):
    down_half(coords, hidden[...], w_down, keep, 0)


def picked_sum(dest_cols, at, m, held):
    d0 = dest_cols[pl.ds(at, m), 2:3].astype(jnp.int32)
    d1 = dest_cols[pl.ds(at, m), 3:4].astype(jnp.int32)
    acc = jnp.zeros((m, held.shape[1]), F32)
    step = 256
    for k in range(GROUP * CAP // step):
        place = lax.broadcasted_iota(jnp.int32, (m, step), 1) + k * step
        pick = jnp.where((place == d0) | (place == d1), 1.0, 0.0).astype(BF16)
        acc += jnp.dot(pick, held[k * step : (k + 1) * step, :], preferred_element_type=F32)
    return acc.astype(BF16)


def combine_kernel(coords, dest_cols, *refs):
    blocks, (part, held) = refs[:8], refs[8:]
    n = held.shape[1]
    for r in range(8):
        held[2 * r * CAP : (2 * r + 1) * CAP, :] = blocks[r][:, :n]
        held[(2 * r + 1) * CAP : (2 * r + 2) * CAP, :] = blocks[r][:, n:]
    m = part.shape[0]
    rows = picked_sum(dest_cols, pl.multiple_of(coords[1] * 2 * m, 16), 2 * m, held)
    part[:, :n] = rows[:m]
    part[:, n:] = rows[m:]


def combine_rest_kernel(coords, dest_cols, held, part, res):
    m, n = part.shape[0], held.shape[1]
    at = coords[1] * 2 * m
    res[pl.ds(pl.multiple_of(at, 16), m), :] = part[:, :n]
    res[pl.ds(pl.multiple_of(at + m, 16), m), :] = part[:, n:]
    at = pl.multiple_of((1 - coords[1]) * 2 * m, 16)
    res[pl.ds(at, 2 * m), :] = picked_sum(dest_cols, at, 2 * m, held)


def own_logits_kernel(dzs, coords, res, table, out, held):
    z = coords[3]
    rows = res.shape[0] // Z
    for i, dz in enumerate(dzs):
        at = pl.ds(pl.multiple_of(((z + dz) & 7) * rows, 16), rows)
        held[i * rows : (i + 1) * rows, :] = res[at, :]
    step = 512
    for k in range(table.shape[1] // step):
        at = slice(k * step, (k + 1) * step)
        out[:, at] = jnp.dot(held[...], table[:, at], preferred_element_type=F32)


def logits_kernel(dzs, coords, first, got_own, got_other, g0, g1, g2, g3, *refs):
    outs, (held, other) = refs[:-2], refs[-2:]
    c, z = coords[1], coords[3]
    m, n = got_own.shape[0], held.shape[1]
    for half, got in ((c, got_own), (1 - c, got_other)):
        other[pl.ds(pl.multiple_of(half * 2 * m, 16), m), :] = got[:, :n]
        other[pl.ds(pl.multiple_of(half * 2 * m + m, 16), m), :] = got[:, n:]
    rows = other.shape[0] // Z
    for i, dz in enumerate(dzs):
        at = pl.ds(pl.multiple_of(((z + dz) & 7) * rows, 16), rows)
        held[i * rows : (i + 1) * rows, :] = other[at, :]
    width = g0.shape[1]
    for k, got in enumerate((g0, g1, g2, g3)):
        val = first[:, k * width : (k + 1) * width]
        val += jnp.dot(held[...], got[...], preferred_element_type=F32)
        val = val.astype(BF16)
        u, at = k // 2, (k % 2) * width
        for i in range(len(dzs)):
            outs[2 * i + u][:, at : at + width] = val[i * rows : (i + 1) * rows, :]


def last_kernel(coords, own, below, above, keep, send, total):
    h = coords[4]
    n = keep.shape[0]
    total[...] = (
        own[...].astype(F32) + below[...].astype(F32) + above[...].astype(F32)
    ).astype(BF16)
    keep[...] = total[pl.ds(pl.multiple_of(h * n, 16), n), :]
    send[...] = total[pl.ds(pl.multiple_of((1 - h) * n, 16), n), :]


def swap(x, axis):
    return lax.ppermute(x, axis, [(0, 1), (1, 0)])


def shift_y(x, dy):
    return lax.ppermute(x, "y", [(y, (y + dy) % Y) for y in range(Y)])


def shift_z(x, dz):
    return lax.ppermute(x, "z", [(z, (z + dz) % Z) for z in range(Z)])


def crossed(x, forward):
    pairs = []
    for y in range(Y):
        for c in range(C):
            far = y if c == 0 else (8 - y if y else 4)
            for v in range(V):
                for z in range(Z):
                    for h in range(H):
                        at = ((y * C + c) * V + v) * Z
                        a = (at + z) * H + h
                        b = (at + (z + far) % Z) * H + (h ^ v)
                        pairs.append((a, b) if forward else (b, a))
    return lax.ppermute(x, ALL, pairs)


def scatter_sum(coords, keep, send, piece):
    got = swap(send, "c")
    one = shape(keep.shape[1:])
    parts = list(call(add_split_kernel, [one] * 4, keep, got, smem=0, size=3 * keep.size * 2))
    parts[3], piece = lax.optimization_barrier((parts[3], piece))
    arrived = [shift_y(parts[dy], dy) for dy in (2, 1, 3)]
    piece = swap(piece, "h")
    arrived[0], piece = lax.optimization_barrier((arrived[0], piece))
    half = (one.shape[0], one.shape[1] // 2)
    own, away = call(
        sum_split_kernel,
        [shape(half, F32), shape(half)],
        coords,
        parts[0],
        *arrived,
        size=6 * parts[0].size * 2,
    )
    return (own + swap(away, "v").astype(F32)).astype(BF16), piece


def gather_all(coords, own, piece):
    got = swap(own, "v")
    pair = call(
        pair_kernel, shape((own.shape[0], 2 * own.shape[1])), coords, own, got, size=8 * own.size
    )
    pair, piece = lax.optimization_barrier((pair, piece))
    near = [pair, None, None, None]
    for dy in (2, 1, 3):
        near[dy] = shift_y(pair, dy)
    piece = swap(piece, "h")
    near[0], near[3] = lax.optimization_barrier((pair, near[3]))
    far = [swap(x, "c") for x in near]
    far[1], piece = lax.optimization_barrier((far[1], piece))
    return near + far, piece


def added(a, b):
    return (a.astype(F32) + b.astype(F32)).astype(BF16)


def per_device(token_ids, routes, gate_weights, embed_table, w_gate, w_up, w_down):
    vocab_rows, width = embed_table.shape
    tokens = token_ids.shape[0]
    coords = jnp.stack(
        [lax.axis_index(a) for a in ALL] + [lax.axis_index(PV), jnp.int32(0), jnp.int32(0)]
    ).astype(jnp.int32)
    table = embed_table.T
    h = lax.axis_index("h")
    eighth = vocab_rows // 8
    quarter = 2 * eighth
    half = 2 * quarter
    slots = (4, CAP, 2 * width)
    def far(x):
        return pltpu.with_memory_space_constraint(x, pltpu.HBM)

    table = far(table)
    send, emb_t, dest_rows = call(
        lookup_kernel,
        [shape(slots), shape((width, tokens)), shape((8, tokens), jnp.int32)],
        coords,
        token_ids.reshape(1, tokens),
        far(routes.T),
        table,
        hbm=2,
        scratch=[
            pltpu.VMEM((2, tokens), jnp.int32),
            pltpu.VMEM((width, vocab_rows), BF16),
            pltpu.SemaphoreType.DMA,
            pltpu.SemaphoreType.DMA((4,)),
        ],
        flops=2 * tokens * width * (vocab_rows + GROUP * CAP),
        size=6 * 1024 * 1024,
    )
    keep, own, *pieces = call(
        rest_kernel,
        [shape(slots), shape((width, half))] + [shape((width, eighth))] * 4,
        coords,
        dest_rows,
        emb_t,
        table,
        hbm=1,
        scratch=[pltpu.SemaphoreType.DMA((5,))],
        flops=2 * tokens * width * GROUP * CAP // 2,
        size=6 * 1024 * 1024,
    )
    dest_cols, slot_w = call(
        slots_kernel,
        [shape((tokens, 8), F32), shape((CAP, 2), F32)],
        coords,
        dest_rows,
        far(gate_weights.T),
        hbm=1,
        scratch=[pltpu.VMEM((2, tokens), F32), pltpu.SemaphoreType.DMA],
        flops=tokens * CAP,
        size=512 * 1024,
    )
    gots = [None] * 4
    rows_in, gots[0] = scatter_sum(coords, keep, send, pieces[0])
    blocks, gots[1] = gather_all(coords, crossed(rows_in, True), pieces[1])
    send, hidden = call(
        expert_kernel,
        [shape(slots), shape((CAP, 128))],
        coords,
        w_gate.reshape(8, 2 * width, 128),
        w_up.reshape(8, 2 * width, 128),
        w_down[0],
        *blocks,
        flops=5 * CAP * GROUP * width * 128,
        size=9 * 1024 * 1024,
    )
    keep = call(
        expert_rest_kernel,
        shape(slots),
        coords,
        hidden,
        w_down[0],
        flops=CAP * GROUP * width * 128,
        size=3 * 1024 * 1024,
    )
    sums, gots[2] = scatter_sum(coords, keep, send, pieces[2])
    back = crossed(sums, False)
    back = (
        slot_w[:, 0:1] * back.astype(F32) + slot_w[:, 1:2] * rows_in.astype(F32)
    ).astype(BF16)
    blocks, gots[3] = gather_all(coords, back, pieces[3])
    part, held = call(
        combine_kernel,
        [shape((tokens // 4, 2 * width)), shape((GROUP * CAP, width))],
        coords,
        dest_cols,
        *blocks,
        flops=tokens * GROUP * CAP * width,
        size=5 * 1024 * 1024,
    )
    res = call(
        combine_rest_kernel,
        shape((tokens, width)),
        coords,
        dest_cols,
        held,
        part,
        flops=tokens * GROUP * CAP * width,
        size=3 * 1024 * 1024,
    )
    got_own = swap(part, "h")
    rows = tokens // Z
    outs = {}
    orders = ((4, 5, 3), (6, 2, 7, 1, 0))
    firsts = []
    for dzs in orders:
        m = len(dzs) * rows
        firsts.append(
            call(
                functools.partial(own_logits_kernel, dzs),
                shape((m, half), F32),
                coords,
                res,
                own,
                scratch=[pltpu.VMEM((m, width), BF16)],
                flops=2 * m * width * half,
                size=6 * 1024 * 1024,
            )
        )
    got_own, *firsts = lax.optimization_barrier((got_own, *firsts))
    got_other = swap(got_own, "c")
    for k, dzs in enumerate(orders):
        m = len(dzs) * rows
        vals = call(
            functools.partial(logits_kernel, dzs),
            [shape((rows, quarter))] * (2 * len(dzs)),
            coords,
            firsts[k],
            got_own,
            got_other,
            *gots,
            scratch=[pltpu.VMEM((m, width), BF16), pltpu.VMEM((tokens, width), BF16)],
            flops=2 * m * width * half,
            size=6 * 1024 * 1024,
        )
        for i, dz in enumerate(dzs):
            outs[dz] = vals[2 * i : 2 * i + 2]
    down = [shift_z(outs[4][0], -1), None]
    up = [None, shift_z(outs[4][1], 1)]
    down[1] = shift_z(outs[5][1], -1)
    up[0] = shift_z(outs[3][0], 1)
    down[0] = shift_z(added(down[0], outs[5][0]), -1)
    up[1] = shift_z(added(up[1], outs[3][1]), 1)
    for k in (2, 1):
        for u in (1, 0):
            down[u] = shift_z(added(down[u], outs[Z - k][u]), -1)
            up[1 - u] = shift_z(added(up[1 - u], outs[k][1 - u]), 1)
    down[0], up[1] = lax.optimization_barrier((down[0], up[1]))
    mine, got = [], []
    for u in range(2):
        keep, send = call(
            last_kernel,
            [shape((rows // 2, quarter))] * 2,
            coords,
            outs[0][u],
            down[u],
            up[u],
            scratch=[pltpu.VMEM((rows, quarter), BF16)],
            size=8 * rows * quarter,
        )
        mine.append(keep)
        got.append(swap(send, "h"))
    return jnp.where(
        h == 0, jnp.concatenate(mine + got, axis=1), jnp.concatenate(got + mine, axis=1)
    )


def solution(mesh):
    finer = Mesh(mesh.devices.reshape(Y, C, V, Z, H), ALL)
    return jax.shard_map(
        per_device,
        mesh=finer,
        in_specs=(
            P(),
            P(),
            P(),
            P(PV, EXPERT),
            P(EXPERT, None, PV),
            P(EXPERT, None, PV),
            P(EXPERT, PV, None),
        ),
        out_specs=P(EXPERT, PV),
        check_vma=False,
    )
```

```python
import functools

import jax
import jax.numpy as jnp
from jax import lax
from jax.experimental import pallas as pl
from jax.experimental.pallas import tpu as pltpu
from jax.sharding import Mesh
from jax.sharding import PartitionSpec as P

Y, C, V, Z, H = 4, 2, 2, 8, 2
ALL = ("y", "c", "v", "z", "h")
PV = ("y", "c", "v")
EXPERT = ("z", "h")
GROUP = 16
CAP = 144
BF16 = jnp.bfloat16
F32 = jnp.float32
LIMIT = 28 * 1024 * 1024

VMEM = pl.BlockSpec(memory_space=pltpu.VMEM)
SMEM = pl.BlockSpec(memory_space=pltpu.SMEM)


def call(kernel, out_shape, *args, smem=1, hbm=0, scratch=(), flops=0, size=0):
    return pl.pallas_call(
        kernel,
        out_shape=out_shape,
        in_specs=[SMEM] * smem
        + [VMEM] * (len(args) - smem - hbm)
        + [pl.BlockSpec(memory_space=pltpu.HBM)] * hbm,
        out_specs=jax.tree.map(lambda _: VMEM, out_shape),
        scratch_shapes=list(scratch),
        compiler_params=pltpu.CompilerParams(vmem_limit_bytes=LIMIT),
        cost_estimate=pl.CostEstimate(flops=flops, bytes_accessed=size, transcendentals=0),
    )(*args)


def shape(dims, dtype=BF16):
    return jax.ShapeDtypeStruct(dims, dtype)


def stride(y, c):
    return jnp.where(c == 0, y, jnp.where(y == 0, 4, 8 - y))


def ranks(coords, experts, sign):
    y, c, z = coords[0], coords[1], coords[3]
    d = (lax.shift_right_logical(experts, 1) - z) & 7
    cc = jnp.where(d >= 4, 1, 0)
    yy = jnp.where(d < 4, d, (8 - d) & 3)
    return ((cc ^ c) * 4 + ((sign * (yy - y)) & 3)) * 2 + (experts & 1)


def spread(dest_rows, emb_t, out, start):
    tokens = dest_rows.shape[1]
    d0, d1 = dest_rows[0:1, :], dest_rows[1:2, :]
    many = 4 * CAP
    for r in range(0, 4, 2):
        slot = lax.broadcasted_iota(jnp.int32, (many, tokens), 0) + 2 * (start + r) * CAP
        hot = jnp.where((slot == d0) | (slot == d1), 1.0, 0.0).astype(BF16)
        rows = lax.dot_general(
            hot, emb_t, (((1,), (1,)), ((), ())), preferred_element_type=F32
        ).astype(BF16)
        for i in range(2):
            at = 2 * i * CAP
            out[r + i] = jnp.concatenate(
                [rows[at : at + CAP], rows[at + CAP : at + 2 * CAP]], axis=1
            )


def lookup_kernel(coords, ids, routes_far, table_far, *refs):
    send, emb_t, dest_rows, routes, table, small, large = refs
    load_routes = pltpu.make_async_copy(routes_far, routes, small)
    tokens = ids.shape[1]
    rows = table.shape[1]
    step = 512
    block = rows // 4
    loads = []
    for b in range(4):
        at = pl.ds(b * block, block)
        loads.append(
            pltpu.make_async_copy(table_far.at[:, at], table.at[:, at], large.at[b])
        )
    load_routes.start()
    for x in loads:
        x.start()
    load_routes.wait()
    experts = lax.broadcasted_iota(jnp.int32, (GROUP, tokens), 0)
    hot0 = experts == routes[0:1, :]
    hot1 = experts == routes[1:2, :]
    named = jnp.where(hot0 | hot1, 1.0, 0.0).astype(BF16)
    earlier = lax.broadcasted_iota(jnp.int32, (tokens, tokens), 0) < lax.broadcasted_iota(
        jnp.int32, (tokens, tokens), 1
    )
    count = jnp.dot(named, jnp.where(earlier, 1.0, 0.0).astype(BF16), preferred_element_type=F32)
    count = count.astype(jnp.int32)

    def picked(hot, sign):
        where = ranks(coords, experts, sign) * CAP + count
        return jnp.sum(jnp.where(hot, where, 0), axis=0, keepdims=True)

    dest_rows[...] = jnp.concatenate(
        [picked(hot0, 1), picked(hot1, 1), picked(hot0, -1), picked(hot1, -1)]
        + [jnp.zeros((4, tokens), jnp.int32)],
        axis=0,
    )
    base = ids[...] - coords[5] * rows
    acc = jnp.zeros((table.shape[0], tokens), F32)
    place = lax.broadcasted_iota(jnp.int32, (step, tokens), 0)
    for k in range(rows // step):
        if k * step % block == 0:
            loads[k * step // block].wait()
        hot = jnp.where(place == base - k * step, 1.0, 0.0).astype(BF16)
        acc += jnp.dot(table[:, k * step : (k + 1) * step], hot, preferred_element_type=F32)
    emb_t[...] = acc.astype(BF16)
    spread(dest_rows, emb_t[...], send, 4)


def rest_kernel(coords, dest_rows, emb_t, table_far, keep, own, p0, p1, p2, p3, sems):
    half = own.shape[1]
    width = p0.shape[1]
    at = pl.multiple_of(coords[4] * half, 128)
    loads = [pltpu.make_async_copy(table_far.at[:, pl.ds(at, half)], own, sems.at[4])]
    for u, piece in enumerate((p0, p1, p2, p3)):
        at = pl.multiple_of((1 - coords[4]) * half + u * width, 128)
        loads.append(
            pltpu.make_async_copy(table_far.at[:, pl.ds(at, width)], piece, sems.at[u])
        )
    for x in loads:
        x.start()
    spread(dest_rows, emb_t[...], keep, 0)
    for x in loads:
        x.wait()


def slots_kernel(coords, dest_rows, gates_far, dest_cols, slot_w, gates, sem):
    load = pltpu.make_async_copy(gates_far, gates, sem)
    load.start()
    tokens = dest_rows.shape[1]
    dest_cols[...] = dest_rows[...].astype(F32).T
    mine = coords[4] ^ coords[2]
    slot = lax.broadcasted_iota(jnp.int32, (CAP, tokens), 0) + mine * CAP
    eq0, eq1 = slot == dest_rows[0:1, :], slot == dest_rows[1:2, :]
    load.wait()
    w = jnp.where(eq0, gates[0:1, :], 0.0) + jnp.where(eq1, gates[1:2, :], 0.0)
    slot_w[:, 0:1] = jnp.sum(w, axis=1, keepdims=True)
    slot_w[:, 1:2] = jnp.sum(jnp.where(eq0, 1.0, 0.0), axis=1, keepdims=True)


def add_split_kernel(keep, got, *outs):
    for i, out in enumerate(outs):
        out[...] = (keep[i].astype(F32) + got[i].astype(F32)).astype(BF16)


def sum_split_kernel(flip, coords, *refs):
    parts, (keep, send) = refs[:4], refs[4:]
    total = parts[0][...].astype(F32)
    for p in parts[1:]:
        total += p[...].astype(F32)
    n = keep.shape[1]
    left, right = total[:, :n], total[:, n:]
    first = (coords[4] ^ coords[2]) == flip
    keep[...] = jnp.where(first, left, right)
    send[...] = jnp.where(first, right, left).astype(BF16)


def pair_kernel(flip, coords, own, got, out):
    first = (coords[4] ^ coords[2]) == flip
    a, b = own[...].astype(F32), got[...].astype(F32)
    out[...] = jnp.concatenate(
        [jnp.where(first, a, b).astype(BF16), jnp.where(first, b, a).astype(BF16)], axis=1
    )


def down_half(coords, hidden, w_down, out, s):
    y, c, z = coords[0], coords[1], coords[3]
    wide = out.shape[2]
    for dy in range(4):
        at = (z - stride((y + dy) & 3, c ^ s)) & 7
        w = w_down[:, pl.ds(pl.multiple_of(at * wide, 128), wide)]
        out[dy] = jnp.dot(hidden, w, preferred_element_type=F32).astype(BF16)


def expert_kernel(coords, w_gate, w_up, w_down, *refs):
    blocks, (send, hidden) = refs[:8], refs[8:]
    y, c, z = coords[0], coords[1], coords[3]
    acc = jnp.zeros((CAP, 256), F32)
    for r in range(8):
        s, dy = r // 4, r % 4
        at = (z - stride((y - dy) & 3, c ^ s)) & 7
        w = jnp.concatenate([w_gate[at], w_up[at]], axis=1)
        acc += jnp.dot(blocks[r][...], w, preferred_element_type=F32)
    gate, up = acc[:, :128], acc[:, 128:]
    hidden[...] = (gate / (1.0 + jnp.exp(-gate)) * up).astype(BF16)
    down_half(coords, hidden[...], w_down, send, 1)


def expert_rest_kernel(coords, hidden, w_down, keep):
    down_half(coords, hidden[...], w_down, keep, 0)


def picked_sum(dest_cols, at, m, held):
    d0 = dest_cols[pl.ds(at, m), 2:3].astype(jnp.int32)
    d1 = dest_cols[pl.ds(at, m), 3:4].astype(jnp.int32)
    acc = jnp.zeros((m, held.shape[1]), F32)
    step = 256
    for k in range(GROUP * CAP // step):
        place = lax.broadcasted_iota(jnp.int32, (m, step), 1) + k * step
        pick = jnp.where((place == d0) | (place == d1), 1.0, 0.0).astype(BF16)
        acc += jnp.dot(pick, held[k * step : (k + 1) * step, :], preferred_element_type=F32)
    return acc.astype(BF16)


def combine_kernel(coords, dest_cols, *refs):
    blocks, (part, held) = refs[:8], refs[8:]
    n = held.shape[1]
    for r in range(8):
        held[2 * r * CAP : (2 * r + 1) * CAP, :] = blocks[r][:, :n]
        held[(2 * r + 1) * CAP : (2 * r + 2) * CAP, :] = blocks[r][:, n:]
    m = part.shape[0]
    rows = picked_sum(dest_cols, pl.multiple_of(coords[1] * 2 * m, 16), 2 * m, held)
    part[:, :n] = rows[:m]
    part[:, n:] = rows[m:]


def combine_rest_kernel(coords, dest_cols, held, part, res):
    m, n = part.shape[0], held.shape[1]
    at = coords[1] * 2 * m
    res[pl.ds(pl.multiple_of(at, 16), m), :] = part[:, :n]
    res[pl.ds(pl.multiple_of(at + m, 16), m), :] = part[:, n:]
    at = pl.multiple_of((1 - coords[1]) * 2 * m, 16)
    res[pl.ds(at, 2 * m), :] = picked_sum(dest_cols, at, 2 * m, held)


def own_logits_kernel(dzs, coords, res, table, out, held):
    z = coords[3]
    rows = res.shape[0] // Z
    for i, dz in enumerate(dzs):
        at = pl.ds(pl.multiple_of(((z + dz) & 7) * rows, 16), rows)
        held[i * rows : (i + 1) * rows, :] = res[at, :]
    step = 512
    for k in range(table.shape[1] // step):
        at = slice(k * step, (k + 1) * step)
        out[:, at] = jnp.dot(held[...], table[:, at], preferred_element_type=F32)


def logits_kernel(dzs, coords, first, got_own, got_other, g0, g1, g2, g3, *refs):
    outs, (held, other) = refs[:-2], refs[-2:]
    c, z = coords[1], coords[3]
    m, n = got_own.shape[0], held.shape[1]
    for half, got in ((c, got_own), (1 - c, got_other)):
        other[pl.ds(pl.multiple_of(half * 2 * m, 16), m), :] = got[:, :n]
        other[pl.ds(pl.multiple_of(half * 2 * m + m, 16), m), :] = got[:, n:]
    rows = other.shape[0] // Z
    for i, dz in enumerate(dzs):
        at = pl.ds(pl.multiple_of(((z + dz) & 7) * rows, 16), rows)
        held[i * rows : (i + 1) * rows, :] = other[at, :]
    width = g0.shape[1]
    for k, got in enumerate((g0, g1, g2, g3)):
        val = first[:, k * width : (k + 1) * width]
        val += jnp.dot(held[...], got[...], preferred_element_type=F32)
        val = val.astype(BF16)
        u, at = k // 2, (k % 2) * width
        for i in range(len(dzs)):
            outs[2 * i + u][:, at : at + width] = val[i * rows : (i + 1) * rows, :]


def last_kernel(coords, own0, own1, below0, below1, above0, above1, keep, send, total):
    h = coords[4]
    n, width = keep.shape[0], own0.shape[1]
    for u, (a, b, d) in enumerate(((own0, below0, above0), (own1, below1, above1))):
        total[:, u * width : (u + 1) * width] = (
            a[...].astype(F32) + b[...].astype(F32) + d[...].astype(F32)
        ).astype(BF16)
    keep[...] = total[pl.ds(pl.multiple_of(h * n, 16), n), :]
    send[...] = total[pl.ds(pl.multiple_of((1 - h) * n, 16), n), :]


def swap(x, axis):
    return lax.ppermute(x, axis, [(0, 1), (1, 0)])


def shift_y(x, dy):
    return lax.ppermute(x, "y", [(y, (y + dy) % Y) for y in range(Y)])


def shift_z(x, dz):
    return lax.ppermute(x, "z", [(z, (z + dz) % Z) for z in range(Z)])


def crossed(x, forward):
    pairs = []
    for y in range(Y):
        for c in range(C):
            far = y if c == 0 else (8 - y if y else 4)
            for v in range(V):
                for z in range(Z):
                    for h in range(H):
                        at = (y * C + c) * V
                        a = ((at + v) * Z + z) * H + h
                        b = ((at + 1 - v) * Z + (z + far) % Z) * H + (h ^ v)
                        pairs.append((a, b) if forward else (b, a))
    return lax.ppermute(x, ALL, pairs)


def scatter_sum(coords, keep, send, piece, flip):
    got = swap(send, "c")
    one = shape(keep.shape[1:])
    parts = list(call(add_split_kernel, [one] * 4, keep, got, smem=0, size=3 * keep.size * 2))
    parts[3], piece = lax.optimization_barrier((parts[3], piece))
    arrived = [shift_y(parts[dy], dy) for dy in (2, 1, 3)]
    piece = swap(piece, "h")
    arrived[0], piece = lax.optimization_barrier((arrived[0], piece))
    half = (one.shape[0], one.shape[1] // 2)
    own, away = call(
        functools.partial(sum_split_kernel, flip),
        [shape(half, F32), shape(half)],
        coords,
        parts[0],
        *arrived,
        size=6 * parts[0].size * 2,
    )
    return (own + swap(away, "v").astype(F32)).astype(BF16), piece


def gather_all(coords, own, piece, flip):
    got = swap(own, "v")
    pair = call(
        functools.partial(pair_kernel, flip),
        shape((own.shape[0], 2 * own.shape[1])),
        coords,
        own,
        got,
        size=8 * own.size,
    )
    pair, piece = lax.optimization_barrier((pair, piece))
    near = [pair, None, None, None]
    for dy in (2, 1, 3):
        near[dy] = shift_y(pair, dy)
    piece = swap(piece, "h")
    near[0], near[3] = lax.optimization_barrier((pair, near[3]))
    far = [swap(x, "c") for x in near]
    far[1], piece = lax.optimization_barrier((far[1], piece))
    return near + far, piece


def added(a, b):
    return (a.astype(F32) + b.astype(F32)).astype(BF16)


def per_device(token_ids, routes, gate_weights, embed_table, w_gate, w_up, w_down):
    vocab_rows, width = embed_table.shape
    tokens = token_ids.shape[0]
    coords = jnp.stack(
        [lax.axis_index(a) for a in ALL] + [lax.axis_index(PV), jnp.int32(0), jnp.int32(0)]
    ).astype(jnp.int32)
    table = embed_table.T
    h = lax.axis_index("h")
    eighth = vocab_rows // 8
    quarter = 2 * eighth
    half = 2 * quarter
    slots = (4, CAP, 2 * width)
    def far(x):
        return pltpu.with_memory_space_constraint(x, pltpu.HBM)

    table = far(table)
    send, emb_t, dest_rows = call(
        lookup_kernel,
        [shape(slots), shape((width, tokens)), shape((8, tokens), jnp.int32)],
        coords,
        token_ids.reshape(1, tokens),
        far(routes.T),
        table,
        hbm=2,
        scratch=[
            pltpu.VMEM((2, tokens), jnp.int32),
            pltpu.VMEM((width, vocab_rows), BF16),
            pltpu.SemaphoreType.DMA,
            pltpu.SemaphoreType.DMA((4,)),
        ],
        flops=2 * tokens * width * (vocab_rows + GROUP * CAP),
        size=6 * 1024 * 1024,
    )
    keep, own, *pieces = call(
        rest_kernel,
        [shape(slots), shape((width, half))] + [shape((width, eighth))] * 4,
        coords,
        dest_rows,
        emb_t,
        table,
        hbm=1,
        scratch=[pltpu.SemaphoreType.DMA((5,))],
        flops=2 * tokens * width * GROUP * CAP // 2,
        size=6 * 1024 * 1024,
    )
    dest_cols, slot_w = call(
        slots_kernel,
        [shape((tokens, 8), F32), shape((CAP, 2), F32)],
        coords,
        dest_rows,
        far(gate_weights.T),
        hbm=1,
        scratch=[pltpu.VMEM((2, tokens), F32), pltpu.SemaphoreType.DMA],
        flops=tokens * CAP,
        size=512 * 1024,
    )
    gots = [None] * 4
    rows_in, gots[0] = scatter_sum(coords, keep, send, pieces[0], 0)
    blocks, gots[1] = gather_all(coords, crossed(rows_in, True), pieces[1], 1)
    send, hidden = call(
        expert_kernel,
        [shape(slots), shape((CAP, 128))],
        coords,
        w_gate.reshape(8, 2 * width, 128),
        w_up.reshape(8, 2 * width, 128),
        w_down[0],
        *blocks,
        flops=5 * CAP * GROUP * width * 128,
        size=9 * 1024 * 1024,
    )
    keep = call(
        expert_rest_kernel,
        shape(slots),
        coords,
        hidden,
        w_down[0],
        flops=CAP * GROUP * width * 128,
        size=3 * 1024 * 1024,
    )
    sums, gots[2] = scatter_sum(coords, keep, send, pieces[2], 1)
    back = crossed(sums, False)
    back = (
        slot_w[:, 0:1] * back.astype(F32) + slot_w[:, 1:2] * rows_in.astype(F32)
    ).astype(BF16)
    blocks, gots[3] = gather_all(coords, back, pieces[3], 0)
    part, held = call(
        combine_kernel,
        [shape((tokens // 4, 2 * width)), shape((GROUP * CAP, width))],
        coords,
        dest_cols,
        *blocks,
        flops=tokens * GROUP * CAP * width,
        size=5 * 1024 * 1024,
    )
    res = call(
        combine_rest_kernel,
        shape((tokens, width)),
        coords,
        dest_cols,
        held,
        part,
        flops=tokens * GROUP * CAP * width,
        size=3 * 1024 * 1024,
    )
    near = [(v * H + h, (1 - v) * H + 1 - h) for v in range(V) for h in range(H)]
    got_own = lax.ppermute(part, ("v", "h"), near)
    rows = tokens // Z
    outs = {}
    orders = ((4, 5, 3), (6, 2, 7, 1, 0))
    firsts = []
    for dzs in orders:
        m = len(dzs) * rows
        firsts.append(
            call(
                functools.partial(own_logits_kernel, dzs),
                shape((m, half), F32),
                coords,
                res,
                own,
                scratch=[pltpu.VMEM((m, width), BF16)],
                flops=2 * m * width * half,
                size=6 * 1024 * 1024,
            )
        )
    got_own, *firsts = lax.optimization_barrier((got_own, *firsts))
    got_other = swap(got_own, "c")
    for k, dzs in enumerate(orders):
        m = len(dzs) * rows
        vals = call(
            functools.partial(logits_kernel, dzs),
            [shape((rows, quarter))] * (2 * len(dzs)),
            coords,
            firsts[k],
            got_own,
            got_other,
            *gots,
            scratch=[pltpu.VMEM((m, width), BF16), pltpu.VMEM((tokens, width), BF16)],
            flops=2 * m * width * half,
            size=6 * 1024 * 1024,
        )
        for i, dz in enumerate(dzs):
            outs[dz] = vals[2 * i : 2 * i + 2]
    down = [shift_z(outs[4][0], -1), None]
    up = [None, shift_z(outs[4][1], 1)]
    down[1] = shift_z(outs[5][1], -1)
    up[0] = shift_z(outs[3][0], 1)
    down[0] = shift_z(added(down[0], outs[5][0]), -1)
    up[1] = shift_z(added(up[1], outs[3][1]), 1)
    for k in (2, 1):
        for u in (1, 0):
            down[u] = shift_z(added(down[u], outs[Z - k][u]), -1)
            up[1 - u] = shift_z(added(up[1 - u], outs[k][1 - u]), 1)
    down[0], up[1] = lax.optimization_barrier((down[0], up[1]))
    mine, theirs = call(
        last_kernel,
        [shape((rows // 2, half))] * 2,
        coords,
        *outs[0],
        *down,
        *up,
        scratch=[pltpu.VMEM((rows, half), BF16)],
        size=8 * rows * half,
    )
    got = swap(theirs, "h")
    return jnp.where(
        lax.axis_index("h") == 0,
        jnp.concatenate([mine, got], axis=1),
        jnp.concatenate([got, mine], axis=1),
    )


def solution(mesh):
    finer = Mesh(mesh.devices.reshape(Y, C, V, Z, H), ALL)
    return jax.shard_map(
        per_device,
        mesh=finer,
        in_specs=(
            P(),
            P(),
            P(),
            P(PV, EXPERT),
            P(EXPERT, None, PV),
            P(EXPERT, None, PV),
            P(EXPERT, PV, None),
        ),
        out_specs=P(EXPERT, PV),
        check_vma=False,
    )
```

```python
import functools

import jax
import jax.numpy as jnp
from jax import lax
from jax.experimental import pallas as pl
from jax.experimental.pallas import tpu as pltpu
from jax.sharding import Mesh
from jax.sharding import PartitionSpec as P

Y, C, V, Z, H = 4, 2, 2, 8, 2
ALL = ("y", "c", "v", "z", "h")
PV = ("y", "c", "v")
EXPERT = ("z", "h")
GROUP = 16
CAP = 144
BF16 = jnp.bfloat16
F32 = jnp.float32
LIMIT = 28 * 1024 * 1024

VMEM = pl.BlockSpec(memory_space=pltpu.VMEM)
SMEM = pl.BlockSpec(memory_space=pltpu.SMEM)


def call(kernel, out_shape, *args, smem=1, hbm=0, scratch=(), flops=0, size=0):
    return pl.pallas_call(
        kernel,
        out_shape=out_shape,
        in_specs=[SMEM] * smem
        + [VMEM] * (len(args) - smem - hbm)
        + [pl.BlockSpec(memory_space=pltpu.HBM)] * hbm,
        out_specs=jax.tree.map(lambda _: VMEM, out_shape),
        scratch_shapes=list(scratch),
        compiler_params=pltpu.CompilerParams(vmem_limit_bytes=LIMIT),
        cost_estimate=pl.CostEstimate(flops=flops, bytes_accessed=size, transcendentals=0),
    )(*args)


def shape(dims, dtype=BF16):
    return jax.ShapeDtypeStruct(dims, dtype)


def stride(y, c):
    return jnp.where(c == 0, y, jnp.where(y == 0, 4, 8 - y))


def ranks(coords, experts, sign):
    y, c, z = coords[0], coords[1], coords[3]
    d = (lax.shift_right_logical(experts, 1) - z) & 7
    cc = jnp.where(d >= 4, 1, 0)
    yy = jnp.where(d < 4, d, (8 - d) & 3)
    return ((cc ^ c) * 4 + ((sign * (yy - y)) & 3)) * 2 + (experts & 1)


def spread(dest_rows, emb_t, out, start):
    tokens = dest_rows.shape[1]
    d0, d1 = dest_rows[0:1, :], dest_rows[1:2, :]
    many = 4 * CAP
    for r in range(0, 4, 2):
        slot = lax.broadcasted_iota(jnp.int32, (many, tokens), 0) + 2 * (start + r) * CAP
        hot = jnp.where((slot == d0) | (slot == d1), 1.0, 0.0).astype(BF16)
        rows = lax.dot_general(
            hot, emb_t, (((1,), (1,)), ((), ())), preferred_element_type=F32
        ).astype(BF16)
        for i in range(2):
            at = 2 * i * CAP
            out[r + i] = jnp.concatenate(
                [rows[at : at + CAP], rows[at + CAP : at + 2 * CAP]], axis=1
            )


def lookup_kernel(coords, ids_far, routes_far, table_far, *refs):
    send, emb_t, dest_rows, ids, routes, table, small, large = refs
    load_ids = pltpu.make_async_copy(ids_far, ids, small.at[0])
    load_routes = pltpu.make_async_copy(routes_far, routes, small.at[1])
    tokens = ids.shape[0]
    rows = table.shape[1]
    step = 512
    block = rows // 4
    loads = []
    for b in range(4):
        at = pl.ds(b * block, block)
        loads.append(
            pltpu.make_async_copy(table_far.at[:, at], table.at[:, at], large.at[b])
        )
    load_routes.start()
    load_ids.start()
    for x in loads:
        x.start()
    load_routes.wait()
    experts = lax.broadcasted_iota(jnp.int32, (GROUP, tokens), 0)
    hot0 = experts == routes[0:1, :]
    hot1 = experts == routes[1:2, :]
    named = jnp.where(hot0 | hot1, 1.0, 0.0).astype(BF16)
    earlier = lax.broadcasted_iota(jnp.int32, (tokens, tokens), 0) < lax.broadcasted_iota(
        jnp.int32, (tokens, tokens), 1
    )
    count = jnp.dot(named, jnp.where(earlier, 1.0, 0.0).astype(BF16), preferred_element_type=F32)
    count = count.astype(jnp.int32)

    def picked(hot, sign):
        where = ranks(coords, experts, sign) * CAP + count
        return jnp.sum(jnp.where(hot, where, 0), axis=0, keepdims=True)

    dest_rows[...] = jnp.concatenate(
        [picked(hot0, 1), picked(hot1, 1), picked(hot0, -1), picked(hot1, -1)]
        + [jnp.zeros((4, tokens), jnp.int32)],
        axis=0,
    )
    load_ids.wait()
    base = ids[...].reshape(1, tokens) - coords[5] * rows
    acc = jnp.zeros((table.shape[0], tokens), F32)
    place = lax.broadcasted_iota(jnp.int32, (step, tokens), 0)
    for k in range(rows // step):
        if k * step % block == 0:
            loads[k * step // block].wait()
        hot = jnp.where(place == base - k * step, 1.0, 0.0).astype(BF16)
        acc += jnp.dot(table[:, k * step : (k + 1) * step], hot, preferred_element_type=F32)
    emb_t[...] = acc.astype(BF16)
    spread(dest_rows, emb_t[...], send, 4)


def rest_kernel(coords, dest_rows, emb_t, table_far, keep, p0, p1, p2, p3, sems):
    width = p0.shape[1]
    half = 4 * width
    loads = []
    for u, piece in enumerate((p0, p1, p2, p3)):
        at = pl.multiple_of((1 - coords[4]) * half + u * width, 128)
        loads.append(
            pltpu.make_async_copy(table_far.at[:, pl.ds(at, width)], piece, sems.at[u])
        )
    for x in loads:
        x.start()
    spread(dest_rows, emb_t[...], keep, 0)
    for x in loads:
        x.wait()


def slots_kernel(
    coords, dest_rows, gates_far, table_far, dest_cols, slot_w, own, gates, sems
):
    half = own.shape[1]
    at = pl.multiple_of(coords[4] * half, 128)
    load = pltpu.make_async_copy(gates_far, gates, sems.at[0])
    load_own = pltpu.make_async_copy(table_far.at[:, pl.ds(at, half)], own, sems.at[1])
    load.start()
    load_own.start()
    tokens = dest_rows.shape[1]
    dest_cols[...] = dest_rows[...].astype(F32).T
    mine = coords[4] ^ coords[2]
    slot = lax.broadcasted_iota(jnp.int32, (CAP, tokens), 0) + mine * CAP
    eq0, eq1 = slot == dest_rows[0:1, :], slot == dest_rows[1:2, :]
    load.wait()
    w = jnp.where(eq0, gates[0:1, :], 0.0) + jnp.where(eq1, gates[1:2, :], 0.0)
    slot_w[:, 0:1] = jnp.sum(w, axis=1, keepdims=True)
    slot_w[:, 1:2] = jnp.sum(jnp.where(eq0, 1.0, 0.0), axis=1, keepdims=True)
    load_own.wait()


def add_split_kernel(keep, got, *outs):
    for i, out in enumerate(outs):
        out[...] = (keep[i].astype(F32) + got[i].astype(F32)).astype(BF16)


def sum_split_kernel(flip, coords, *refs):
    parts, (keep, send) = refs[:4], refs[4:]
    total = parts[0][...].astype(F32)
    for p in parts[1:]:
        total += p[...].astype(F32)
    n = keep.shape[1]
    left, right = total[:, :n], total[:, n:]
    first = (coords[4] ^ coords[2]) == flip
    keep[...] = jnp.where(first, left, right)
    send[...] = jnp.where(first, right, left).astype(BF16)


def pair_kernel(flip, coords, own, got, out):
    first = (coords[4] ^ coords[2]) == flip
    a, b = own[...].astype(F32), got[...].astype(F32)
    out[...] = jnp.concatenate(
        [jnp.where(first, a, b).astype(BF16), jnp.where(first, b, a).astype(BF16)], axis=1
    )


def down_half(coords, hidden, w_down, out, s):
    y, c, z = coords[0], coords[1], coords[3]
    wide = out.shape[2]
    for dy in range(4):
        at = (z - stride((y + dy) & 3, c ^ s)) & 7
        w = w_down[:, pl.ds(pl.multiple_of(at * wide, 128), wide)]
        out[dy] = jnp.dot(hidden, w, preferred_element_type=F32).astype(BF16)


def expert_kernel(coords, w_gate, w_up, w_down, *refs):
    blocks, (send, hidden) = refs[:8], refs[8:]
    y, c, z = coords[0], coords[1], coords[3]
    acc = jnp.zeros((CAP, 256), F32)
    for r in range(8):
        s, dy = r // 4, r % 4
        at = (z - stride((y - dy) & 3, c ^ s)) & 7
        w = jnp.concatenate([w_gate[at], w_up[at]], axis=1)
        acc += jnp.dot(blocks[r][...], w, preferred_element_type=F32)
    gate, up = acc[:, :128], acc[:, 128:]
    hidden[...] = (gate / (1.0 + jnp.exp(-gate)) * up).astype(BF16)
    down_half(coords, hidden[...], w_down, send, 1)


def expert_rest_kernel(coords, hidden, w_down, keep):
    down_half(coords, hidden[...], w_down, keep, 0)


def picked_sum(dest_cols, at, m, held):
    d0 = dest_cols[pl.ds(at, m), 2:3].astype(jnp.int32)
    d1 = dest_cols[pl.ds(at, m), 3:4].astype(jnp.int32)
    acc = jnp.zeros((m, held.shape[1]), F32)
    step = 256
    for k in range(GROUP * CAP // step):
        place = lax.broadcasted_iota(jnp.int32, (m, step), 1) + k * step
        pick = jnp.where((place == d0) | (place == d1), 1.0, 0.0).astype(BF16)
        acc += jnp.dot(pick, held[k * step : (k + 1) * step, :], preferred_element_type=F32)
    return acc.astype(BF16)


def combine_kernel(coords, dest_cols, *refs):
    blocks, (part, held) = refs[:8], refs[8:]
    n = held.shape[1]
    for r in range(8):
        held[2 * r * CAP : (2 * r + 1) * CAP, :] = blocks[r][:, :n]
        held[(2 * r + 1) * CAP : (2 * r + 2) * CAP, :] = blocks[r][:, n:]
    m = part.shape[0]
    rows = picked_sum(dest_cols, pl.multiple_of(coords[1] * 2 * m, 16), 2 * m, held)
    part[:, :n] = rows[:m]
    part[:, n:] = rows[m:]


def combine_rest_kernel(coords, dest_cols, held, part, res):
    m, n = part.shape[0], held.shape[1]
    at = coords[1] * 2 * m
    res[pl.ds(pl.multiple_of(at, 16), m), :] = part[:, :n]
    res[pl.ds(pl.multiple_of(at + m, 16), m), :] = part[:, n:]
    at = pl.multiple_of((1 - coords[1]) * 2 * m, 16)
    res[pl.ds(at, 2 * m), :] = picked_sum(dest_cols, at, 2 * m, held)


def own_logits_kernel(dzs, coords, res, table, out, held):
    z = coords[3]
    rows = res.shape[0] // Z
    for i, dz in enumerate(dzs):
        at = pl.ds(pl.multiple_of(((z + dz) & 7) * rows, 16), rows)
        held[i * rows : (i + 1) * rows, :] = res[at, :]
    step = 512
    for k in range(table.shape[1] // step):
        at = slice(k * step, (k + 1) * step)
        out[:, at] = jnp.dot(held[...], table[:, at], preferred_element_type=F32)


def logits_kernel(dzs, coords, first, got_own, got_other, g0, g1, g2, g3, *refs):
    outs, (held, other) = refs[:-2], refs[-2:]
    c, z = coords[1], coords[3]
    m, n = got_own.shape[0], held.shape[1]
    for half, got in ((c, got_own), (1 - c, got_other)):
        other[pl.ds(pl.multiple_of(half * 2 * m, 16), m), :] = got[:, :n]
        other[pl.ds(pl.multiple_of(half * 2 * m + m, 16), m), :] = got[:, n:]
    rows = other.shape[0] // Z
    for i, dz in enumerate(dzs):
        at = pl.ds(pl.multiple_of(((z + dz) & 7) * rows, 16), rows)
        held[i * rows : (i + 1) * rows, :] = other[at, :]
    width = g0.shape[1]
    for k, got in enumerate((g0, g1, g2, g3)):
        val = first[:, k * width : (k + 1) * width]
        val += jnp.dot(held[...], got[...], preferred_element_type=F32)
        val = val.astype(BF16)
        u, at = k // 2, (k % 2) * width
        for i in range(len(dzs)):
            outs[2 * i + u][:, at : at + width] = val[i * rows : (i + 1) * rows, :]


def last_kernel(coords, own0, own1, below0, below1, above0, above1, keep, send, total):
    h = coords[4]
    n, width = keep.shape[0], own0.shape[1]
    for u, (a, b, d) in enumerate(((own0, below0, above0), (own1, below1, above1))):
        total[:, u * width : (u + 1) * width] = (
            a[...].astype(F32) + b[...].astype(F32) + d[...].astype(F32)
        ).astype(BF16)
    keep[...] = total[pl.ds(pl.multiple_of(h * n, 16), n), :]
    send[...] = total[pl.ds(pl.multiple_of((1 - h) * n, 16), n), :]


def swap(x, axis):
    return lax.ppermute(x, axis, [(0, 1), (1, 0)])


def shift_y(x, dy):
    return lax.ppermute(x, "y", [(y, (y + dy) % Y) for y in range(Y)])


def shift_z(x, dz):
    return lax.ppermute(x, "z", [(z, (z + dz) % Z) for z in range(Z)])


def crossed(x, forward):
    pairs = []
    for y in range(Y):
        for c in range(C):
            far = y if c == 0 else (8 - y if y else 4)
            for v in range(V):
                for z in range(Z):
                    for h in range(H):
                        at = (y * C + c) * V
                        a = ((at + v) * Z + z) * H + h
                        b = ((at + 1 - v) * Z + (z + far) % Z) * H + (h ^ v)
                        pairs.append((a, b) if forward else (b, a))
    return lax.ppermute(x, ALL, pairs)


def scatter_sum(coords, keep, send, piece, flip):
    got = swap(send, "c")
    one = shape(keep.shape[1:])
    parts = list(call(add_split_kernel, [one] * 4, keep, got, smem=0, size=3 * keep.size * 2))
    parts[3], piece = lax.optimization_barrier((parts[3], piece))
    arrived = [shift_y(parts[dy], dy) for dy in (2, 1, 3)]
    piece = swap(piece, "h")
    arrived[0], piece = lax.optimization_barrier((arrived[0], piece))
    half = (one.shape[0], one.shape[1] // 2)
    own, away = call(
        functools.partial(sum_split_kernel, flip),
        [shape(half, F32), shape(half)],
        coords,
        parts[0],
        *arrived,
        size=6 * parts[0].size * 2,
    )
    return (own + swap(away, "v").astype(F32)).astype(BF16), piece


def gather_all(coords, own, piece, flip):
    got = swap(own, "v")
    pair = call(
        functools.partial(pair_kernel, flip),
        shape((own.shape[0], 2 * own.shape[1])),
        coords,
        own,
        got,
        size=8 * own.size,
    )
    pair, piece = lax.optimization_barrier((pair, piece))
    near = [pair, None, None, None]
    for dy in (2, 1, 3):
        near[dy] = shift_y(pair, dy)
    piece = swap(piece, "h")
    near[0], near[3] = lax.optimization_barrier((pair, near[3]))
    far = [swap(x, "c") for x in near]
    far[1], piece = lax.optimization_barrier((far[1], piece))
    return near + far, piece


def added(a, b):
    return (a.astype(F32) + b.astype(F32)).astype(BF16)


def per_device(token_ids, routes, gate_weights, embed_table, w_gate, w_up, w_down):
    vocab_rows, width = embed_table.shape
    tokens = token_ids.shape[0]
    coords = jnp.stack(
        [lax.axis_index(a) for a in ALL] + [lax.axis_index(PV), jnp.int32(0), jnp.int32(0)]
    ).astype(jnp.int32)
    table = embed_table.T
    h = lax.axis_index("h")
    eighth = vocab_rows // 8
    quarter = 2 * eighth
    half = 2 * quarter
    slots = (4, CAP, 2 * width)
    def far(x):
        return pltpu.with_memory_space_constraint(x, pltpu.HBM)

    table = far(table)
    send, emb_t, dest_rows = call(
        lookup_kernel,
        [shape(slots), shape((width, tokens)), shape((8, tokens), jnp.int32)],
        coords,
        far(token_ids),
        far(routes.T),
        table,
        hbm=3,
        scratch=[
            pltpu.VMEM((tokens,), jnp.int32),
            pltpu.VMEM((2, tokens), jnp.int32),
            pltpu.VMEM((width, vocab_rows), BF16),
            pltpu.SemaphoreType.DMA((2,)),
            pltpu.SemaphoreType.DMA((4,)),
        ],
        flops=2 * tokens * width * (vocab_rows + GROUP * CAP),
        size=6 * 1024 * 1024,
    )
    keep, *pieces = call(
        rest_kernel,
        [shape(slots)] + [shape((width, eighth))] * 4,
        coords,
        dest_rows,
        emb_t,
        table,
        hbm=1,
        scratch=[pltpu.SemaphoreType.DMA((4,))],
        flops=2 * tokens * width * GROUP * CAP // 2,
        size=6 * 1024 * 1024,
    )
    dest_cols, slot_w, own = call(
        slots_kernel,
        [shape((tokens, 8), F32), shape((CAP, 2), F32), shape((width, half))],
        coords,
        dest_rows,
        far(gate_weights.T),
        table,
        hbm=2,
        scratch=[pltpu.VMEM((2, tokens), F32), pltpu.SemaphoreType.DMA((2,))],
        flops=tokens * CAP,
        size=3 * 1024 * 1024,
    )
    gots = [None] * 4
    rows_in, gots[0] = scatter_sum(coords, keep, send, pieces[0], 0)
    blocks, gots[1] = gather_all(coords, crossed(rows_in, True), pieces[1], 1)
    send, hidden = call(
        expert_kernel,
        [shape(slots), shape((CAP, 128))],
        coords,
        w_gate.reshape(8, 2 * width, 128),
        w_up.reshape(8, 2 * width, 128),
        w_down[0],
        *blocks,
        flops=5 * CAP * GROUP * width * 128,
        size=9 * 1024 * 1024,
    )
    keep = call(
        expert_rest_kernel,
        shape(slots),
        coords,
        hidden,
        w_down[0],
        flops=CAP * GROUP * width * 128,
        size=3 * 1024 * 1024,
    )
    sums, gots[2] = scatter_sum(coords, keep, send, pieces[2], 1)
    back = crossed(sums, False)
    back = (
        slot_w[:, 0:1] * back.astype(F32) + slot_w[:, 1:2] * rows_in.astype(F32)
    ).astype(BF16)
    blocks, gots[3] = gather_all(coords, back, pieces[3], 0)
    part, held = call(
        combine_kernel,
        [shape((tokens // 4, 2 * width)), shape((GROUP * CAP, width))],
        coords,
        dest_cols,
        *blocks,
        flops=tokens * GROUP * CAP * width,
        size=5 * 1024 * 1024,
    )
    res = call(
        combine_rest_kernel,
        shape((tokens, width)),
        coords,
        dest_cols,
        held,
        part,
        flops=tokens * GROUP * CAP * width,
        size=3 * 1024 * 1024,
    )
    near = [(v * H + h, (1 - v) * H + 1 - h) for v in range(V) for h in range(H)]
    got_own = lax.ppermute(part, ("v", "h"), near)
    rows = tokens // Z
    outs = {}
    orders = ((4, 5, 3), (6, 2, 7, 1, 0))
    firsts = []
    for dzs in orders:
        m = len(dzs) * rows
        firsts.append(
            call(
                functools.partial(own_logits_kernel, dzs),
                shape((m, half), F32),
                coords,
                res,
                own,
                scratch=[pltpu.VMEM((m, width), BF16)],
                flops=2 * m * width * half,
                size=6 * 1024 * 1024,
            )
        )
    got_own, *firsts = lax.optimization_barrier((got_own, *firsts))
    got_other = swap(got_own, "c")
    for k, dzs in enumerate(orders):
        m = len(dzs) * rows
        vals = call(
            functools.partial(logits_kernel, dzs),
            [shape((rows, quarter))] * (2 * len(dzs)),
            coords,
            firsts[k],
            got_own,
            got_other,
            *gots,
            scratch=[pltpu.VMEM((m, width), BF16), pltpu.VMEM((tokens, width), BF16)],
            flops=2 * m * width * half,
            size=6 * 1024 * 1024,
        )
        for i, dz in enumerate(dzs):
            outs[dz] = vals[2 * i : 2 * i + 2]
    down = [shift_z(outs[4][0], -1), None]
    up = [None, shift_z(outs[4][1], 1)]
    down[1] = shift_z(outs[5][1], -1)
    up[0] = shift_z(outs[3][0], 1)
    down[0] = shift_z(added(down[0], outs[5][0]), -1)
    up[1] = shift_z(added(up[1], outs[3][1]), 1)
    for k in (2, 1):
        for u in (1, 0):
            down[u] = shift_z(added(down[u], outs[Z - k][u]), -1)
            up[1 - u] = shift_z(added(up[1 - u], outs[k][1 - u]), 1)
    down[0], up[1] = lax.optimization_barrier((down[0], up[1]))
    mine, theirs = call(
        last_kernel,
        [shape((rows // 2, half))] * 2,
        coords,
        *outs[0],
        *down,
        *up,
        scratch=[pltpu.VMEM((rows, half), BF16)],
        size=8 * rows * half,
    )
    got = swap(theirs, "h")
    return jnp.where(
        lax.axis_index("h") == 0,
        jnp.concatenate([mine, got], axis=1),
        jnp.concatenate([got, mine], axis=1),
    )


def solution(mesh):
    finer = Mesh(mesh.devices.reshape(Y, C, V, Z, H), ALL)
    return jax.shard_map(
        per_device,
        mesh=finer,
        in_specs=(
            P(),
            P(),
            P(),
            P(PV, EXPERT),
            P(EXPERT, None, PV),
            P(EXPERT, None, PV),
            P(EXPERT, PV, None),
        ),
        out_specs=P(EXPERT, PV),
        check_vma=False,
    )
```

```python
import functools

import jax
import jax.numpy as jnp
from jax import lax
from jax.experimental import pallas as pl
from jax.experimental.pallas import tpu as pltpu
from jax.sharding import Mesh
from jax.sharding import PartitionSpec as P

Y, C, V, Z, H = 4, 2, 2, 8, 2
ALL = ("y", "c", "v", "z", "h")
PV = ("y", "c", "v")
EXPERT = ("z", "h")
GROUP = 16
CAP = 144
BF16 = jnp.bfloat16
F32 = jnp.float32
LIMIT = 28 * 1024 * 1024

VMEM = pl.BlockSpec(memory_space=pltpu.VMEM)
SMEM = pl.BlockSpec(memory_space=pltpu.SMEM)


def call(kernel, out_shape, *args, smem=1, hbm=0, scratch=(), flops=0, size=0):
    return pl.pallas_call(
        kernel,
        out_shape=out_shape,
        in_specs=[SMEM] * smem
        + [VMEM] * (len(args) - smem - hbm)
        + [pl.BlockSpec(memory_space=pltpu.HBM)] * hbm,
        out_specs=jax.tree.map(lambda _: VMEM, out_shape),
        scratch_shapes=list(scratch),
        compiler_params=pltpu.CompilerParams(vmem_limit_bytes=LIMIT),
        cost_estimate=pl.CostEstimate(flops=flops, bytes_accessed=size, transcendentals=0),
    )(*args)


def shape(dims, dtype=BF16):
    return jax.ShapeDtypeStruct(dims, dtype)


def stride(y, c):
    return jnp.where(c == 0, y, jnp.where(y == 0, 4, 8 - y))


def ranks(coords, experts, sign):
    y, c, z = coords[0], coords[1], coords[3]
    d = (lax.shift_right_logical(experts, 1) - z) & 7
    cc = jnp.where(d >= 4, 1, 0)
    yy = jnp.where(d < 4, d, (8 - d) & 3)
    return ((cc ^ c) * 4 + ((sign * (yy - y)) & 3)) * 2 + (experts & 1)


def spread(dest_rows, emb_t, out, start):
    tokens = dest_rows.shape[1]
    d0, d1 = dest_rows[0:1, :], dest_rows[1:2, :]
    many = 4 * CAP
    for r in range(0, 4, 2):
        slot = lax.broadcasted_iota(jnp.int32, (many, tokens), 0) + 2 * (start + r) * CAP
        hot = jnp.where((slot == d0) | (slot == d1), 1.0, 0.0).astype(BF16)
        rows = lax.dot_general(
            hot, emb_t, (((1,), (1,)), ((), ())), preferred_element_type=F32
        ).astype(BF16)
        for i in range(2):
            at = 2 * i * CAP
            out[r + i] = jnp.concatenate(
                [rows[at : at + CAP], rows[at + CAP : at + 2 * CAP]], axis=1
            )


def lookup_kernel(coords, ids_far, routes_far, table_far, *refs):
    send, emb_t, dest_rows, ids, routes, table, small, large = refs
    load_ids = pltpu.make_async_copy(ids_far, ids, small.at[0])
    load_routes = pltpu.make_async_copy(routes_far, routes, small.at[1])
    tokens = ids.shape[0]
    rows = table.shape[1]
    step = 512
    block = rows // 4
    loads = []
    for b in range(4):
        at = pl.ds(b * block, block)
        loads.append(
            pltpu.make_async_copy(table_far.at[:, at], table.at[:, at], large.at[b])
        )
    load_routes.start()
    load_ids.start()
    for x in loads:
        x.start()
    load_routes.wait()
    experts = lax.broadcasted_iota(jnp.int32, (GROUP, tokens), 0)
    hot0 = experts == routes[0:1, :]
    hot1 = experts == routes[1:2, :]
    named = jnp.where(hot0 | hot1, 1.0, 0.0).astype(BF16)
    earlier = lax.broadcasted_iota(jnp.int32, (tokens, tokens), 0) < lax.broadcasted_iota(
        jnp.int32, (tokens, tokens), 1
    )
    count = jnp.dot(named, jnp.where(earlier, 1.0, 0.0).astype(BF16), preferred_element_type=F32)
    count = count.astype(jnp.int32)

    def picked(hot, sign):
        where = ranks(coords, experts, sign) * CAP + count
        return jnp.sum(jnp.where(hot, where, 0), axis=0, keepdims=True)

    dest_rows[...] = jnp.concatenate(
        [picked(hot0, 1), picked(hot1, 1), picked(hot0, -1), picked(hot1, -1)]
        + [jnp.zeros((4, tokens), jnp.int32)],
        axis=0,
    )
    load_ids.wait()
    base = ids[...].reshape(1, tokens) - coords[5] * rows
    acc = jnp.zeros((table.shape[0], tokens), F32)
    place = lax.broadcasted_iota(jnp.int32, (step, tokens), 0)
    for k in range(rows // step):
        if k * step % block == 0:
            loads[k * step // block].wait()
        hot = jnp.where(place == base - k * step, 1.0, 0.0).astype(BF16)
        acc += jnp.dot(table[:, k * step : (k + 1) * step], hot, preferred_element_type=F32)
    emb_t[...] = acc.astype(BF16)
    spread(dest_rows, emb_t[...], send, 4)


def rest_kernel(coords, dest_rows, emb_t, table_far, keep, p0, p1, p2, p3, sems):
    width = p0.shape[1]
    half = 4 * width
    loads = []
    for u, piece in enumerate((p0, p1, p2, p3)):
        at = pl.multiple_of((1 - coords[4]) * half + u * width, 128)
        loads.append(
            pltpu.make_async_copy(table_far.at[:, pl.ds(at, width)], piece, sems.at[u])
        )
    for x in loads:
        x.start()
    spread(dest_rows, emb_t[...], keep, 0)
    for x in loads:
        x.wait()


def slots_kernel(
    coords, dest_rows, gates_far, table_far, dest_cols, slot_w, own, gates, sems
):
    half = own.shape[1]
    at = pl.multiple_of(coords[4] * half, 128)
    load = pltpu.make_async_copy(gates_far, gates, sems.at[0])
    load_own = pltpu.make_async_copy(table_far.at[:, pl.ds(at, half)], own, sems.at[1])
    load.start()
    load_own.start()
    tokens = dest_rows.shape[1]
    dest_cols[...] = dest_rows[...].astype(F32).T
    mine = coords[4] ^ coords[2]
    slot = lax.broadcasted_iota(jnp.int32, (CAP, tokens), 0) + mine * CAP
    eq0, eq1 = slot == dest_rows[0:1, :], slot == dest_rows[1:2, :]
    load.wait()
    w = jnp.where(eq0, gates[0:1, :], 0.0) + jnp.where(eq1, gates[1:2, :], 0.0)
    slot_w[:, 0:1] = jnp.sum(w, axis=1, keepdims=True)
    slot_w[:, 1:2] = jnp.sum(jnp.where(eq0, 1.0, 0.0), axis=1, keepdims=True)
    load_own.wait()


def add_split_kernel(keep, got, *outs):
    for i, out in enumerate(outs):
        out[...] = (keep[i].astype(F32) + got[i].astype(F32)).astype(BF16)


def sum_split_kernel(flip, coords, *refs):
    parts, (keep, send) = refs[:4], refs[4:]
    total = parts[0][...].astype(F32)
    for p in parts[1:]:
        total += p[...].astype(F32)
    n = keep.shape[1]
    left, right = total[:, :n], total[:, n:]
    first = (coords[4] ^ coords[2]) == flip
    keep[...] = jnp.where(first, left, right)
    send[...] = jnp.where(first, right, left).astype(BF16)


def pair_kernel(flip, coords, own, got, out):
    first = (coords[4] ^ coords[2]) == flip
    a, b = own[...].astype(F32), got[...].astype(F32)
    out[...] = jnp.concatenate(
        [jnp.where(first, a, b).astype(BF16), jnp.where(first, b, a).astype(BF16)], axis=1
    )


def down_half(coords, hidden, w_down, out, s):
    y, c, z = coords[0], coords[1], coords[3]
    wide = out.shape[2]
    for dy in range(4):
        at = (z - stride((y + dy) & 3, c ^ s)) & 7
        w = w_down[:, pl.ds(pl.multiple_of(at * wide, 128), wide)]
        out[dy] = jnp.dot(hidden, w, preferred_element_type=F32).astype(BF16)


def expert_kernel(coords, w_gate, w_up, w_down, *refs):
    blocks, (send, hidden) = refs[:8], refs[8:]
    y, c, z = coords[0], coords[1], coords[3]
    acc = jnp.zeros((CAP, 256), F32)
    for r in range(8):
        s, dy = r // 4, r % 4
        at = (z - stride((y - dy) & 3, c ^ s)) & 7
        w = jnp.concatenate([w_gate[at], w_up[at]], axis=1)
        acc += jnp.dot(blocks[r][...], w, preferred_element_type=F32)
    gate, up = acc[:, :128], acc[:, 128:]
    hidden[...] = (gate / (1.0 + jnp.exp(-gate)) * up).astype(BF16)
    down_half(coords, hidden[...], w_down, send, 1)


def expert_rest_kernel(coords, hidden, w_down, keep):
    down_half(coords, hidden[...], w_down, keep, 0)


def picked_sum(dest_cols, at, m, held):
    d0 = dest_cols[pl.ds(at, m), 2:3].astype(jnp.int32)
    d1 = dest_cols[pl.ds(at, m), 3:4].astype(jnp.int32)
    acc = jnp.zeros((m, held.shape[1]), F32)
    step = 256
    for k in range(GROUP * CAP // step):
        place = lax.broadcasted_iota(jnp.int32, (m, step), 1) + k * step
        pick = jnp.where((place == d0) | (place == d1), 1.0, 0.0).astype(BF16)
        acc += jnp.dot(pick, held[k * step : (k + 1) * step, :], preferred_element_type=F32)
    return acc.astype(BF16)


def combine_kernel(coords, dest_cols, *refs):
    blocks, (part, held) = refs[:8], refs[8:]
    n = held.shape[1]
    for r in range(8):
        held[2 * r * CAP : (2 * r + 1) * CAP, :] = blocks[r][:, :n]
        held[(2 * r + 1) * CAP : (2 * r + 2) * CAP, :] = blocks[r][:, n:]
    m = part.shape[0]
    rows = picked_sum(dest_cols, pl.multiple_of(coords[1] * 2 * m, 16), 2 * m, held)
    part[:, :n] = rows[:m]
    part[:, n:] = rows[m:]


def combine_rest_kernel(coords, dest_cols, held, part, res):
    m, n = part.shape[0], held.shape[1]
    at = coords[1] * 2 * m
    res[pl.ds(pl.multiple_of(at, 16), m), :] = part[:, :n]
    res[pl.ds(pl.multiple_of(at + m, 16), m), :] = part[:, n:]
    at = pl.multiple_of((1 - coords[1]) * 2 * m, 16)
    res[pl.ds(at, 2 * m), :] = picked_sum(dest_cols, at, 2 * m, held)


def own_logits_kernel(dzs, coords, res, table, out, held):
    z = coords[3]
    rows = res.shape[0] // Z
    for i, dz in enumerate(dzs):
        at = pl.ds(pl.multiple_of(((z + dz) & 7) * rows, 16), rows)
        held[i * rows : (i + 1) * rows, :] = res[at, :]
    step = 512
    for k in range(table.shape[1] // step):
        at = slice(k * step, (k + 1) * step)
        out[:, at] = jnp.dot(held[...], table[:, at], preferred_element_type=F32)


def logits_kernel(dzs, coords, first, got_own, got_other, g0, g1, g2, g3, *refs):
    outs, (held, other) = refs[:-2], refs[-2:]
    c, z = coords[1], coords[3]
    m, n = got_own.shape[0], held.shape[1]
    for half, got in ((c, got_own), (1 - c, got_other)):
        other[pl.ds(pl.multiple_of(half * 2 * m, 16), m), :] = got[:, :n]
        other[pl.ds(pl.multiple_of(half * 2 * m + m, 16), m), :] = got[:, n:]
    rows = other.shape[0] // Z
    for i, dz in enumerate(dzs):
        at = pl.ds(pl.multiple_of(((z + dz) & 7) * rows, 16), rows)
        held[i * rows : (i + 1) * rows, :] = other[at, :]
    width = g0.shape[1]
    for k, got in enumerate((g0, g1, g2, g3)):
        val = first[:, k * width : (k + 1) * width]
        val += jnp.dot(held[...], got[...], preferred_element_type=F32)
        val = val.astype(BF16)
        u, at = k // 2, (k % 2) * width
        for i in range(len(dzs)):
            outs[2 * i + u][:, at : at + width] = val[i * rows : (i + 1) * rows, :]


def last_kernel(coords, own0, own1, below0, below1, above0, above1, keep, send, total):
    h = coords[4]
    n, width = keep.shape[0], own0.shape[1]
    for u, (a, b, d) in enumerate(((own0, below0, above0), (own1, below1, above1))):
        total[:, u * width : (u + 1) * width] = (
            a[...].astype(F32) + b[...].astype(F32) + d[...].astype(F32)
        ).astype(BF16)
    keep[...] = total[pl.ds(pl.multiple_of(h * n, 16), n), :]
    send[...] = total[pl.ds(pl.multiple_of((1 - h) * n, 16), n), :]


def swap(x, axis):
    return lax.ppermute(x, axis, [(0, 1), (1, 0)])


def shift_y(x, dy):
    return lax.ppermute(x, "y", [(y, (y + dy) % Y) for y in range(Y)])


def shift_z(x, dz):
    return lax.ppermute(x, "z", [(z, (z + dz) % Z) for z in range(Z)])


def crossed(x, forward):
    pairs = []
    for y in range(Y):
        for c in range(C):
            far = y if c == 0 else (8 - y if y else 4)
            for v in range(V):
                for z in range(Z):
                    for h in range(H):
                        at = (y * C + c) * V
                        a = ((at + v) * Z + z) * H + h
                        b = ((at + 1 - v) * Z + (z + far) % Z) * H + (h ^ v)
                        pairs.append((a, b) if forward else (b, a))
    return lax.ppermute(x, ALL, pairs)


def scatter_sum(coords, keep, send, piece, flip):
    got = swap(send, "c")
    one = shape(keep.shape[1:])
    parts = list(call(add_split_kernel, [one] * 4, keep, got, smem=0, size=3 * keep.size * 2))
    arrived = [shift_y(parts[dy], dy) for dy in (2, 1, 3)]
    piece = swap(piece, "h")
    arrived[0], piece = lax.optimization_barrier((arrived[0], piece))
    half = (one.shape[0], one.shape[1] // 2)
    own, away = call(
        functools.partial(sum_split_kernel, flip),
        [shape(half, F32), shape(half)],
        coords,
        parts[0],
        *arrived,
        size=6 * parts[0].size * 2,
    )
    return (own + swap(away, "v").astype(F32)).astype(BF16), piece


def gather_all(coords, own, piece, flip):
    got = swap(own, "v")
    pair = call(
        functools.partial(pair_kernel, flip),
        shape((own.shape[0], 2 * own.shape[1])),
        coords,
        own,
        got,
        size=8 * own.size,
    )
    pair, piece = lax.optimization_barrier((pair, piece))
    near = [pair, None, None, None]
    for dy in (2, 1, 3):
        near[dy] = shift_y(pair, dy)
    piece = swap(piece, "h")
    near[0], near[3] = lax.optimization_barrier((pair, near[3]))
    far = [swap(x, "c") for x in near]
    far[1], piece = lax.optimization_barrier((far[1], piece))
    return near + far, piece


def added(a, b):
    return (a.astype(F32) + b.astype(F32)).astype(BF16)


def per_device(token_ids, routes, gate_weights, embed_table, w_gate, w_up, w_down):
    vocab_rows, width = embed_table.shape
    tokens = token_ids.shape[0]
    coords = jnp.stack(
        [lax.axis_index(a) for a in ALL] + [lax.axis_index(PV), jnp.int32(0), jnp.int32(0)]
    ).astype(jnp.int32)
    table = embed_table.T
    h = lax.axis_index("h")
    eighth = vocab_rows // 8
    quarter = 2 * eighth
    half = 2 * quarter
    slots = (4, CAP, 2 * width)
    def far(x):
        return pltpu.with_memory_space_constraint(x, pltpu.HBM)

    table = far(table)
    send, emb_t, dest_rows = call(
        lookup_kernel,
        [shape(slots), shape((width, tokens)), shape((8, tokens), jnp.int32)],
        coords,
        far(token_ids),
        far(routes.T),
        table,
        hbm=3,
        scratch=[
            pltpu.VMEM((tokens,), jnp.int32),
            pltpu.VMEM((2, tokens), jnp.int32),
            pltpu.VMEM((width, vocab_rows), BF16),
            pltpu.SemaphoreType.DMA((2,)),
            pltpu.SemaphoreType.DMA((4,)),
        ],
        flops=2 * tokens * width * (vocab_rows + GROUP * CAP),
        size=6 * 1024 * 1024,
    )
    keep, *pieces = call(
        rest_kernel,
        [shape(slots)] + [shape((width, eighth))] * 4,
        coords,
        dest_rows,
        emb_t,
        table,
        hbm=1,
        scratch=[pltpu.SemaphoreType.DMA((4,))],
        flops=2 * tokens * width * GROUP * CAP // 2,
        size=6 * 1024 * 1024,
    )
    dest_cols, slot_w, own = call(
        slots_kernel,
        [shape((tokens, 8), F32), shape((CAP, 2), F32), shape((width, half))],
        coords,
        dest_rows,
        far(gate_weights.T),
        table,
        hbm=2,
        scratch=[pltpu.VMEM((2, tokens), F32), pltpu.SemaphoreType.DMA((2,))],
        flops=tokens * CAP,
        size=3 * 1024 * 1024,
    )
    gots = [None] * 4
    rows_in, gots[0] = scatter_sum(coords, keep, send, pieces[0], 0)
    blocks, gots[1] = gather_all(coords, crossed(rows_in, True), pieces[1], 1)
    send, hidden = call(
        expert_kernel,
        [shape(slots), shape((CAP, 128))],
        coords,
        w_gate.reshape(8, 2 * width, 128),
        w_up.reshape(8, 2 * width, 128),
        w_down[0],
        *blocks,
        flops=5 * CAP * GROUP * width * 128,
        size=9 * 1024 * 1024,
    )
    keep = call(
        expert_rest_kernel,
        shape(slots),
        coords,
        hidden,
        w_down[0],
        flops=CAP * GROUP * width * 128,
        size=3 * 1024 * 1024,
    )
    sums, gots[2] = scatter_sum(coords, keep, send, pieces[2], 1)
    back = crossed(sums, False)
    back = (
        slot_w[:, 0:1] * back.astype(F32) + slot_w[:, 1:2] * rows_in.astype(F32)
    ).astype(BF16)
    blocks, gots[3] = gather_all(coords, back, pieces[3], 0)
    part, held = call(
        combine_kernel,
        [shape((tokens // 4, 2 * width)), shape((GROUP * CAP, width))],
        coords,
        dest_cols,
        *blocks,
        flops=tokens * GROUP * CAP * width,
        size=5 * 1024 * 1024,
    )
    res = call(
        combine_rest_kernel,
        shape((tokens, width)),
        coords,
        dest_cols,
        held,
        part,
        flops=tokens * GROUP * CAP * width,
        size=3 * 1024 * 1024,
    )
    near = [(v * H + h, (1 - v) * H + 1 - h) for v in range(V) for h in range(H)]
    got_own = lax.ppermute(part, ("v", "h"), near)
    rows = tokens // Z
    outs = {}
    orders = ((4, 5, 3), (6, 2, 7, 1, 0))
    firsts = []
    for dzs in orders:
        m = len(dzs) * rows
        firsts.append(
            call(
                functools.partial(own_logits_kernel, dzs),
                shape((m, half), F32),
                coords,
                res,
                own,
                scratch=[pltpu.VMEM((m, width), BF16)],
                flops=2 * m * width * half,
                size=6 * 1024 * 1024,
            )
        )
    got_own, *firsts = lax.optimization_barrier((got_own, *firsts))
    got_other = swap(got_own, "c")
    for k, dzs in enumerate(orders):
        m = len(dzs) * rows
        vals = call(
            functools.partial(logits_kernel, dzs),
            [shape((rows, quarter))] * (2 * len(dzs)),
            coords,
            firsts[k],
            got_own,
            got_other,
            *gots,
            scratch=[pltpu.VMEM((m, width), BF16), pltpu.VMEM((tokens, width), BF16)],
            flops=2 * m * width * half,
            size=6 * 1024 * 1024,
        )
        for i, dz in enumerate(dzs):
            outs[dz] = vals[2 * i : 2 * i + 2]
    down = [shift_z(outs[4][0], -1), None]
    up = [None, shift_z(outs[4][1], 1)]
    down[1] = shift_z(outs[5][1], -1)
    up[0] = shift_z(outs[3][0], 1)
    down[0] = shift_z(added(down[0], outs[5][0]), -1)
    up[1] = shift_z(added(up[1], outs[3][1]), 1)
    for k in (2, 1):
        for u in (1, 0):
            down[u] = shift_z(added(down[u], outs[Z - k][u]), -1)
            up[1 - u] = shift_z(added(up[1 - u], outs[k][1 - u]), 1)
    down[0], up[1] = lax.optimization_barrier((down[0], up[1]))
    mine, theirs = call(
        last_kernel,
        [shape((rows // 2, half))] * 2,
        coords,
        *outs[0],
        *down,
        *up,
        scratch=[pltpu.VMEM((rows, half), BF16)],
        size=8 * rows * half,
    )
    got = swap(theirs, "h")
    return jnp.where(
        lax.axis_index("h") == 0,
        jnp.concatenate([mine, got], axis=1),
        jnp.concatenate([got, mine], axis=1),
    )


def solution(mesh):
    finer = Mesh(mesh.devices.reshape(Y, C, V, Z, H), ALL)
    return jax.shard_map(
        per_device,
        mesh=finer,
        in_specs=(
            P(),
            P(),
            P(),
            P(PV, EXPERT),
            P(EXPERT, None, PV),
            P(EXPERT, None, PV),
            P(EXPERT, PV, None),
        ),
        out_specs=P(EXPERT, PV),
        check_vma=False,
    )
```
